256 devices in a mesh: gz: 16 (over z, x_lo), gy: 16 (over x_hi, y, core).
Axes of the slice: x: 4 (x_hi: 2, x_lo: 2; x = x_hi * 2 + x_lo), y: 4, z: 8, core: 2. Of those that a mesh axis runs over, the one named last changes fastest.
Arguments:
- displacement: float32 [3, 256, 512, 256], P(None, 'gz', 'gy'), may hold values from -6 to 6
- design: float32 [256, 512, 256], P('gz', 'gy'), may hold values from 0.1 to 0.95
- void_mask: int32 [256, 512, 256], P('gz', 'gy'), may hold values 0 or 1
- solid_mask: int32 [256, 512, 256], P('gz', 'gy'), may hold values 0 or 1
- stiffness: float32 [24, 24], replicated, as said below
Outputs:
- new_design: float32 [256, 512, 256], P('gz', 'gy')
- sensitivity: float32 [256, 512, 256], P('gz', 'gy')
The draws below stay inside these ranges and needn't reach their ends.
Inputs may be any that keep to these rules, and one draw needn't show every extreme that they name: stiffness is symmetric, and each diagonal entry exceeds the sum of magnitudes of the rest of its row.
All inputs are finite; a program needn't handle non-finite values. No bound on the sum of `void_mask` or of `solid_mask` on one device may be relied on, other than what follows from the above.
Results may differ from the reference program's by a relative error of at most 0.0001.
Values sent between devices are 32-bit elements; how exact they have to be, the bound alone decides.
A program may use at most 64 MiB of HBM per device.

```python
import math
import jax
import jax.numpy as jnp
from jax import lax

EX = 256
ITERS = 8
EZ = 256
EY = 512


def draw_stiffness(key, part):
    key = jax.random.fold_in(key, 7)
    key_off, key_diag = jax.random.split(key)
    random_part = jax.random.uniform(key_off, (24, 24), jnp.float32, -0.1, 0.1)
    coupling = 0.5 * (random_part + random_part.T)
    identity = jnp.eye(24, dtype=jnp.float32)
    diagonal = 2.5 + jax.random.uniform(key_diag, (24,), jnp.float32)
    return coupling * (1.0 - identity) + identity * diagonal[None, :]


def draw_displacement(key, part):
    key = jax.random.fold_in(key, 11)
    key_phase, key_noise = jax.random.split(key)
    phases = jax.random.uniform(key_phase, (3,), jnp.float32, 0.0, 1.0)
    level_z = (jnp.arange(EZ, dtype=jnp.float32) + 0.5) / EZ
    level_y = (jnp.arange(EY, dtype=jnp.float32) + 0.5) / EY
    level_x = (jnp.arange(EX, dtype=jnp.float32) + 0.5) / EX
    wave_z = jnp.sin(2.0 * math.pi * (level_z + phases[0]))
    wave_y = jnp.cos(2.0 * math.pi * (level_y + phases[1]))
    wave_x = jnp.sin(2.0 * math.pi * (level_x + phases[2]))
    log_amplitude = 0.8 * wave_z[:, None, None] * wave_y[None, :, None] + 0.7 * wave_x[None, None, :]
    amplitude = jnp.exp(log_amplitude)
    noise = jnp.clip(jax.random.normal(key_noise, (3, EZ, EY, EX), jnp.float32), -5.0, 5.0)
    return 0.2 * noise * amplitude[None]


def with_ends(result, key, low, high):
    spot = [jax.random.randint(jax.random.fold_in(key, axis), (), 0, length) for axis, length in enumerate(result.shape)]
    main_axis = result.shape.index(max(result.shape))
    next_to = spot[:main_axis] + [(spot[main_axis] + 1) % result.shape[main_axis]] + spot[main_axis + 1:]
    return result.at[tuple(spot)].set(low).at[tuple(next_to)].set(high)


def block_scale(stream_key, shape, cuts, low, top_value):
    def one(axis_at, shards_of):
        heights = jax.random.uniform(jax.random.fold_in(jax.random.fold_in(stream_key, 6), axis_at), (shards_of,), jnp.float32, low / len(cuts), top_value / len(cuts))
        return jnp.repeat(jnp.exp(heights), shape[axis_at] // shards_of).reshape((-1,) + (1,) * (len(shape) - axis_at - 1))

    gain = one(*cuts[0])
    for cut in cuts[1:]:
        gain = gain * one(*cut)
    return gain


def setup_inputs(seed: int = 0) -> dict:
    splits = jax.random.split(jax.random.key(seed), 6)
    displacement = draw_displacement(jax.random.fold_in(splits[5], 71), 0)
    design = jnp.clip(0.1 + 0.84999999 * jax.random.uniform(splits[1], (EZ, EY, EX), jnp.float32) ** block_scale(splits[1], (EZ, EY, EX), ((0, 16), (1, 16)), -0.2, 0.2), 0.1, 0.95)
    void_mask = with_ends((jax.random.randint(splits[2], (EZ, EY, EX), 0, 10) < 1).astype(jnp.int32), jax.random.fold_in(splits[2], 1), 0, 1)
    solid_mask = with_ends((jax.random.randint(splits[3], (EZ, EY, EX), 0, 10) < 1).astype(jnp.int32), jax.random.fold_in(splits[3], 1), 0, 1)
    stiffness = draw_stiffness(jax.random.fold_in(splits[5], 71), 0)
    return {"displacement": displacement, "design": design, "void_mask": void_mask, "solid_mask": solid_mask, "stiffness": stiffness}


TAP_TABLE = (1.0, 2.0, 3.0, 4.0, 3.0, 2.0, 1.0)
LOW_LOG = -25.0
HIGH_LOG = 25.0
MOVE_LIMIT = 0.2
VOLUME_FRACTION = 0.5
PENALTY = 3.0

def line_weights(position, extent):
    offsets = jnp.arange(-3, 4, dtype=jnp.int32)
    tap_values = jnp.asarray(TAP_TABLE, jnp.float32)

    def row_total(locations):
        nearby = locations[:, None] + offsets[None, :]
        inside = ((nearby >= 0) & (nearby < extent)).astype(jnp.float32)
        return lax.optimization_barrier(jnp.sum(inside * tap_values[None, :], axis=1))
    totals = row_total(position)
    nearby = position[:, None] + offsets[None, :]
    inside = ((nearby >= 0) & (nearby < extent)).astype(jnp.float32)
    near_totals = row_total(nearby.reshape(-1)).reshape(nearby.shape)
    spread = lax.optimization_barrier(jnp.sum(inside * tap_values[None, :] / near_totals, axis=1))
    return (totals, spread)

def pass_along(padded, dimension, extent):
    summed = TAP_TABLE[0] * lax.slice_in_dim(padded, 0, extent, axis=dimension)
    for tap_index in range(1, 7):
        summed = summed + TAP_TABLE[tap_index] * lax.slice_in_dim(padded, tap_index, tap_index + extent, axis=dimension)
    return summed

def energies(extended, stiffness, layer_count, row_count, col_count):

    def one_layer(layer):
        slab_pair = lax.dynamic_slice_in_dim(extended, layer, 2, 1)
        corners = []
        for step_z in range(2):
            for step_y in range(2):
                for step_x in range(2):
                    for component in range(3):
                        corners.append(slab_pair[component, step_z, step_y:step_y + row_count, step_x:step_x + col_count])
        stacked = jnp.stack(corners)
        forces = jnp.einsum('ab,byx->ayx', stiffness, stacked, precision=lax.Precision.HIGHEST)
        return lax.optimization_barrier(jnp.sum(stacked * forces, axis=0))
    return lax.map(one_layer, jnp.arange(layer_count, dtype=jnp.int32))

def smooth(field):
    layer_count, row_count, col_count = field.shape
    padded = jnp.pad(field, ((3, 3), (0, 0), (0, 0)))
    along_z = pass_along(padded, 0, layer_count)
    padded = jnp.pad(along_z, ((0, 0), (3, 3), (0, 0)))
    along_y = pass_along(padded, 1, row_count)
    padded = jnp.pad(along_y, ((0, 0), (0, 0), (3, 3)))
    return pass_along(padded, 2, col_count)

def reference(displacement, design, void_mask, solid_mask, stiffness):
    layer_count, row_count, col_count = design.shape
    extended = jnp.pad(displacement, ((0, 0), (0, 1), (0, 1), (0, 1)))
    energy = energies(extended, stiffness, layer_count, row_count, col_count)
    totals_z, spread_z = line_weights(jnp.arange(layer_count, dtype=jnp.int32), layer_count)
    totals_y, spread_y = line_weights(jnp.arange(row_count, dtype=jnp.int32), row_count)
    totals_x, spread_x = line_weights(jnp.arange(col_count, dtype=jnp.int32), col_count)
    inverse_total = 1.0 / (totals_z[:, None, None] * totals_y[None, :, None] * totals_x[None, None, :])
    volume_weight = spread_z[:, None, None] * spread_y[None, :, None] * spread_x[None, None, :]
    physical = smooth(design) * inverse_total
    sensitivity = smooth(-PENALTY * physical * physical * energy * inverse_total)
    root = jnp.sqrt(-sensitivity / volume_weight)
    lower = jnp.maximum(design - MOVE_LIMIT, 0.0)
    upper = jnp.minimum(design + MOVE_LIMIT, 1.0)
    target = VOLUME_FRACTION * layer_count * row_count * col_count

    def candidate(log_value):
        moved = jnp.clip(design * root * jnp.exp(-0.5 * log_value), lower, upper)
        return jnp.where(solid_mask == 1, 1.0, jnp.where(void_mask == 1, 0.0, moved))

    def volume(log_value):
        return jnp.sum(smooth(candidate(log_value)) * inverse_total)
    low_log = jnp.asarray(LOW_LOG, jnp.float32)
    high_log = jnp.asarray(HIGH_LOG, jnp.float32)
    low_volume = volume(low_log)
    high_volume = volume(high_log)
    for step in range(ITERS):
        middle = 0.5 * (low_log + high_log)
        middle_volume = volume(middle)
        above = middle_volume > target
        low_log = jnp.where(above, middle, low_log)
        low_volume = jnp.where(above, middle_volume, low_volume)
        high_log = jnp.where(above, high_log, middle)
        high_volume = jnp.where(above, high_volume, middle_volume)
    fraction = (low_volume - target) / (low_volume - high_volume)
    final = low_log + fraction * (high_log - low_log)
    return (candidate(final), sensitivity)
```

```python
import functools

import jax
import jax.numpy as jnp
from jax import lax
from jax.experimental import pallas as pl
from jax.experimental.pallas import tpu as pltpu
from jax.sharding import PartitionSpec as P

MESH = pl.DeviceIdType.MESH
F32 = jnp.float32
BF16 = jnp.bfloat16

TAPS = (1.0, 2.0, 3.0, 4.0, 3.0, 2.0, 1.0)
LOW_LOG = -25.0
HIGH_LOG = 25.0
MOVE_LIMIT = 0.2
VOLUME_FRACTION = 0.5
PENALTY = 3.0
SPLIT = 16

H = 3
Y0 = 8


def line_total(p, extent):
    low = jnp.maximum(3 - p, 0)
    high = jnp.maximum(p - (extent - 4), 0)
    missing = low * (low + 1) + high * (high + 1)
    return 16.0 - 0.5 * missing.astype(F32)


def line_spread(p, extent):
    total = None
    for d in range(-3, 4):
        near = p + d
        term = jnp.where(
            (near >= 0) & (near < extent), TAPS[d + 3] / line_total(near, extent), 0.0
        )
        total = term if total is None else total + term
    return total


def iota(shape, dim):
    return lax.broadcasted_iota(jnp.int32, shape, dim)


def split_bf16(x):
    high = x.astype(BF16)
    low = (x - high.astype(F32)).astype(BF16)
    return high, low


def dot(a, b):
    return jnp.dot(a, b, preferred_element_type=F32)


def row_filter(ref, layer, rows):
    c = [ref[layer, Y0 - H + t : Y0 - H + t + rows, :] for t in range(7)]
    return (c[0] + c[6]) + 2.0 * (c[1] + c[5]) + 3.0 * (c[2] + c[4]) + 4.0 * c[3]


def layer_filter(src, dst, layers):
    _, rows, cols = src.shape
    for r in range(0, rows, 8):
        for c in range(0, cols, 128):
            at = (slice(r, r + 8), slice(c, c + 128))
            f = [src[(k,) + at] for k in range(layers + 2 * H)]
            f = [a + b for a, b in zip(f, f[1:])]
            f = [a + b for a, b in zip(f, f[2:])]
            f = [a + b for a, b in zip(f, f[1:])]
            f = [a + b for a, b in zip(f, f[2:])]
            for k in range(layers):
                dst[(k,) + at] = f[k]


def kernel(
    nz, ny,
    disp, design, void, solid, stiff,
    new_design, sens,
    dpad, fpad, qpad, zbuf, ybuf, void_v, solid_v, energy, amount, low_v, high_v, sens_v, new_v,
    tx, k_high, k_low, cube_yx, weight_yx, inv_weight_yx, z_rows, sums,
    load_sem, store_sem, send1, recv1, send2, recv2, send_r, recv_r,
):
    lz, ly, lx = design.shape
    gz, gy = lax.axis_index("gz"), lax.axis_index("gy")
    has = {
        (1, 0): gz < nz - 1, (-1, 0): gz > 0, (0, 1): gy < ny - 1, (0, -1): gy > 0,
    }
    for dz in (-1, 1):
        for dy in (-1, 1):
            has[dz, dy] = has[dz, 0] & has[0, dy]

    def peer(dz, dy):
        return (lax.rem(gz + dz + nz, nz), lax.rem(gy + dy + ny, ny))

    own_f = fpad.at[H : H + lz, Y0 : Y0 + ly, :]
    loads = [
        pltpu.make_async_copy(disp, dpad.at[:, 0:lz, 0:ly, :], load_sem.at[0]),
        pltpu.make_async_copy(design, own_f, load_sem.at[1]),
        pltpu.make_async_copy(void, void_v, load_sem.at[2]),
        pltpu.make_async_copy(solid, solid_v, load_sem.at[3]),
    ]
    for copy in loads:
        copy.start()

    barrier = pltpu.get_barrier_semaphore()
    partners = [peer(d, 0) for d in range(1, nz)] + [peer(0, d) for d in range(1, ny)]
    partners += [peer(dz, dy) for dz in (-1, 1) for dy in (-1, 1)]
    for partner in partners:
        pl.semaphore_signal(barrier, inc=1, device_id=partner, device_id_type=MESH)

    for pad in (fpad, qpad):
        @pl.when(gz == 0)
        def _():
            pad[0:H] = jnp.zeros_like(pad[0:H])

        @pl.when(gz == nz - 1)
        def _():
            pad[lz + H :] = jnp.zeros_like(pad[lz + H :])

        @pl.when(gy == 0)
        def _():
            pad[:, 0:Y0] = jnp.zeros_like(pad[:, 0:Y0])

        @pl.when(gy == ny - 1)
        def _():
            pad[:, Y0 + ly :] = jnp.zeros_like(pad[:, Y0 + ly :])

    @pl.when(gz == nz - 1)
    def _():
        dpad[:, lz] = jnp.zeros_like(dpad[:, lz])

    @pl.when(gy == ny - 1)
    def _():
        dpad[:, :, ly:] = jnp.zeros_like(dpad[:, :, ly:])

    pl.semaphore_wait(barrier, len(partners))

    near_z = {1: slice(lz - H, lz), -1: slice(0, H), 0: slice(0, lz)}
    near_y = {1: slice(ly - H, ly), -1: slice(0, H), 0: slice(0, ly)}
    far_z = {1: slice(0, H), -1: slice(H + lz, lz + 2 * H), 0: slice(H, H + lz)}
    far_y = {1: slice(Y0 - H, Y0), -1: slice(Y0 + ly, Y0 + ly + H), 0: slice(Y0, Y0 + ly)}
    directions = [(1, 0), (-1, 0), (0, 1), (0, -1), (1, 1), (1, -1), (-1, 1), (-1, -1)]

    def halo(src, src_at, pad, send, recv, n):
        dz, dy = directions[n]
        return pltpu.make_async_remote_copy(
            src_ref=src.at[src_at[0][dz], src_at[1][dy], :],
            dst_ref=pad.at[far_z[dz], far_y[dy], :],
            send_sem=send.at[n], recv_sem=recv.at[n],
            device_id=peer(dz, dy), device_id_type=MESH,
        )

    def start(direction, copy):
        @pl.when(has[direction])
        def _():
            copy.start()

    def wait_recv(direction, copy):
        @pl.when(has[-direction[0], -direction[1]])
        def _():
            copy.wait_recv()

    def wait_send(direction, copy):
        @pl.when(has[direction])
        def _():
            copy.wait_send()

    def nodes(n, direction, layers, rows, to_layers, to_rows):
        return direction, pltpu.make_async_remote_copy(
            src_ref=disp.at[:, layers, rows, :],
            dst_ref=dpad.at[:, to_layers, to_rows, :],
            send_sem=send1.at[8 + n], recv_sem=recv1.at[8 + n],
            device_id=peer(*direction), device_id_type=MESH,
        )

    first_z, top_z = slice(0, 1), slice(lz, lz + 1)
    first_y, top_y = slice(0, 1), slice(ly, ly + 1)
    own_z, own_y = slice(0, lz), slice(0, ly)
    node_copies = [
        nodes(0, (0, -1), own_z, first_y, own_z, top_y),
        nodes(1, (-1, -1), first_z, first_y, top_z, top_y),
        nodes(2, (-1, 0), first_z, own_y, top_z, own_y),
    ]
    design_copies = [
        (directions[n], halo(design, (near_z, near_y), fpad, send1, recv1, n)) for n in range(8)
    ]
    start(*node_copies[0])
    start(*node_copies[1])
    start(*design_copies[0])
    start(*design_copies[1])
    start(*node_copies[2])
    for n in range(2, 8):
        start(*design_copies[n])

    across = jnp.abs(iota((lx, lx), 0) - iota((lx, lx), 1))
    tx[...] = jnp.maximum(4 - across, 0).astype(F32).astype(BF16)
    full_z, full_y = lz * nz, ly * ny
    row_at = iota((ly, lx), 0) + gy * ly
    col_at = iota((ly, lx), 1)
    inv_yx = 1.0 / (line_total(row_at, full_y) * line_total(col_at, lx))
    cube_yx[...] = (-PENALTY) * inv_yx * inv_yx * inv_yx
    spread_yx = line_spread(row_at, full_y) * line_spread(col_at, lx)
    weight_yx[...] = spread_yx
    inv_weight_yx[...] = 1.0 / spread_yx
    layer_at = iota((lz, lx), 0) + gz * lz
    inv_z = 1.0 / line_total(layer_at, full_z)
    spread_z = line_spread(layer_at, full_z)
    z_rows[0] = inv_z * inv_z * inv_z
    z_rows[1] = spread_z
    z_rows[2] = 1.0 / spread_z

    size = 24 * 8
    pick = (lax.shift_right_logical(iota((size, 24), 0), 3) == iota((size, 24), 1)).astype(F32).astype(BF16)
    pick_t = (iota((24, size), 0) == lax.shift_right_logical(iota((24, size), 1), 3)).astype(F32).astype(BF16)
    same = (iota((size, size), 0) & 7) == (iota((size, size), 1) & 7)
    for part, ref in zip(split_bf16(stiff[...]), (k_high, k_low)):
        spread_k = dot(dot(pick, part).astype(BF16), pick_t)
        ref[...] = jnp.where(same, spread_k, 0.0).astype(BF16)

    last_col = iota((8, lx), 1) == lx - 1

    def element_rows(k, tile):
        at = tile * 8
        u = []
        for a in range(2):
            for b in range(2):
                here = [dpad[q, k + a, pl.ds(at + b, 8), :] for q in range(3)]
                u += here
                u += [jnp.where(last_col, 0.0, pltpu.roll(v, lx - 1, 1)) for v in here]
        u = jnp.concatenate(u, axis=0)
        high = u.astype(BF16)
        forces = dot(k_high[...], high) + dot(k_low[...], high)
        terms = (2.0 * u - high.astype(F32)) * forces
        total = jnp.sum(terms.reshape(24, 8, lx), axis=0)
        energy[k, pl.ds(at, 8), :] = jnp.maximum(total, 0.0)

    tiles = ly // 8
    loads[0].wait()

    def inner_layer(k, carry):
        for tile in range(tiles - 1):
            element_rows(k, tile)
        return carry

    lax.fori_loop(0, lz - 1, inner_layer, 0)
    for copy in node_copies:
        wait_recv(*copy)

    def edge_rows(k, carry):
        element_rows(k, tiles - 1)
        return carry

    lax.fori_loop(0, lz - 1, edge_rows, 0)
    for tile in range(tiles):
        element_rows(lz - 1, tile)

    loads[1].wait()
    for copy in design_copies:
        wait_recv(*copy)
    layer_filter(fpad, zbuf, lz)

    def source_layers(first, last):
        for k in range(first, last):
            ybuf[k * ly : (k + 1) * ly, :] = row_filter(zbuf, k, ly)
        high, low = split_bf16(ybuf[first * ly : last * ly, :])
        filtered = dot(high, tx[...]) + dot(low, tx[...])
        for k in range(first, last):
            f = filtered[(k - first) * ly : (k - first + 1) * ly]
            ybuf[k * ly : (k + 1) * ly, :] = (
                f * f * energy[k] * (cube_yx[...] * z_rows[0, k : k + 1, :])
            )
        high, low = split_bf16(ybuf[first * ly : last * ly, :])
        filtered = dot(high, tx[...]) + dot(low, tx[...])
        for k in range(first, last):
            qpad[H + k, Y0 : Y0 + ly, :] = filtered[(k - first) * ly : (k - first + 1) * ly]

    own_zq = {1: slice(lz, lz + H), -1: slice(H, 2 * H), 0: slice(H, H + lz)}
    own_yq = {1: slice(Y0 + ly - H, Y0 + ly), -1: slice(Y0, Y0 + H), 0: slice(Y0, Y0 + ly)}
    source_copies = [
        (directions[n], halo(qpad, (own_zq, own_yq), qpad, send2, recv2, n)) for n in range(8)
    ]
    source_layers(lz - H, lz)
    start(*source_copies[0])
    source_layers(0, H)
    start(*source_copies[1])
    for n in range(4, 8):
        start(*source_copies[n])
    source_layers(H, lz // 2)
    source_layers(lz // 2, lz - H)
    start(*source_copies[2])
    start(*source_copies[3])

    loads[2].wait()
    loads[3].wait()

    def bounds(k, carry):
        weight = weight_yx[...] * z_rows[1, pl.ds(k, 1), :]
        d = fpad[H + k, Y0 : Y0 + ly, :]
        is_solid, is_void = solid_v[k] == 1, void_v[k] == 1
        low = jnp.maximum(d - MOVE_LIMIT, 0.0) * weight
        high = jnp.minimum(d + MOVE_LIMIT, 1.0) * weight
        low_v[k] = jnp.where(is_solid, weight, jnp.where(is_void, 0.0, low))
        high_v[k] = jnp.where(is_solid, weight, jnp.where(is_void, 0.0, high))
        return carry

    lax.fori_loop(0, lz, bounds, 0)

    for copy in source_copies:
        wait_recv(*copy)
    layer_filter(qpad, zbuf, lz)
    for k in range(lz):
        s = row_filter(zbuf, k, ly)
        sens_v[k] = s
        d = fpad[H + k, Y0 : Y0 + ly, :]
        amount[k] = d * jnp.sqrt(-s * (weight_yx[...] * z_rows[1, k : k + 1, :]))
    store_sens = pltpu.make_async_copy(sens_v, sens, store_sem.at[0])
    store_sens.start()

    lane = iota((1, 128), 1)
    points = SPLIT + 1
    rows_p = -(-points // 8) * 8

    def exchange(row, n, axis_at, size, to):
        slot = pl.ds(axis_at, 1)
        sums[n, slot, :] = row
        copies = []
        for d in range(1, size):
            copies.append(
                pltpu.make_async_remote_copy(
                    src_ref=sums.at[n, slot, :], dst_ref=sums.at[n, slot, :],
                    send_sem=send_r.at[n], recv_sem=recv_r.at[n],
                    device_id=to(d), device_id_type=MESH,
                )
            )
        for copy in copies:
            copy.start()
        everyone = sums.at[n, pl.ds(0, size - 1), :]
        pltpu.make_async_copy(everyone, everyone, recv_r.at[n]).wait()
        total = jnp.sum(sums[n, 0:size, :], axis=0, keepdims=True)
        return total

    def volumes(scale, step, first):
        factors = [first * 2.718281828459045 ** (-0.5 * step * j) for j in range(points)]

        def layer(k, totals):
            totals = list(totals)
            for r in range(0, ly, 8):
                for c in range(0, lx, 128):
                    at = (k, slice(r, r + 8), slice(c, c + 128))
                    a, low, high = amount[at], low_v[at], high_v[at]
                    if scale is not None:
                        a = a * scale
                    for j in range(points):
                        totals[j] = totals[j] + jnp.minimum(jnp.maximum(a * factors[j], low), high)
            return tuple(totals)

        totals = lax.fori_loop(
            0, lz, layer, tuple(jnp.zeros((8, 128), F32) for _ in range(points))
        )
        sub = iota((rows_p, 128), 0)
        stacked = jnp.zeros((rows_p, 128), F32)
        for j in range(points):
            stacked = jnp.where(sub == j, jnp.sum(totals[j], axis=0, keepdims=True), stacked)
        line = jnp.sum(stacked, axis=1, keepdims=True)
        return jnp.sum(jnp.where(sub == iota((rows_p, 128), 1), line, 0.0), axis=0, keepdims=True)

    def everywhere(row, n):
        row = exchange(row, 2 * n, gz, nz, lambda d: peer(d, 0))
        return exchange(row, 2 * n + 1, gy, ny, lambda d: peer(0, d))

    target = VOLUME_FRACTION * full_z * full_y * lx
    inside = (lane >= 1) & (lane < SPLIT)

    def cell(row):
        above = jnp.where(inside & (row > target), 1.0, 0.0)
        return jnp.sum(above, axis=1, keepdims=True)

    wide = (HIGH_LOG - LOW_LOG) / SPLIT
    fine = wide / SPLIT
    row = everywhere(volumes(None, wide, 2.718281828459045 ** (-0.5 * LOW_LOG)), 0)
    low = LOW_LOG + wide * cell(row)
    row = everywhere(volumes(jnp.exp(-0.5 * low), fine, 1.0), 1)
    index = cell(row)
    at_lane = lane.astype(F32)
    low_volume = jnp.sum(jnp.where(at_lane == index, row, 0.0), axis=1, keepdims=True)
    high_volume = jnp.sum(jnp.where(at_lane == index + 1.0, row, 0.0), axis=1, keepdims=True)
    low = low + fine * index
    final = low + fine * ((low_volume - target) / (low_volume - high_volume))
    factor = jnp.exp(-0.5 * final)

    def finish(k, carry):
        d = fpad[H + k, Y0 : Y0 + ly, :]
        moved = amount[k] * (inv_weight_yx[...] * (z_rows[2, pl.ds(k, 1), :] * factor))
        moved = jnp.minimum(
            jnp.maximum(moved, jnp.maximum(d - MOVE_LIMIT, 0.0)), jnp.minimum(d + MOVE_LIMIT, 1.0)
        )
        new_v[k] = jnp.where(solid_v[k] == 1, 1.0, jnp.where(void_v[k] == 1, 0.0, moved))
        return carry

    lax.fori_loop(0, lz, finish, 0)
    store_new = pltpu.make_async_copy(new_v, new_design, store_sem.at[1])
    store_new.start()

    for copy in node_copies + design_copies + source_copies:
        wait_send(*copy)
    for n, size in enumerate((nz, ny, nz, ny)):
        everyone = sums.at[n, pl.ds(0, size - 1), :]
        pltpu.make_async_copy(everyone, everyone, send_r.at[n]).wait()
    store_sens.wait()
    store_new.wait()


def per_device(displacement, design, void_mask, solid_mask, stiffness):
    nz, ny = lax.axis_size("gz"), lax.axis_size("gy")
    lz, ly, lx = design.shape
    brick = jax.ShapeDtypeStruct(design.shape, F32)
    padded = (lz + 2 * H, ly + 16, lx)
    anywhere = pl.BlockSpec(memory_space=pl.ANY)
    new_design, sens = pl.pallas_call(
        functools.partial(kernel, nz, ny),
        out_shape=(brick, brick),
        in_specs=[anywhere] * 4 + [pl.BlockSpec(memory_space=pltpu.VMEM)],
        out_specs=(anywhere, anywhere),
        scratch_shapes=[
            pltpu.VMEM((3, lz + 1, ly + 8, lx), F32),
            pltpu.VMEM(padded, F32),
            pltpu.VMEM(padded, F32),
            pltpu.VMEM((lz, ly + 16, lx), F32),
            pltpu.VMEM((lz * ly, lx), F32),
            pltpu.VMEM(design.shape, jnp.int32),
            pltpu.VMEM(design.shape, jnp.int32),
            pltpu.VMEM(design.shape, F32),
            pltpu.VMEM(design.shape, F32),
            pltpu.VMEM(design.shape, F32),
            pltpu.VMEM(design.shape, F32),
            pltpu.VMEM(design.shape, F32),
            pltpu.VMEM(design.shape, F32),
            pltpu.VMEM((lx, lx), BF16),
            pltpu.VMEM((192, 192), BF16),
            pltpu.VMEM((192, 192), BF16),
            pltpu.VMEM((ly, lx), F32),
            pltpu.VMEM((ly, lx), F32),
            pltpu.VMEM((ly, lx), F32),
            pltpu.VMEM((3, lz, lx), F32),
            pltpu.VMEM((4, max(nz, ny), 128), F32),
            pltpu.SemaphoreType.DMA((4,)),
            pltpu.SemaphoreType.DMA((2,)),
            pltpu.SemaphoreType.DMA((11,)),
            pltpu.SemaphoreType.DMA((11,)),
            pltpu.SemaphoreType.DMA((8,)),
            pltpu.SemaphoreType.DMA((8,)),
            pltpu.SemaphoreType.DMA((4,)),
            pltpu.SemaphoreType.DMA((4,)),
        ],
        compiler_params=pltpu.CompilerParams(
            collective_id=0, has_side_effects=True, vmem_limit_bytes=40 * 1024 * 1024
        ),
    )(displacement, design, void_mask, solid_mask, stiffness)
    return new_design, sens


def solution(mesh):
    return jax.shard_map(
        per_device,
        mesh=mesh,
        in_specs=(
            P(None, "gz", "gy", None),
            P("gz", "gy", None),
            P("gz", "gy", None),
            P("gz", "gy", None),
            P(),
        ),
        out_specs=(P("gz", "gy", None), P("gz", "gy", None)),
        check_vma=False,
    )
```

```python
import functools

import jax
import jax.numpy as jnp
from jax import lax
from jax.experimental import pallas as pl
from jax.experimental.pallas import tpu as pltpu
from jax.sharding import PartitionSpec as P

MESH = pl.DeviceIdType.MESH
F32 = jnp.float32
BF16 = jnp.bfloat16

TAPS = (1.0, 2.0, 3.0, 4.0, 3.0, 2.0, 1.0)
LOW_LOG = -25.0
HIGH_LOG = 25.0
MOVE_LIMIT = 0.2
VOLUME_FRACTION = 0.5
PENALTY = 3.0
SPLIT = 16

H = 3
Y0 = 8


def line_total(p, extent):
    low = jnp.maximum(3 - p, 0)
    high = jnp.maximum(p - (extent - 4), 0)
    missing = low * (low + 1) + high * (high + 1)
    return 16.0 - 0.5 * missing.astype(F32)


def line_spread(p, extent):
    total = None
    for d in range(-3, 4):
        near = p + d
        term = jnp.where(
            (near >= 0) & (near < extent), TAPS[d + 3] / line_total(near, extent), 0.0
        )
        total = term if total is None else total + term
    return total


def iota(shape, dim):
    return lax.broadcasted_iota(jnp.int32, shape, dim)


def split_bf16(x):
    high = x.astype(BF16)
    low = (x - high.astype(F32)).astype(BF16)
    return high, low


def dot(a, b):
    return jnp.dot(a, b, preferred_element_type=F32)


def row_filter(ref, layer, rows, first=0):
    at = Y0 - H + first
    c = [ref[layer, at + t : at + t + rows, :] for t in range(7)]
    return (c[0] + c[6]) + 2.0 * (c[1] + c[5]) + 3.0 * (c[2] + c[4]) + 4.0 * c[3]


def layer_filter(src, dst, layers):
    _, rows, cols = src.shape
    for r in range(0, rows, 8):
        for c in range(0, cols, 128):
            at = (slice(r, r + 8), slice(c, c + 128))
            f = [src[(k,) + at] for k in range(layers + 2 * H)]
            f = [a + b for a, b in zip(f, f[1:])]
            f = [a + b for a, b in zip(f, f[2:])]
            f = [a + b for a, b in zip(f, f[1:])]
            f = [a + b for a, b in zip(f, f[2:])]
            for k in range(layers):
                dst[(k,) + at] = f[k]


def kernel(
    nz, ny,
    disp, design, void, solid, stiff,
    new_design, sens,
    dpad, fpad, qpad, zbuf, void_v, solid_v, energy, amount, low_v, high_v, sens_v, new_v,
    tx, k_high, k_low, cube_yx, weight_yx, inv_weight_yx, z_rows, sums,
    load_sem, store_sem, send1, recv1, send2, recv2, send_r, recv_r, known,
):
    lz, ly, lx = design.shape
    gz, gy = lax.axis_index("gz"), lax.axis_index("gy")
    has = {
        (1, 0): gz < nz - 1, (-1, 0): gz > 0, (0, 1): gy < ny - 1, (0, -1): gy > 0,
    }
    for dz in (-1, 1):
        for dy in (-1, 1):
            has[dz, dy] = has[dz, 0] & has[0, dy]

    def peer(dz, dy):
        return (lax.rem(gz + dz + nz, nz), lax.rem(gy + dy + ny, ny))

    own_f = fpad.at[H : H + lz, Y0 : Y0 + ly, :]
    loads = [
        pltpu.make_async_copy(disp, dpad.at[:, 0:lz, 0:ly, :], load_sem.at[0]),
        pltpu.make_async_copy(design, own_f, load_sem.at[1]),
        pltpu.make_async_copy(void, void_v, load_sem.at[2]),
        pltpu.make_async_copy(solid, solid_v, load_sem.at[3]),
    ]
    for copy in loads:
        copy.start()

    barrier = pltpu.get_barrier_semaphore()
    partners = [peer(1, 0), peer(-1, 0), peer(0, 1), peer(0, -1)]
    partners += [peer(dz, dy) for dz in (-1, 1) for dy in (-1, 1)]
    for partner in partners:
        pl.semaphore_signal(barrier, inc=1, device_id=partner, device_id_type=MESH)

    def tell(level):
        reach = 1 << level
        for axis, way in enumerate(((reach, 0), (0, reach))):
            for sign in (1, -1):
                pl.semaphore_signal(
                    known.at[2 * level + axis], inc=1,
                    device_id=peer(sign * way[0], sign * way[1]), device_id_type=MESH,
                )

    def hear(level):
        for axis in range(2):
            pl.semaphore_wait(known.at[2 * level + axis], 2)

    for pad in (fpad, qpad):
        @pl.when(gz == 0)
        def _():
            pad[0:H] = jnp.zeros_like(pad[0:H])

        @pl.when(gz == nz - 1)
        def _():
            pad[lz + H :] = jnp.zeros_like(pad[lz + H :])

        @pl.when(gy == 0)
        def _():
            pad[:, 0:Y0] = jnp.zeros_like(pad[:, 0:Y0])

        @pl.when(gy == ny - 1)
        def _():
            pad[:, Y0 + ly :] = jnp.zeros_like(pad[:, Y0 + ly :])

    @pl.when(gz == nz - 1)
    def _():
        dpad[:, lz] = jnp.zeros_like(dpad[:, lz])

    @pl.when(gy == ny - 1)
    def _():
        dpad[:, :, ly:] = jnp.zeros_like(dpad[:, :, ly:])

    pl.semaphore_wait(barrier, len(partners))
    tell(0)

    near_z = {1: slice(lz - H, lz), -1: slice(0, H), 0: slice(0, lz)}
    near_y = {1: slice(ly - H, ly), -1: slice(0, H), 0: slice(0, ly)}
    far_z = {1: slice(0, H), -1: slice(H + lz, lz + 2 * H), 0: slice(H, H + lz)}
    far_y = {1: slice(Y0 - H, Y0), -1: slice(Y0 + ly, Y0 + ly + H), 0: slice(Y0, Y0 + ly)}
    directions = [(1, 0), (-1, 0), (0, 1), (0, -1), (1, 1), (1, -1), (-1, 1), (-1, -1)]

    def halo(src, src_at, pad, send, recv, n):
        dz, dy = directions[n]
        return pltpu.make_async_remote_copy(
            src_ref=src.at[src_at[0][dz], src_at[1][dy], :],
            dst_ref=pad.at[far_z[dz], far_y[dy], :],
            send_sem=send.at[n], recv_sem=recv.at[n],
            device_id=peer(dz, dy), device_id_type=MESH,
        )

    def start(direction, copy):
        @pl.when(has[direction])
        def _():
            copy.start()

    def wait_recv(direction, copy):
        @pl.when(has[-direction[0], -direction[1]])
        def _():
            copy.wait_recv()

    def wait_send(direction, copy):
        @pl.when(has[direction])
        def _():
            copy.wait_send()

    def nodes(n, direction, layers, rows, to_layers, to_rows):
        return direction, pltpu.make_async_remote_copy(
            src_ref=disp.at[:, layers, rows, :],
            dst_ref=dpad.at[:, to_layers, to_rows, :],
            send_sem=send1.at[8 + n], recv_sem=recv1.at[8 + n],
            device_id=peer(*direction), device_id_type=MESH,
        )

    first_z, top_z = slice(0, 1), slice(lz, lz + 1)
    first_y, top_y = slice(0, 1), slice(ly, ly + 1)
    own_z, own_y = slice(0, lz), slice(0, ly)
    node_copies = [
        nodes(0, (0, -1), own_z, first_y, own_z, top_y),
        nodes(1, (-1, -1), first_z, first_y, top_z, top_y),
        nodes(2, (-1, 0), first_z, own_y, top_z, own_y),
    ]
    design_copies = [
        (directions[n], halo(design, (near_z, near_y), fpad, send1, recv1, n)) for n in range(8)
    ]
    start(*design_copies[0])
    start(*design_copies[1])
    start(*node_copies[0])
    start(*node_copies[1])
    for n in range(2, 8):
        start(*design_copies[n])

    across = jnp.abs(iota((lx, lx), 0) - iota((lx, lx), 1))
    tx[...] = jnp.maximum(4 - across, 0).astype(F32).astype(BF16)
    full_z, full_y = lz * nz, ly * ny
    row_at = iota((ly, lx), 0) + gy * ly
    col_at = iota((ly, lx), 1)
    inv_yx = 1.0 / (line_total(row_at, full_y) * line_total(col_at, lx))
    cube_yx[...] = (-PENALTY) * inv_yx * inv_yx * inv_yx
    spread_yx = line_spread(row_at, full_y) * line_spread(col_at, lx)
    weight_yx[...] = spread_yx
    inv_weight_yx[...] = 1.0 / spread_yx
    layer_at = iota((lz, lx), 0) + gz * lz
    inv_z = 1.0 / line_total(layer_at, full_z)
    spread_z = line_spread(layer_at, full_z)
    z_rows[0] = inv_z * inv_z * inv_z
    z_rows[1] = spread_z
    z_rows[2] = 1.0 / spread_z

    size = 24 * 8
    pick = (lax.shift_right_logical(iota((size, 24), 0), 3) == iota((size, 24), 1)).astype(F32).astype(BF16)
    pick_t = (iota((24, size), 0) == lax.shift_right_logical(iota((24, size), 1), 3)).astype(F32).astype(BF16)
    same = (iota((size, size), 0) & 7) == (iota((size, size), 1) & 7)
    for part, ref in zip(split_bf16(stiff[...]), (k_high, k_low)):
        spread_k = dot(dot(pick, part).astype(BF16), pick_t)
        ref[...] = jnp.where(same, spread_k, 0.0).astype(BF16)

    last_col = iota((8, lx), 1) == lx - 1

    def element_rows(k, tile):
        at = tile * 8
        u = []
        for a in range(2):
            for b in range(2):
                here = [dpad[q, k + a, pl.ds(at + b, 8), :] for q in range(3)]
                u += here
                u += [jnp.where(last_col, 0.0, pltpu.roll(v, lx - 1, 1)) for v in here]
        u = jnp.concatenate(u, axis=0)
        high = u.astype(BF16)
        forces = dot(k_high[...], high) + dot(k_low[...], high)
        terms = (2.0 * u - high.astype(F32)) * forces
        total = jnp.sum(terms.reshape(24, 8, lx), axis=0)
        energy[k, pl.ds(at, 8), :] = jnp.maximum(total, 0.0)

    tiles = ly // 8

    def energy_of(count, layer_of, tiles_of):
        def body(n, carry):
            for k in layer_of(n):
                for tile in tiles_of:
                    element_rows(k, tile)
            return carry

        lax.fori_loop(0, count, body, 0)

    loads[0].wait()
    inner = lz - 2 * H
    energy_of(2 * H - 1, lambda n: [n + (n // H) * inner], range(tiles - 1))
    start(*node_copies[2])
    hear(0)
    tell(1)
    energy_of(inner // 2, lambda n: [H + 2 * n, H + 2 * n + 1], [0])
    wait_recv(*node_copies[0])
    wait_recv(*node_copies[1])
    energy_of((lz - 1) // 3, lambda n: [3 * n, 3 * n + 1, 3 * n + 2], [tiles - 1])

    loads[1].wait()
    for copy in design_copies:
        wait_recv(*copy)
    layer_filter(fpad, zbuf, lz)

    def source(layers, first, last):
        n = last - first
        f = jnp.concatenate([row_filter(zbuf, k, n, first) for k in layers], axis=0)
        high, low = split_bf16(f)
        f = dot(high, tx[...]) + dot(low, tx[...])
        cube = cube_yx[first:last]
        f = jnp.concatenate(
            [
                f[i * n : (i + 1) * n] * f[i * n : (i + 1) * n]
                * (energy[k, first:last] * (cube * z_rows[0, k : k + 1, :]))
                for i, k in enumerate(layers)
            ],
            axis=0,
        )
        high, low = split_bf16(f)
        f = dot(high, tx[...]) + dot(low, tx[...])
        for i, k in enumerate(layers):
            qpad[H + k, Y0 + first : Y0 + last, :] = f[i * n : (i + 1) * n]

    own_zq = {1: slice(lz, lz + H), -1: slice(H, 2 * H), 0: slice(H, H + lz)}
    own_yq = {1: slice(Y0 + ly - H, Y0 + ly), -1: slice(Y0, Y0 + H), 0: slice(Y0, Y0 + ly)}
    source_copies = [
        (directions[n], halo(qpad, (own_zq, own_yq), qpad, send2, recv2, n)) for n in range(8)
    ]
    source(range(H), 0, ly)
    start(*source_copies[1])
    start(*source_copies[6])
    start(*source_copies[7])
    wait_recv(*node_copies[2])
    for tile in range(tiles):
        element_rows(lz - 1, tile)
    source(range(lz - H, lz), 0, ly)
    start(*source_copies[0])
    start(*source_copies[4])
    start(*source_copies[5])
    middle = range(H, lz - H)
    source(middle, 0, 8)
    start(*source_copies[3])
    source(middle, ly - 8, ly)
    start(*source_copies[2])
    hear(1)
    tell(2)
    energy_of(inner // 2, lambda n: [H + 2 * n, H + 2 * n + 1], range(1, tiles - 1))
    source(range(H, lz // 2), 8, ly - 8)
    source(range(lz // 2, lz - H), 8, ly - 8)

    loads[2].wait()
    loads[3].wait()

    def bounds(k, carry):
        weight = weight_yx[...] * z_rows[1, pl.ds(k, 1), :]
        d = fpad[H + k, Y0 : Y0 + ly, :]
        is_solid, is_void = solid_v[k] == 1, void_v[k] == 1
        low = jnp.maximum(d - MOVE_LIMIT, 0.0) * weight
        high = jnp.minimum(d + MOVE_LIMIT, 1.0) * weight
        low_v[k] = jnp.where(is_solid, weight, jnp.where(is_void, 0.0, low))
        high_v[k] = jnp.where(is_solid, weight, jnp.where(is_void, 0.0, high))
        return carry

    lax.fori_loop(0, lz, bounds, 0)

    for copy in source_copies:
        wait_recv(*copy)
    layer_filter(qpad, zbuf, lz)
    for k in range(lz):
        s = row_filter(zbuf, k, ly)
        sens_v[k] = s
        d = fpad[H + k, Y0 : Y0 + ly, :]
        amount[k] = d * jnp.sqrt(-s * (weight_yx[...] * z_rows[1, k : k + 1, :]))
    store_sens = pltpu.make_async_copy(sens_v, sens, store_sem.at[0])
    store_sens.start()

    lane = iota((1, 128), 1)
    points = SPLIT + 1
    rows_p = -(-points // 8) * 8

    def exchange(row, n, axis_at, size, to):
        sums[n, axis_at] = row
        copies = []
        for d in range(1, size):
            copies.append(
                pltpu.make_async_remote_copy(
                    src_ref=sums.at[n, axis_at], dst_ref=sums.at[n, axis_at],
                    send_sem=send_r.at[n], recv_sem=recv_r.at[n],
                    device_id=to(d), device_id_type=MESH,
                )
            )
        for copy in copies:
            copy.start()
        everyone = sums.at[n, 0 : size - 1]
        pltpu.make_async_copy(everyone, everyone, recv_r.at[n]).wait()
        return jnp.sum(sums[n, 0:size], axis=0)

    def volumes(scale, step, first, at_lanes):
        factors = [first * 2.718281828459045 ** (-0.5 * step * j) for j in at_lanes]
        points = len(factors)

        def layer(k, totals):
            totals = list(totals)
            for r in range(0, ly, 8):
                for c in range(0, lx, 128):
                    at = (k, slice(r, r + 8), slice(c, c + 128))
                    a, low, high = amount[at], low_v[at], high_v[at]
                    if scale is not None:
                        a = a * scale
                    for j in range(points):
                        totals[j] = totals[j] + jnp.minimum(jnp.maximum(a * factors[j], low), high)
            return tuple(totals)

        totals = lax.fori_loop(
            0, lz, layer, tuple(jnp.zeros((8, 128), F32) for _ in range(points))
        )
        sub = iota((rows_p, 128), 0)
        stacked = jnp.zeros((rows_p, 128), F32)
        for j in range(points):
            stacked = jnp.where(sub == at_lanes[j], jnp.sum(totals[j], axis=0, keepdims=True), stacked)
        line = jnp.sum(stacked, axis=1, keepdims=True)
        return jnp.sum(jnp.where(sub == iota((rows_p, 128), 1), line, 0.0), axis=0, keepdims=True)

    def everywhere(row, n):
        row = exchange(row, 2 * n, gz, nz, lambda d: peer(d, 0))
        return exchange(row, 2 * n + 1, gy, ny, lambda d: peer(0, d))

    target = VOLUME_FRACTION * full_z * full_y * lx
    inside = (lane >= 1) & (lane < SPLIT)

    def cell(row):
        above = jnp.where(inside & (row > target), 1.0, 0.0)
        return jnp.sum(above, axis=1, keepdims=True)

    wide = (HIGH_LOG - LOW_LOG) / SPLIT
    fine = wide / SPLIT
    at_lane = lane.astype(F32)

    def entry(row, index):
        return jnp.sum(jnp.where(at_lane == index, row, 0.0), axis=1, keepdims=True)

    start_factor = 2.718281828459045 ** (-0.5 * LOW_LOG)
    hear(2)
    row = everywhere(volumes(None, wide, start_factor, range(points)), 0)
    index = cell(row)
    low = LOW_LOG + wide * index
    ends = (entry(row, index), entry(row, index + 1.0))
    row = everywhere(volumes(jnp.exp(-0.5 * low), fine, 1.0, range(1, SPLIT)), 1)
    row = jnp.where(lane == 0, ends[0], jnp.where(lane == SPLIT, ends[1], row))
    index = cell(row)
    low_volume, high_volume = entry(row, index), entry(row, index + 1.0)
    low = low + fine * index
    final = low + fine * ((low_volume - target) / (low_volume - high_volume))
    factor = jnp.exp(-0.5 * final)

    def finish(k, carry):
        d = fpad[H + k, Y0 : Y0 + ly, :]
        moved = amount[k] * (inv_weight_yx[...] * (z_rows[2, pl.ds(k, 1), :] * factor))
        moved = jnp.minimum(
            jnp.maximum(moved, jnp.maximum(d - MOVE_LIMIT, 0.0)), jnp.minimum(d + MOVE_LIMIT, 1.0)
        )
        new_v[k] = jnp.where(solid_v[k] == 1, 1.0, jnp.where(void_v[k] == 1, 0.0, moved))
        return carry

    lax.fori_loop(0, lz, finish, 0)
    store_new = pltpu.make_async_copy(new_v, new_design, store_sem.at[1])
    store_new.start()

    for copy in node_copies + design_copies + source_copies:
        wait_send(*copy)
    for n, size in enumerate((nz, ny, nz, ny)):
        everyone = sums.at[n, 0 : size - 1]
        pltpu.make_async_copy(everyone, everyone, send_r.at[n]).wait()
    store_sens.wait()
    store_new.wait()


def per_device(displacement, design, void_mask, solid_mask, stiffness):
    nz, ny = lax.axis_size("gz"), lax.axis_size("gy")
    lz, ly, lx = design.shape
    brick = jax.ShapeDtypeStruct(design.shape, F32)
    padded = (lz + 2 * H, ly + 16, lx)
    anywhere = pl.BlockSpec(memory_space=pltpu.HBM)
    new_design, sens = pl.pallas_call(
        functools.partial(kernel, nz, ny),
        out_shape=(brick, brick),
        in_specs=[anywhere] * 4 + [pl.BlockSpec(memory_space=pltpu.VMEM)],
        out_specs=(anywhere, anywhere),
        scratch_shapes=[
            pltpu.VMEM((3, lz + 1, ly + 8, lx), F32),
            pltpu.VMEM(padded, F32),
            pltpu.VMEM(padded, F32),
            pltpu.VMEM((lz, ly + 16, lx), F32),
            pltpu.VMEM(design.shape, jnp.int32),
            pltpu.VMEM(design.shape, jnp.int32),
            pltpu.VMEM(design.shape, F32),
            pltpu.VMEM(design.shape, F32),
            pltpu.VMEM(design.shape, F32),
            pltpu.VMEM(design.shape, F32),
            pltpu.VMEM(design.shape, F32),
            pltpu.VMEM(design.shape, F32),
            pltpu.VMEM((lx, lx), BF16),
            pltpu.VMEM((192, 192), BF16),
            pltpu.VMEM((192, 192), BF16),
            pltpu.VMEM((ly, lx), F32),
            pltpu.VMEM((ly, lx), F32),
            pltpu.VMEM((ly, lx), F32),
            pltpu.VMEM((3, lz, lx), F32),
            pltpu.VMEM((4, max(nz, ny), 1, 128), F32),
            pltpu.SemaphoreType.DMA((4,)),
            pltpu.SemaphoreType.DMA((2,)),
            pltpu.SemaphoreType.DMA((11,)),
            pltpu.SemaphoreType.DMA((11,)),
            pltpu.SemaphoreType.DMA((8,)),
            pltpu.SemaphoreType.DMA((8,)),
            pltpu.SemaphoreType.DMA((4,)),
            pltpu.SemaphoreType.DMA((4,)),
            pltpu.SemaphoreType.REGULAR((6,)),
        ],
        compiler_params=pltpu.CompilerParams(
            collective_id=0, has_side_effects=True, vmem_limit_bytes=60 * 1024 * 1024
        ),
    )(displacement, design, void_mask, solid_mask, stiffness)
    return new_design, sens


def solution(mesh):
    return jax.shard_map(
        per_device,
        mesh=mesh,
        in_specs=(
            P(None, "gz", "gy", None),
            P("gz", "gy", None),
            P("gz", "gy", None),
            P("gz", "gy", None),
            P(),
        ),
        out_specs=(P("gz", "gy", None), P("gz", "gy", None)),
        check_vma=False,
    )
```

```python
import functools

import jax
import jax.numpy as jnp
from jax import lax
from jax.experimental import pallas as pl
from jax.experimental.pallas import tpu as pltpu
from jax.sharding import PartitionSpec as P

MESH = pl.DeviceIdType.MESH
NEAR_Z = [(d, 0) for d in (2, -2, 3, -3, 4, -4, 5, -5, 6, -6)]
NEAR_Y = [(0, d) for d in (2, -2, 8, 7, 9, 6, 10)]
F32 = jnp.float32
BF16 = jnp.bfloat16

TAPS = (1.0, 2.0, 3.0, 4.0, 3.0, 2.0, 1.0)
LOW_LOG = -25.0
HIGH_LOG = 25.0
MOVE_LIMIT = 0.2
VOLUME_FRACTION = 0.5
PENALTY = 3.0
SPLIT = 16
GRID = SPLIT * SPLIT
FINE = (HIGH_LOG - LOW_LOG) / GRID
ROUGH = 64
WINDOW = 14
E = 2.718281828459045

H = 3
Y0 = 8


def line_total(p, extent):
    low = jnp.maximum(3 - p, 0)
    high = jnp.maximum(p - (extent - 4), 0)
    missing = low * (low + 1) + high * (high + 1)
    return 16.0 - 0.5 * missing.astype(F32)


def line_spread(p, extent):
    total = None
    for d in range(-3, 4):
        near = p + d
        term = jnp.where(
            (near >= 0) & (near < extent), TAPS[d + 3] / line_total(near, extent), 0.0
        )
        total = term if total is None else total + term
    return total


def iota(shape, dim):
    return lax.broadcasted_iota(jnp.int32, shape, dim)


def split_bf16(x):
    high = x.astype(BF16)
    low = (x - high.astype(F32)).astype(BF16)
    return high, low


def dot(a, b):
    return jnp.dot(a, b, preferred_element_type=F32)


def row_filter(ref, layer, rows, first=0):
    at = Y0 - H + first
    c = [ref[layer, at + t : at + t + rows, :] for t in range(7)]
    return (c[0] + c[6]) + 2.0 * (c[1] + c[5]) + 3.0 * (c[2] + c[4]) + 4.0 * c[3]


def layer_filter(src, dst, layers, first=0, rows=None, first_row=0):
    rows = src.shape[1] if rows is None else rows
    for r in range(0, rows, 8):
        for c in range(0, src.shape[2], 128):
            col = slice(c, c + 128)
            f = [src[first + k, first_row + r : first_row + r + 8, col] for k in range(layers + 2 * H)]
            f = [a + b for a, b in zip(f, f[1:])]
            f = [a + b for a, b in zip(f, f[2:])]
            f = [a + b for a, b in zip(f, f[1:])]
            f = [a + b for a, b in zip(f, f[2:])]
            for k in range(layers):
                dst[k, r : r + 8, col] = f[k]


def sum_start(n, row, at, size, to, sums, send, recv):
    sums[n, at] = row
    copies = [
        pltpu.make_async_remote_copy(
            src_ref=sums.at[n, at], dst_ref=sums.at[n, at],
            send_sem=send.at[n], recv_sem=recv.at[n],
            device_id=to(d), device_id_type=MESH,
        )
        for d in range(1, size)
    ]
    for copy in copies:
        copy.start()


def sum_finish(n, size, sums, recv):
    everyone = sums.at[n, 0 : size - 1]
    pltpu.make_async_copy(everyone, everyone, recv.at[n]).wait()
    return jnp.sum(sums[n, 0:size], axis=0)


def sum_sent(n, size, sums, send):
    everyone = sums.at[n, 0 : size - 1]
    pltpu.make_async_copy(everyone, everyone, send.at[n]).wait()


def to_lanes(rows, lanes):
    count = -(-(max(lanes) + 1) // 8) * 8
    sub = iota((count, 128), 0)
    stacked = jnp.zeros((count, 128), F32)
    for row, j in zip(rows, lanes):
        stacked = jnp.where(sub == j, jnp.sum(row, axis=0, keepdims=True), stacked)
    line = jnp.sum(stacked, axis=1, keepdims=True)
    return jnp.sum(jnp.where(sub == iota((count, 128), 1), line, 0.0), axis=0, keepdims=True)


def volumes(amount, low_v, high_v, scale, factors, lanes):
    lz, ly, lx = amount.shape

    def layer(k, totals):
        totals = list(totals)
        for r in range(0, ly, 8):
            for c in range(0, lx, 128):
                at = (k, slice(r, r + 8), slice(c, c + 128))
                a, low, high = amount[at], low_v[at], high_v[at]
                if scale is not None:
                    a = a * scale
                for j, factor in enumerate(factors):
                    totals[j] = totals[j] + jnp.minimum(jnp.maximum(a * factor, low), high)
        return tuple(totals)

    totals = lax.fori_loop(0, lz, layer, tuple(jnp.zeros((8, 128), F32) for _ in factors))
    return to_lanes(totals, lanes)


def count_above(row, inside, target):
    return jnp.sum(jnp.where(inside & (row > target), 1.0, 0.0), axis=1, keepdims=True)


def entry(row, index):
    at = iota(row.shape, 1).astype(F32)
    return jnp.sum(jnp.where(at == index, row, 0.0), axis=1, keepdims=True)


def secant(low, low_volume, high_volume, target):
    return low + FINE * ((low_volume - target) / (low_volume - high_volume))


def weights(ref, z_ref, gy, ny, gz, nz):
    ly, lx = ref.shape
    lz = z_ref.shape[0]
    ref[...] = line_spread(iota((ly, lx), 0) + gy * ly, ly * ny) * line_spread(iota((ly, lx), 1), lx)
    z_ref[...] = line_spread(iota((lz, lx), 0) + gz * lz, lz * nz)


def bounds(weight, d, solid, void):
    low = jnp.maximum(d - MOVE_LIMIT, 0.0) * weight
    high = jnp.minimum(d + MOVE_LIMIT, 1.0) * weight
    is_solid, is_void = solid == 1, void == 1
    low = jnp.where(is_solid, weight, jnp.where(is_void, 0.0, low))
    high = jnp.where(is_solid, weight, jnp.where(is_void, 0.0, high))
    return low, high


def finished(a, weight, factor, d, solid, void):
    moved = (a / weight) * factor
    moved = jnp.minimum(
        jnp.maximum(moved, jnp.maximum(d - MOVE_LIMIT, 0.0)), jnp.minimum(d + MOVE_LIMIT, 1.0)
    )
    return jnp.where(solid == 1, 1.0, jnp.where(void == 1, 0.0, moved))


def total_target(lz, ly, lx, nz, ny):
    return VOLUME_FRACTION * (lz * nz) * (ly * ny) * lx


def kernel(
    nz, ny,
    disp, design, void, solid, stiff,
    new_design, sens, found,
    dpad, fpad, qpad, zbuf, void_v, solid_v, energy, amount, low_v, high_v, sens_v, new_v,
    tx, k_high, k_low, cube_yx, weight_yx, cube_z, weight_z, zs, qs, zq, sums,
    load_sem, store_sem, send1, recv1, send2, recv2, send_r, recv_r, known,
):
    lz, ly, lx = design.shape
    gz, gy = lax.axis_index("gz"), lax.axis_index("gy")
    has = {
        (1, 0): gz < nz - 1, (-1, 0): gz > 0, (0, 1): gy < ny - 1, (0, -1): gy > 0,
    }
    for dz in (-1, 1):
        for dy in (-1, 1):
            has[dz, dy] = has[dz, 0] & has[0, dy]

    def peer(dz, dy):
        return (lax.rem(gz + dz % nz, nz), lax.rem(gy + dy % ny, ny))

    directions = [(1, 0), (-1, 0), (0, 1), (0, -1), (1, 1), (1, -1), (-1, 1), (-1, -1)]

    own_f = fpad.at[H : H + lz, Y0 : Y0 + ly, :]
    loads = [
        pltpu.make_async_copy(disp, dpad.at[:, 0:lz, 0:ly, :], load_sem.at[0]),
        pltpu.make_async_copy(design, own_f, load_sem.at[1]),
        pltpu.make_async_copy(void, void_v, load_sem.at[2]),
        pltpu.make_async_copy(solid, solid_v, load_sem.at[3]),
    ]
    for copy in loads:
        copy.start()

    barrier = pltpu.get_barrier_semaphore()
    ways = directions + NEAR_Z + NEAR_Y
    for way in ways:
        pl.semaphore_signal(barrier, inc=1, device_id=peer(*way), device_id_type=MESH)

    tells = ((2, 0), (-2, 0), (0, 2), (0, -2))

    for pad in (fpad, qpad):
        @pl.when(gz == 0)
        def _():
            pad[0:H] = jnp.zeros_like(pad[0:H])

        @pl.when(gz == nz - 1)
        def _():
            pad[lz + H :] = jnp.zeros_like(pad[lz + H :])

        @pl.when(gy == 0)
        def _():
            pad[:, 0:Y0] = jnp.zeros_like(pad[:, 0:Y0])

        @pl.when(gy == ny - 1)
        def _():
            pad[:, Y0 + ly :] = jnp.zeros_like(pad[:, Y0 + ly :])

    @pl.when(gz == nz - 1)
    def _():
        dpad[:, lz] = jnp.zeros_like(dpad[:, lz])

    @pl.when(gy == ny - 1)
    def _():
        dpad[:, :, ly:] = jnp.zeros_like(dpad[:, :, ly:])

    pl.semaphore_wait(barrier, len(ways))
    for way in tells:
        pl.semaphore_signal(known, inc=1, device_id=peer(*way), device_id_type=MESH)

    near_z = {1: slice(lz - H, lz), -1: slice(0, H), 0: slice(0, lz)}
    near_y = {1: slice(ly - H, ly), -1: slice(0, H), 0: slice(0, ly)}
    far_z = {1: slice(0, H), -1: slice(H + lz, lz + 2 * H), 0: slice(H, H + lz)}
    far_y = {1: slice(Y0 - H, Y0), -1: slice(Y0 + ly, Y0 + ly + H), 0: slice(Y0, Y0 + ly)}

    def halo(src, src_at, pad, send, recv, n):
        dz, dy = directions[n]
        return pltpu.make_async_remote_copy(
            src_ref=src.at[src_at[0][dz], src_at[1][dy], :],
            dst_ref=pad.at[far_z[dz], far_y[dy], :],
            send_sem=send.at[n], recv_sem=recv.at[n],
            device_id=peer(dz, dy), device_id_type=MESH,
        )

    def start(direction, copy):
        @pl.when(has[direction])
        def _():
            copy.start()

    def wait_recv(direction, copy):
        @pl.when(has[-direction[0], -direction[1]])
        def _():
            copy.wait_recv()

    def wait_send(direction, copy):
        @pl.when(has[direction])
        def _():
            copy.wait_send()

    def nodes(n, direction, layers, rows, to_layers, to_rows):
        return direction, pltpu.make_async_remote_copy(
            src_ref=disp.at[:, layers, rows, :],
            dst_ref=dpad.at[:, to_layers, to_rows, :],
            send_sem=send1.at[8 + n], recv_sem=recv1.at[8 + n],
            device_id=peer(*direction), device_id_type=MESH,
        )

    first_z, top_z = slice(0, 1), slice(lz, lz + 1)
    first_y, top_y = slice(0, 1), slice(ly, ly + 1)
    own_z, own_y = slice(0, lz), slice(0, ly)
    node_copies = [
        nodes(0, (0, -1), own_z, first_y, own_z, top_y),
        nodes(1, (-1, -1), first_z, first_y, top_z, top_y),
        nodes(2, (-1, 0), first_z, own_y, top_z, own_y),
    ]
    design_copies = [
        (directions[n], halo(design, (near_z, near_y), fpad, send1, recv1, n)) for n in range(8)
    ]
    start(*design_copies[0])
    start(*design_copies[1])
    start(*node_copies[0])
    start(*node_copies[1])
    for n in range(2, 8):
        start(*design_copies[n])

    across = jnp.abs(iota((lx, lx), 0) - iota((lx, lx), 1))
    tx[...] = jnp.maximum(4 - across, 0).astype(F32).astype(BF16)
    full_z, full_y = lz * nz, ly * ny
    row_at = iota((ly, lx), 0) + gy * ly
    col_at = iota((ly, lx), 1)
    inv_yx = 1.0 / (line_total(row_at, full_y) * line_total(col_at, lx))
    cube_yx[...] = (-PENALTY) * inv_yx * inv_yx * inv_yx
    layer_at = iota((lz, lx), 0) + gz * lz
    inv_z = 1.0 / line_total(layer_at, full_z)
    cube_z[...] = inv_z * inv_z * inv_z
    weights(weight_yx, weight_z, gy, ny, gz, nz)

    size = 24 * 8
    pick = (lax.shift_right_logical(iota((size, 24), 0), 3) == iota((size, 24), 1)).astype(F32).astype(BF16)
    pick_t = (iota((24, size), 0) == lax.shift_right_logical(iota((24, size), 1), 3)).astype(F32).astype(BF16)
    same = (iota((size, size), 0) & 7) == (iota((size, size), 1) & 7)
    for part, ref in zip(split_bf16(stiff[...]), (k_high, k_low)):
        spread_k = dot(dot(pick, part).astype(BF16), pick_t)
        ref[...] = jnp.where(same, spread_k, 0.0).astype(BF16)

    last_col = iota((8, lx), 1) == lx - 1

    def element_rows(k, tile):
        at = tile * 8
        u = []
        for a in range(2):
            for b in range(2):
                here = [dpad[q, k + a, pl.ds(at + b, 8), :] for q in range(3)]
                u += here
                u += [jnp.where(last_col, 0.0, pltpu.roll(v, lx - 1, 1)) for v in here]
        u = jnp.concatenate(u, axis=0)
        high = u.astype(BF16)
        forces = dot(k_high[...], high) + dot(k_low[...], high)
        terms = (2.0 * u - high.astype(F32)) * forces
        total = jnp.sum(terms.reshape(24, 8, lx), axis=0)
        energy[k, pl.ds(at, 8), :] = jnp.maximum(total, 0.0)

    tiles = ly // 8

    def energy_of(count, layer_of, tiles_of):
        def body(n, carry):
            for k in layer_of(n):
                for tile in tiles_of:
                    element_rows(k, tile)
            return carry

        lax.fori_loop(0, count, body, 0)

    inner = lz - 2 * H
    sums_z, sums_y = lambda d: peer(d, 0), lambda d: peer(0, d)
    target = total_target(lz, ly, lx, nz, ny)
    lane = iota((1, 128), 1)

    def weight_of(k):
        return weight_yx[...] * weight_z[pl.ds(k, 1), :]

    s_z, s_y = lz // 2 - 1, ly // 2 - 4
    q_z, q_y = s_z - H, s_y - 4
    for load in loads:
        load.wait()
    energy_of(4, lambda n: [q_z + 2 * n, q_z + 2 * n + 1], [q_y // 8, q_y // 8 + 1])
    start(*node_copies[2])
    layer_filter(fpad, zs, 8, H + q_z - H, ly, Y0)
    f = jnp.concatenate([row_filter(zs, k, 16, q_y - Y0) for k in range(8)], axis=0)
    high, low = split_bf16(f)
    f = dot(high, tx[...]) + dot(low, tx[...])
    f = jnp.concatenate(
        [
            f[16 * k : 16 * k + 16] * f[16 * k : 16 * k + 16]
            * (energy[q_z + k, q_y : q_y + 16] * (cube_yx[q_y : q_y + 16] * cube_z[q_z + k : q_z + k + 1]))
            for k in range(8)
        ],
        axis=0,
    )
    high, low = split_bf16(f)
    f = dot(high, tx[...]) + dot(low, tx[...])
    for k in range(8):
        qs[k] = f[16 * k : 16 * k + 16]
    layer_filter(qs, zq, 2)
    sample = []
    for k in range(2):
        rows = slice(s_y, s_y + 8)
        d = fpad[H + s_z + k, Y0 + s_y : Y0 + s_y + 8]
        weight = weight_yx[rows] * weight_z[s_z + k : s_z + k + 1]
        a = d * jnp.sqrt(-row_filter(zq, k, 8, 4 - (Y0)) * weight)
        lo, hi = bounds(weight, d, solid_v[s_z + k, rows], void_v[s_z + k, rows])
        for c in range(0, lx, 128):
            sample.append((a[:, c : c + 128], lo[:, c : c + 128], hi[:, c : c + 128]))
    rough = (HIGH_LOG - LOW_LOG) / ROUGH
    totals = []
    for j in range(ROUGH):
        factor = E ** (-0.5 * (LOW_LOG + rough * j))
        parts = [jnp.minimum(jnp.maximum(a * factor, lo), hi) for a, lo, hi in sample]
        total = parts[0]
        for part in parts[1:]:
            total = total + part
        totals.append(total)
    row = to_lanes(totals, range(ROUGH))
    pl.semaphore_wait(known, len(tells))
    sum_start(0, row, gz, nz, sums_z, sums, send_r, recv_r)

    energy_of(2 * H - 1, lambda n: [n + (n // H) * inner], range(tiles - 1))
    rest = [k for k in range(H, lz - H) if not q_z <= k < q_z + 8]
    others = [t for t in range(1, tiles - 1) if not q_y // 8 <= t < q_y // 8 + 2]
    energy_of(1, lambda n: rest, range(1, tiles - 1))
    if others:
        energy_of(8, lambda n: [q_z + n], others)
    energy_of(inner // 2, lambda n: [H + 2 * n, H + 2 * n + 1], [0])
    wait_recv(*node_copies[0])
    wait_recv(*node_copies[1])
    energy_of((lz - 1) // 3, lambda n: [3 * n, 3 * n + 1, 3 * n + 2], [tiles - 1])

    for copy in design_copies:
        wait_recv(*copy)
    layer_filter(fpad, zbuf, lz)

    def source(layers, first, last):
        n = last - first
        f = jnp.concatenate([row_filter(zbuf, k, n, first) for k in layers], axis=0)
        high, low = split_bf16(f)
        f = dot(high, tx[...]) + dot(low, tx[...])
        cube = cube_yx[first:last]
        f = jnp.concatenate(
            [
                f[i * n : (i + 1) * n] * f[i * n : (i + 1) * n]
                * (energy[k, first:last] * (cube * cube_z[k : k + 1, :]))
                for i, k in enumerate(layers)
            ],
            axis=0,
        )
        high, low = split_bf16(f)
        f = dot(high, tx[...]) + dot(low, tx[...])
        for i, k in enumerate(layers):
            qpad[H + k, Y0 + first : Y0 + last, :] = f[i * n : (i + 1) * n]

    own_zq = {1: slice(lz, lz + H), -1: slice(H, 2 * H), 0: slice(H, H + lz)}
    own_yq = {1: slice(Y0 + ly - H, Y0 + ly), -1: slice(Y0, Y0 + H), 0: slice(Y0, Y0 + ly)}
    source_copies = [
        (directions[n], halo(qpad, (own_zq, own_yq), qpad, send2, recv2, n)) for n in range(8)
    ]
    source(range(H), 0, ly)
    start(*source_copies[1])
    start(*source_copies[6])
    start(*source_copies[7])
    wait_recv(*node_copies[2])
    for tile in range(tiles):
        element_rows(lz - 1, tile)
    source(range(lz - H, lz), 0, ly)
    start(*source_copies[0])
    start(*source_copies[4])
    start(*source_copies[5])
    middle = range(H, lz - H)
    source(middle, 0, 8)
    start(*source_copies[3])
    source(middle, ly - 8, ly)
    start(*source_copies[2])
    source(range(H, lz // 2), 8, ly - 8)
    source(range(lz // 2, lz - H), 8, ly - 8)

    def bounds_of(k, carry):
        low_v[k], high_v[k] = bounds(weight_of(k), fpad[H + k, Y0 : Y0 + ly, :], solid_v[k], void_v[k])
        return carry

    lax.fori_loop(0, lz, bounds_of, 0)

    row = sum_finish(0, nz, sums, recv_r)
    sum_start(1, row, gy, ny, sums_y, sums, send_r, recv_r)

    for copy in source_copies:
        wait_recv(*copy)
    layer_filter(qpad, zbuf, lz)
    for k in range(lz):
        s = row_filter(zbuf, k, ly)
        sens_v[k] = s
        amount[k] = fpad[H + k, Y0 : Y0 + ly, :] * jnp.sqrt(-s * weight_of(k))
    store_sens = pltpu.make_async_copy(sens_v, sens, store_sem.at[0])
    store_sens.start()

    row = sum_finish(1, ny, sums, recv_r)
    part = target * (16.0 / (lz * ly))
    index = count_above(row, lane < ROUGH, part)
    below, above = entry(row, index - 1.0), entry(row, index)
    step = jnp.where((index > 0.0) & (index < ROUGH), (below - part) / (below - above), 0.0)
    guess = (GRID // ROUGH) * (index - 1.0 + step)
    first = jnp.clip(jnp.floor(guess) - (WINDOW // 2 - 1), 0.0, GRID + 1.0 - WINDOW)
    low = LOW_LOG + FINE * first
    factors = [E ** (-0.5 * FINE * j) for j in range(WINDOW)]
    row = volumes(amount, low_v, high_v, jnp.exp(-0.5 * low), factors, range(WINDOW))
    sum_start(2, row, gz, nz, sums_z, sums, send_r, recv_r)
    row = sum_finish(2, nz, sums, recv_r)
    sum_start(3, row, gy, ny, sums_y, sums, send_r, recv_r)
    row = sum_finish(3, ny, sums, recv_r)
    index = count_above(row, lane < WINDOW, target)
    hit = (index > 0.0) & (index < WINDOW)
    found[...] = jnp.broadcast_to(jnp.where(hit, 1.0, 0.0), found.shape)
    index = index - 1.0
    final = secant(low + FINE * index, entry(row, index), entry(row, index + 1.0), target)
    factor = jnp.exp(-0.5 * final)

    def finish(k, carry):
        d = fpad[H + k, Y0 : Y0 + ly, :]
        new_v[k] = finished(amount[k], weight_of(k), factor, d, solid_v[k], void_v[k])
        return carry

    lax.fori_loop(0, lz, finish, 0)
    store_new = pltpu.make_async_copy(new_v, new_design, store_sem.at[1])
    store_new.start()

    for copy in node_copies + design_copies + source_copies:
        wait_send(*copy)
    for n, size in enumerate((nz, ny, nz, ny)):
        sum_sent(n, size, sums, send_r)
    store_sens.wait()
    store_new.wait()


def exact_kernel(
    nz, ny,
    design, void, solid, sens,
    new_design,
    design_v, void_v, solid_v, amount, low_v, high_v, new_v, weight_yx, weight_z, sums,
    load_sem, store_sem, send_r, recv_r,
):
    lz, ly, lx = design.shape
    gz, gy = lax.axis_index("gz"), lax.axis_index("gy")

    def sums_z(d):
        return (lax.rem(gz + d, nz), gy)

    def sums_y(d):
        return (gz, lax.rem(gy + d, ny))

    loads = [
        pltpu.make_async_copy(src, dst, load_sem.at[n])
        for n, (src, dst) in enumerate(
            ((design, design_v), (void, void_v), (solid, solid_v), (sens, amount))
        )
    ]
    for load in loads:
        load.start()
    barrier = pltpu.get_barrier_semaphore()
    partners = [sums_z(d) for d in range(1, nz)] + [sums_y(d) for d in range(1, ny)]
    for partner in partners:
        pl.semaphore_signal(barrier, inc=1, device_id=partner, device_id_type=MESH)
    weights(weight_yx, weight_z, gy, ny, gz, nz)
    for load in loads:
        load.wait()

    def weight_of(k):
        return weight_yx[...] * weight_z[pl.ds(k, 1), :]

    def prepare(k, carry):
        d = design_v[k]
        low_v[k], high_v[k] = bounds(weight_of(k), d, solid_v[k], void_v[k])
        amount[k] = d * jnp.sqrt(-amount[k] * weight_of(k))
        return carry

    lax.fori_loop(0, lz, prepare, 0)
    pl.semaphore_wait(barrier, len(partners))

    def everywhere(n, row):
        sum_start(n, row, gz, nz, sums_z, sums, send_r, recv_r)
        row = sum_finish(n, nz, sums, recv_r)
        sum_start(n + 1, row, gy, ny, sums_y, sums, send_r, recv_r)
        return sum_finish(n + 1, ny, sums, recv_r)

    target = total_target(lz, ly, lx, nz, ny)
    lane = iota((1, 128), 1)
    inside = (lane >= 1) & (lane < SPLIT)
    wide = FINE * SPLIT
    factors = [E ** (-0.5 * (LOW_LOG + wide * j)) for j in range(SPLIT + 1)]
    row = everywhere(0, volumes(amount, low_v, high_v, None, factors, range(SPLIT + 1)))
    index = count_above(row, inside, target)
    low = LOW_LOG + wide * index
    ends = (entry(row, index), entry(row, index + 1.0))
    factors = [E ** (-0.5 * FINE * j) for j in range(1, SPLIT)]
    row = everywhere(
        2, volumes(amount, low_v, high_v, jnp.exp(-0.5 * low), factors, range(1, SPLIT))
    )
    row = jnp.where(lane == 0, ends[0], jnp.where(lane == SPLIT, ends[1], row))
    index = count_above(row, inside, target)
    final = secant(low + FINE * index, entry(row, index), entry(row, index + 1.0), target)
    factor = jnp.exp(-0.5 * final)

    def finish(k, carry):
        new_v[k] = finished(amount[k], weight_of(k), factor, design_v[k], solid_v[k], void_v[k])
        return carry

    lax.fori_loop(0, lz, finish, 0)
    store = pltpu.make_async_copy(new_v, new_design, store_sem)
    store.start()
    for n, size in enumerate((nz, ny, nz, ny)):
        sum_sent(n, size, sums, send_r)
    store.wait()


def per_device(displacement, design, void_mask, solid_mask, stiffness):
    nz, ny = lax.axis_size("gz"), lax.axis_size("gy")
    lz, ly, lx = design.shape
    brick = jax.ShapeDtypeStruct(design.shape, F32)
    padded = (lz + 2 * H, ly + 16, lx)
    anywhere = pl.BlockSpec(memory_space=pltpu.HBM)
    sem = pltpu.SemaphoreType
    line, table = pltpu.VMEM((lz, lx), F32), pltpu.VMEM((ly, lx), F32)
    bricks = [pltpu.VMEM(design.shape, F32)] * 4
    masks = [pltpu.VMEM(design.shape, jnp.int32)] * 2
    sums = pltpu.VMEM((4, max(nz, ny), 1, 128), F32)
    new_design, sens, found = pl.pallas_call(
        functools.partial(kernel, nz, ny),
        out_shape=(brick, brick, jax.ShapeDtypeStruct((8, 128), F32)),
        in_specs=[anywhere] * 4 + [pl.BlockSpec(memory_space=pltpu.VMEM)],
        out_specs=(anywhere, anywhere, pl.BlockSpec(memory_space=pltpu.VMEM)),
        scratch_shapes=[
            pltpu.VMEM((3, lz + 1, ly + 8, lx), F32),
            pltpu.VMEM(padded, F32),
            pltpu.VMEM(padded, F32),
            pltpu.VMEM((lz, ly + 16, lx), F32),
            *masks,
            *bricks,
            pltpu.VMEM(design.shape, F32),
            pltpu.VMEM(design.shape, F32),
            pltpu.VMEM((lx, lx), BF16),
            pltpu.VMEM((192, 192), BF16),
            pltpu.VMEM((192, 192), BF16),
            table, table, line, line,
            pltpu.VMEM((8, ly, lx), F32),
            pltpu.VMEM((8, 16, lx), F32),
            pltpu.VMEM((2, 16, lx), F32),
            sums,
            sem.DMA((4,)), sem.DMA((2,)),
            sem.DMA((11,)), sem.DMA((11,)), sem.DMA((8,)), sem.DMA((8,)),
            sem.DMA((4,)), sem.DMA((4,)), sem.REGULAR,
        ],
        compiler_params=pltpu.CompilerParams(
            collective_id=0, has_side_effects=True, vmem_limit_bytes=60 * 1024 * 1024
        ),
    )(displacement, design, void_mask, solid_mask, stiffness)

    def exact(new_design, design, void_mask, solid_mask, sens):
        return pl.pallas_call(
            functools.partial(exact_kernel, nz, ny),
            out_shape=brick,
            in_specs=[anywhere] * 4,
            out_specs=anywhere,
            scratch_shapes=[
                pltpu.VMEM(design.shape, F32), *masks,
                *bricks,
                table, line, sums,
                sem.DMA((4,)), sem.DMA, sem.DMA((4,)), sem.DMA((4,)),
            ],
            compiler_params=pltpu.CompilerParams(
                collective_id=1, has_side_effects=True, vmem_limit_bytes=60 * 1024 * 1024
            ),
        )(design, void_mask, solid_mask, sens)

    new_design = lax.cond(
        found[0, 0] > 0.5, lambda new_design, *rest: new_design, exact,
        new_design, design, void_mask, solid_mask, sens,
    )
    return new_design, sens


def solution(mesh):
    return jax.shard_map(
        per_device,
        mesh=mesh,
        in_specs=(
            P(None, "gz", "gy", None),
            P("gz", "gy", None),
            P("gz", "gy", None),
            P("gz", "gy", None),
            P(),
        ),
        out_specs=(P("gz", "gy", None), P("gz", "gy", None)),
        check_vma=False,
    )
```

```python
import functools

import jax
import jax.numpy as jnp
from jax import lax
from jax.experimental import pallas as pl
from jax.experimental.pallas import tpu as pltpu
from jax.sharding import PartitionSpec as P

MESH = pl.DeviceIdType.MESH
NEAR_Z = [(d, 0) for d in (2, -2, 3, -3, 4, -4, 5, -5, 6, -6)]
NEAR_Y = [(0, d) for d in (2, -2, 8, 7, 9, 6, 10)]
F32 = jnp.float32
BF16 = jnp.bfloat16

TAPS = (1.0, 2.0, 3.0, 4.0, 3.0, 2.0, 1.0)
LOW_LOG = -25.0
HIGH_LOG = 25.0
MOVE_LIMIT = 0.2
VOLUME_FRACTION = 0.5
PENALTY = 3.0
SPLIT = 16
GRID = SPLIT * SPLIT
FINE = (HIGH_LOG - LOW_LOG) / GRID
ROUGH = 64
WINDOW = 14
E = 2.718281828459045

H = 3
Y0 = 8


def line_total(p, extent):
    low = jnp.maximum(3 - p, 0)
    high = jnp.maximum(p - (extent - 4), 0)
    missing = low * (low + 1) + high * (high + 1)
    return 16.0 - 0.5 * missing.astype(F32)


def line_spread(p, extent):
    total = None
    for d in range(-3, 4):
        near = p + d
        term = jnp.where(
            (near >= 0) & (near < extent), TAPS[d + 3] / line_total(near, extent), 0.0
        )
        total = term if total is None else total + term
    return total


def iota(shape, dim):
    return lax.broadcasted_iota(jnp.int32, shape, dim)


def split_bf16(x):
    high = x.astype(BF16)
    low = (x - high.astype(F32)).astype(BF16)
    return high, low


def dot(a, b):
    return jnp.dot(a, b, preferred_element_type=F32)


def row_filter(ref, layer, rows, first=0):
    at = Y0 - H + first
    c = [ref[layer, at + t : at + t + rows, :] for t in range(7)]
    return (c[0] + c[6]) + 2.0 * (c[1] + c[5]) + 3.0 * (c[2] + c[4]) + 4.0 * c[3]


def layer_filter(src, dst, layers, first=0, rows=None, first_row=0):
    rows = src.shape[1] if rows is None else rows
    for r in range(0, rows, 8):
        for c in range(0, src.shape[2], 128):
            col = slice(c, c + 128)
            f = [src[first + k, first_row + r : first_row + r + 8, col] for k in range(layers + 2 * H)]
            f = [a + b for a, b in zip(f, f[1:])]
            f = [a + b for a, b in zip(f, f[2:])]
            f = [a + b for a, b in zip(f, f[1:])]
            f = [a + b for a, b in zip(f, f[2:])]
            for k in range(layers):
                dst[k, r : r + 8, col] = f[k]


def sum_start(n, row, at, size, to, sums, send, recv):
    sums[n, at] = row
    copies = [
        pltpu.make_async_remote_copy(
            src_ref=sums.at[n, at], dst_ref=sums.at[n, at],
            send_sem=send.at[n], recv_sem=recv.at[n],
            device_id=to(d), device_id_type=MESH,
        )
        for d in range(1, size)
    ]
    for copy in copies:
        copy.start()


def sum_finish(n, size, sums, recv):
    everyone = sums.at[n, 0 : size - 1]
    pltpu.make_async_copy(everyone, everyone, recv.at[n]).wait()
    return jnp.sum(sums[n, 0:size], axis=0)


def sum_sent(n, size, sums, send):
    everyone = sums.at[n, 0 : size - 1]
    pltpu.make_async_copy(everyone, everyone, send.at[n]).wait()


def to_lanes(rows, lanes):
    count = -(-(max(lanes) + 1) // 8) * 8
    sub = iota((count, 128), 0)
    stacked = jnp.zeros((count, 128), F32)
    for row, j in zip(rows, lanes):
        stacked = jnp.where(sub == j, jnp.sum(row, axis=0, keepdims=True), stacked)
    line = jnp.sum(stacked, axis=1, keepdims=True)
    return jnp.sum(jnp.where(sub == iota((count, 128), 1), line, 0.0), axis=0, keepdims=True)


def volumes(amount, low_v, high_v, scale, factors, lanes):
    lz, ly, lx = amount.shape

    def layer(k, totals):
        totals = list(totals)
        for r in range(0, ly, 8):
            for c in range(0, lx, 128):
                at = (k, slice(r, r + 8), slice(c, c + 128))
                a, low, high = amount[at], low_v[at], high_v[at]
                if scale is not None:
                    a = a * scale
                for j, factor in enumerate(factors):
                    totals[j] = totals[j] + jnp.minimum(jnp.maximum(a * factor, low), high)
        return tuple(totals)

    totals = lax.fori_loop(0, lz, layer, tuple(jnp.zeros((8, 128), F32) for _ in factors))
    return to_lanes(totals, lanes)


def count_above(row, inside, target):
    return jnp.sum(jnp.where(inside & (row > target), 1.0, 0.0), axis=1, keepdims=True)


def entry(row, index):
    at = iota(row.shape, 1).astype(F32)
    return jnp.sum(jnp.where(at == index, row, 0.0), axis=1, keepdims=True)


def secant(low, low_volume, high_volume, target):
    return low + FINE * ((low_volume - target) / (low_volume - high_volume))


def weights(ref, z_ref, gy, ny, gz, nz):
    ly, lx = ref.shape
    lz = z_ref.shape[0]
    ref[...] = line_spread(iota((ly, lx), 0) + gy * ly, ly * ny) * line_spread(iota((ly, lx), 1), lx)
    z_ref[...] = line_spread(iota((lz, lx), 0) + gz * lz, lz * nz)


def bounds(weight, d, solid, void):
    low = jnp.maximum(d - MOVE_LIMIT, 0.0) * weight
    high = jnp.minimum(d + MOVE_LIMIT, 1.0) * weight
    is_solid, is_void = solid == 1, void == 1
    low = jnp.where(is_solid, weight, jnp.where(is_void, 0.0, low))
    high = jnp.where(is_solid, weight, jnp.where(is_void, 0.0, high))
    return low, high


def finished(a, weight, factor, d, solid, void):
    moved = (a / weight) * factor
    moved = jnp.minimum(
        jnp.maximum(moved, jnp.maximum(d - MOVE_LIMIT, 0.0)), jnp.minimum(d + MOVE_LIMIT, 1.0)
    )
    return jnp.where(solid == 1, 1.0, jnp.where(void == 1, 0.0, moved))


def total_target(lz, ly, lx, nz, ny):
    return VOLUME_FRACTION * (lz * nz) * (ly * ny) * lx


def kernel(
    nz, ny,
    disp, design, void, solid, stiff,
    new_design, sens, found,
    dpad, fpad, qpad, zbuf, void_v, solid_v, energy, amount, low_v, high_v, sens_v, new_v,
    shifted, double, double_s, edge, tx, k_rows, cube_yx, weight_yx, cube_z, weight_z, zs, qs, zq, sums,
    load_sem, store_sem, send1, recv1, send2, recv2, send_r, recv_r, known,
):
    lz, ly, lx = design.shape
    gz, gy = lax.axis_index("gz"), lax.axis_index("gy")
    has = {
        (1, 0): gz < nz - 1, (-1, 0): gz > 0, (0, 1): gy < ny - 1, (0, -1): gy > 0,
    }
    for dz in (-1, 1):
        for dy in (-1, 1):
            has[dz, dy] = has[dz, 0] & has[0, dy]

    def peer(dz, dy):
        return (lax.rem(gz + dz % nz, nz), lax.rem(gy + dy % ny, ny))

    directions = [(1, 0), (-1, 0), (0, 1), (0, -1), (1, 1), (1, -1), (-1, 1), (-1, -1)]

    own_f = fpad.at[H : H + lz, Y0 : Y0 + ly, :]
    loads = [
        pltpu.make_async_copy(disp, dpad.at[:, 0:lz, 0:ly, :], load_sem.at[0]),
        pltpu.make_async_copy(design, own_f, load_sem.at[1]),
        pltpu.make_async_copy(void, void_v, load_sem.at[2]),
        pltpu.make_async_copy(solid, solid_v, load_sem.at[3]),
    ]
    for copy in loads:
        copy.start()

    barrier = pltpu.get_barrier_semaphore()
    ways = directions + NEAR_Z + NEAR_Y
    for way in ways:
        pl.semaphore_signal(barrier, inc=1, device_id=peer(*way), device_id_type=MESH)

    tells = ((2, 0), (-2, 0), (0, 2), (0, -2))

    for pad in (fpad, qpad):
        @pl.when(gz == 0)
        def _():
            pad[0:H] = jnp.zeros_like(pad[0:H])

        @pl.when(gz == nz - 1)
        def _():
            pad[lz + H :] = jnp.zeros_like(pad[lz + H :])

        @pl.when(gy == 0)
        def _():
            pad[:, 0:Y0] = jnp.zeros_like(pad[:, 0:Y0])

        @pl.when(gy == ny - 1)
        def _():
            pad[:, Y0 + ly :] = jnp.zeros_like(pad[:, Y0 + ly :])

    @pl.when(gz == nz - 1)
    def _():
        dpad[:, lz] = jnp.zeros_like(dpad[:, lz])

    @pl.when(gy == ny - 1)
    def _():
        dpad[:, :, ly:] = jnp.zeros_like(dpad[:, :, ly:])

    pl.semaphore_wait(barrier, len(ways))
    for way in tells:
        pl.semaphore_signal(known, inc=1, device_id=peer(*way), device_id_type=MESH)

    near_z = {1: slice(lz - H, lz), -1: slice(0, H), 0: slice(0, lz)}
    near_y = {1: slice(ly - H, ly), -1: slice(0, H), 0: slice(0, ly)}
    far_z = {1: slice(0, H), -1: slice(H + lz, lz + 2 * H), 0: slice(H, H + lz)}
    far_y = {1: slice(Y0 - H, Y0), -1: slice(Y0 + ly, Y0 + ly + H), 0: slice(Y0, Y0 + ly)}

    def halo(src, src_at, pad, send, recv, n):
        dz, dy = directions[n]
        return pltpu.make_async_remote_copy(
            src_ref=src.at[src_at[0][dz], src_at[1][dy], :],
            dst_ref=pad.at[far_z[dz], far_y[dy], :],
            send_sem=send.at[n], recv_sem=recv.at[n],
            device_id=peer(dz, dy), device_id_type=MESH,
        )

    def start(direction, copy):
        @pl.when(has[direction])
        def _():
            copy.start()

    def wait_recv(direction, copy):
        @pl.when(has[-direction[0], -direction[1]])
        def _():
            copy.wait_recv()

    def wait_send(direction, copy):
        @pl.when(has[direction])
        def _():
            copy.wait_send()

    def nodes(n, direction, layers, rows, to_layers, to_rows):
        return direction, pltpu.make_async_remote_copy(
            src_ref=disp.at[:, layers, rows, :],
            dst_ref=dpad.at[:, to_layers, to_rows, :],
            send_sem=send1.at[8 + n], recv_sem=recv1.at[8 + n],
            device_id=peer(*direction), device_id_type=MESH,
        )

    first_z, top_z = slice(0, 1), slice(lz, lz + 1)
    first_y, top_y = slice(0, 1), slice(ly, ly + 1)
    own_z, own_y = slice(0, lz), slice(0, ly)
    node_copies = [
        nodes(0, (0, -1), own_z, first_y, own_z, top_y),
        nodes(1, (-1, -1), first_z, first_y, top_z, top_y),
        nodes(2, (-1, 0), first_z, own_y, top_z, own_y),
    ]
    design_copies = [
        (directions[n], halo(design, (near_z, near_y), fpad, send1, recv1, n)) for n in range(8)
    ]
    start(*design_copies[0])
    start(*design_copies[1])
    start(*node_copies[0])
    start(*node_copies[1])
    for n in range(2, 8):
        start(*design_copies[n])

    across = jnp.abs(iota((lx, lx), 0) - iota((lx, lx), 1))
    tx[...] = jnp.maximum(4 - across, 0).astype(F32).astype(BF16)
    full_z, full_y = lz * nz, ly * ny
    row_at = iota((ly, lx), 0) + gy * ly
    col_at = iota((ly, lx), 1)
    inv_yx = 1.0 / (line_total(row_at, full_y) * line_total(col_at, lx))
    cube_yx[...] = (-PENALTY) * inv_yx * inv_yx * inv_yx
    layer_at = iota((lz, lx), 0) + gz * lz
    inv_z = 1.0 / line_total(layer_at, full_z)
    cube_z[...] = inv_z * inv_z * inv_z
    weights(weight_yx, weight_z, gy, ny, gz, nz)

    size, width = 24 * 8, 12 * 8 + 16
    pick = (lax.shift_right_logical(iota((size, 24), 0), 3) == iota((size, 24), 1)).astype(F32).astype(BF16)
    entry_at, col = iota((24, 2 * width), 0), iota((24, 2 * width), 1)

    def part_col(col):
        return jnp.where(col >= width, col - width, col)

    col = part_col(col)
    corner = sum((entry_at >= 6 * n).astype(jnp.int32) for n in (1, 2, 3))
    step_y = corner & 1
    rest = entry_at - 6 * corner
    group = jnp.where(corner >= 2, 6, 0) + rest
    tail = col - 12 * 8
    tail_rest = tail & 7
    tail_group = jnp.where(tail_rest < 6, jnp.where(tail >= 8, 6, 0) + tail_rest, -1)
    col_group = jnp.where(col < 12 * 8, lax.shift_right_logical(col, 3), tail_group)
    places = [
        ((group == col_group) & (step_y == n)).astype(F32).astype(BF16) for n in range(2)
    ]
    col = part_col(iota((size, 2 * width), 1))
    up = jnp.where(col < 12 * 8, col & 7, 8) - (iota((size, 2 * width), 0) & 7)
    halves = []
    for part in split_bf16(stiff[...]):
        rows = dot(pick, part).astype(BF16)
        same, next_row = dot(rows, places[0]), dot(rows, places[1])
        halves.append(jnp.where(up == 0, same, jnp.where(up == 1, next_row, 0.0)))
    is_low = iota((size, 2 * width), 1) >= width
    k_rows[...] = jnp.where(is_low, halves[1], halves[0]).astype(BF16)

    def nodes_at(k, first, last):
        at = slice(first, last)
        last_col = iota((last - first, lx), 1) == lx - 1
        for q in range(3):
            u = dpad[q, k, at]
            v = jnp.where(last_col, 0.0, pltpu.roll(u, lx - 1, 1))
            shifted[q, k, at] = v
            double[q, k, at] = 2.0 * u - u.astype(BF16).astype(F32)
            double_s[q, k, at] = 2.0 * v - v.astype(BF16).astype(F32)

    def ninth_rows(k, tiles_of):
        for tile in tiles_of:
            at = slice(8 * tile + 8, 8 * tile + 9)
            rows = [ref[q, k, at, :] for ref in (dpad, shifted) for q in range(3)]
            edge[k, tile] = jnp.concatenate(rows + [jnp.zeros((2, lx), F32)], axis=0)

    def element_rows(k, tile):
        at = slice(8 * tile, 8 * tile + 8)
        u = [ref[q, k + a, at, :] for a in range(2) for ref in (dpad, shifted) for q in range(3)]
        u += [edge[k + a, tile] for a in range(2)]
        high = jnp.concatenate(u, axis=0).astype(BF16)
        forces = dot(k_rows[...], jnp.concatenate([high, high], axis=0))
        total = None
        for n in range(24):
            a, b, c, q = n // 12, n // 6 % 2, n // 3 % 2, n % 3
            ref = double_s if c else double
            term = ref[q, k + a, 8 * tile + b : 8 * tile + b + 8, :] * forces[8 * n : 8 * n + 8]
            total = term if total is None else total + term
        energy[k, at, :] = jnp.maximum(total, 0.0)

    tiles = ly // 8

    def energy_of(count, layer_of, tiles_of):
        def body(n, carry):
            for k in layer_of(n):
                for tile in tiles_of:
                    element_rows(k, tile)
            return carry

        lax.fori_loop(0, count, body, 0)

    inner = lz - 2 * H
    sums_z, sums_y = lambda d: peer(d, 0), lambda d: peer(0, d)
    target = total_target(lz, ly, lx, nz, ny)
    lane = iota((1, 128), 1)

    def weight_of(k):
        return weight_yx[...] * weight_z[pl.ds(k, 1), :]

    s_z, s_y = lz // 2 - 1, ly // 2 - 4
    q_z, q_y = s_z - H, s_y - 4
    for load in loads:
        load.wait()

    def own_nodes(k, carry):
        nodes_at(k, 0, ly)
        ninth_rows(k, range(tiles - 1))
        return carry

    lax.fori_loop(0, lz, own_nodes, 0)
    energy_of(4, lambda n: [q_z + 2 * n, q_z + 2 * n + 1], [q_y // 8, q_y // 8 + 1])
    start(*node_copies[2])
    layer_filter(fpad, zs, 8, H + q_z - H, ly, Y0)
    f = jnp.concatenate([row_filter(zs, k, 16, q_y - Y0) for k in range(8)], axis=0)
    high, low = split_bf16(f)
    f = dot(high, tx[...]) + dot(low, tx[...])
    f = jnp.concatenate(
        [
            f[16 * k : 16 * k + 16] * f[16 * k : 16 * k + 16]
            * (energy[q_z + k, q_y : q_y + 16] * (cube_yx[q_y : q_y + 16] * cube_z[q_z + k : q_z + k + 1]))
            for k in range(8)
        ],
        axis=0,
    )
    high, low = split_bf16(f)
    f = dot(high, tx[...]) + dot(low, tx[...])
    for k in range(8):
        qs[k] = f[16 * k : 16 * k + 16]
    layer_filter(qs, zq, 2)
    sample = []
    for k in range(2):
        rows = slice(s_y, s_y + 8)
        d = fpad[H + s_z + k, Y0 + s_y : Y0 + s_y + 8]
        weight = weight_yx[rows] * weight_z[s_z + k : s_z + k + 1]
        a = d * jnp.sqrt(-row_filter(zq, k, 8, 4 - (Y0)) * weight)
        lo, hi = bounds(weight, d, solid_v[s_z + k, rows], void_v[s_z + k, rows])
        for c in range(0, lx, 128):
            sample.append((a[:, c : c + 128], lo[:, c : c + 128], hi[:, c : c + 128]))
    rough = (HIGH_LOG - LOW_LOG) / ROUGH
    totals = []
    for j in range(ROUGH):
        factor = E ** (-0.5 * (LOW_LOG + rough * j))
        parts = [jnp.minimum(jnp.maximum(a * factor, lo), hi) for a, lo, hi in sample]
        total = parts[0]
        for part in parts[1:]:
            total = total + part
        totals.append(total)
    row = to_lanes(totals, range(ROUGH))
    pl.semaphore_wait(known, len(tells))
    sum_start(0, row, gz, nz, sums_z, sums, send_r, recv_r)

    energy_of(2 * H - 1, lambda n: [n + (n // H) * inner], range(tiles - 1))
    rest = [k for k in range(H, lz - H) if not q_z <= k < q_z + 8]
    others = [t for t in range(1, tiles - 1) if not q_y // 8 <= t < q_y // 8 + 2]
    energy_of(1, lambda n: rest, range(1, tiles - 1))
    if others:
        energy_of(8, lambda n: [q_z + n], others)
    energy_of(inner // 2, lambda n: [H + 2 * n, H + 2 * n + 1], [0])
    wait_recv(*node_copies[0])
    wait_recv(*node_copies[1])

    def side_nodes(k, carry):
        nodes_at(k, ly, ly + 8)
        ninth_rows(k, [tiles - 1])
        return carry

    lax.fori_loop(0, lz, side_nodes, 0)
    energy_of((lz - 1) // 3, lambda n: [3 * n, 3 * n + 1, 3 * n + 2], [tiles - 1])

    for copy in design_copies:
        wait_recv(*copy)
    layer_filter(fpad, zbuf, lz)

    def source(layers, first, last):
        n = last - first
        f = jnp.concatenate([row_filter(zbuf, k, n, first) for k in layers], axis=0)
        high, low = split_bf16(f)
        f = dot(high, tx[...]) + dot(low, tx[...])
        cube = cube_yx[first:last]
        f = jnp.concatenate(
            [
                f[i * n : (i + 1) * n] * f[i * n : (i + 1) * n]
                * (energy[k, first:last] * (cube * cube_z[k : k + 1, :]))
                for i, k in enumerate(layers)
            ],
            axis=0,
        )
        high, low = split_bf16(f)
        f = dot(high, tx[...]) + dot(low, tx[...])
        for i, k in enumerate(layers):
            qpad[H + k, Y0 + first : Y0 + last, :] = f[i * n : (i + 1) * n]

    own_zq = {1: slice(lz, lz + H), -1: slice(H, 2 * H), 0: slice(H, H + lz)}
    own_yq = {1: slice(Y0 + ly - H, Y0 + ly), -1: slice(Y0, Y0 + H), 0: slice(Y0, Y0 + ly)}
    source_copies = [
        (directions[n], halo(qpad, (own_zq, own_yq), qpad, send2, recv2, n)) for n in range(8)
    ]
    source(range(H), 0, ly)
    start(*source_copies[1])
    start(*source_copies[6])
    start(*source_copies[7])
    wait_recv(*node_copies[2])
    nodes_at(lz, 0, ly + 8)
    ninth_rows(lz, range(tiles))
    for tile in range(tiles):
        element_rows(lz - 1, tile)
    source(range(lz - H, lz), 0, ly)
    start(*source_copies[0])
    start(*source_copies[4])
    start(*source_copies[5])
    middle = range(H, lz - H)
    source(middle, 0, 8)
    start(*source_copies[3])
    source(middle, ly - 8, ly)
    start(*source_copies[2])
    source(range(H, lz // 2), 8, ly - 8)
    source(range(lz // 2, lz - H), 8, ly - 8)

    def bounds_of(k, carry):
        low_v[k], high_v[k] = bounds(weight_of(k), fpad[H + k, Y0 : Y0 + ly, :], solid_v[k], void_v[k])
        return carry

    lax.fori_loop(0, lz, bounds_of, 0)

    row = sum_finish(0, nz, sums, recv_r)
    sum_start(1, row, gy, ny, sums_y, sums, send_r, recv_r)

    for copy in source_copies:
        wait_recv(*copy)
    layer_filter(qpad, zbuf, lz)
    for k in range(lz):
        s = row_filter(zbuf, k, ly)
        sens_v[k] = s
        amount[k] = fpad[H + k, Y0 : Y0 + ly, :] * jnp.sqrt(-s * weight_of(k))
    store_sens = pltpu.make_async_copy(sens_v, sens, store_sem.at[0])
    store_sens.start()

    row = sum_finish(1, ny, sums, recv_r)
    part = target * (16.0 / (lz * ly))
    index = count_above(row, lane < ROUGH, part)
    below, above = entry(row, index - 1.0), entry(row, index)
    step = jnp.where((index > 0.0) & (index < ROUGH), (below - part) / (below - above), 0.0)
    guess = (GRID // ROUGH) * (index - 1.0 + step)
    first = jnp.clip(jnp.floor(guess) - (WINDOW // 2 - 1), 0.0, GRID + 1.0 - WINDOW)
    low = LOW_LOG + FINE * first
    factors = [E ** (-0.5 * FINE * j) for j in range(WINDOW)]
    row = volumes(amount, low_v, high_v, jnp.exp(-0.5 * low), factors, range(WINDOW))
    sum_start(2, row, gz, nz, sums_z, sums, send_r, recv_r)
    row = sum_finish(2, nz, sums, recv_r)
    sum_start(3, row, gy, ny, sums_y, sums, send_r, recv_r)
    row = sum_finish(3, ny, sums, recv_r)
    index = count_above(row, lane < WINDOW, target)
    hit = (index > 0.0) & (index < WINDOW)
    found[0] = jnp.sum(jnp.where(hit, 1.0, 0.0)).astype(jnp.int32)
    index = index - 1.0
    final = secant(low + FINE * index, entry(row, index), entry(row, index + 1.0), target)
    factor = jnp.exp(-0.5 * final)

    def finish(k, carry):
        d = fpad[H + k, Y0 : Y0 + ly, :]
        new_v[k] = finished(amount[k], weight_of(k), factor, d, solid_v[k], void_v[k])
        return carry

    lax.fori_loop(0, lz, finish, 0)
    store_new = pltpu.make_async_copy(new_v, new_design, store_sem.at[1])
    store_new.start()

    for copy in node_copies + design_copies + source_copies:
        wait_send(*copy)
    for n, size in enumerate((nz, ny, nz, ny)):
        sum_sent(n, size, sums, send_r)
    store_sens.wait()
    store_new.wait()


def exact_kernel(
    nz, ny,
    design, void, solid, sens,
    new_design,
    design_v, void_v, solid_v, amount, low_v, high_v, new_v, weight_yx, weight_z, sums,
    load_sem, store_sem, send_r, recv_r,
):
    lz, ly, lx = design.shape
    gz, gy = lax.axis_index("gz"), lax.axis_index("gy")

    def sums_z(d):
        return (lax.rem(gz + d, nz), gy)

    def sums_y(d):
        return (gz, lax.rem(gy + d, ny))

    loads = [
        pltpu.make_async_copy(src, dst, load_sem.at[n])
        for n, (src, dst) in enumerate(
            ((design, design_v), (void, void_v), (solid, solid_v), (sens, amount))
        )
    ]
    for load in loads:
        load.start()
    barrier = pltpu.get_barrier_semaphore()
    partners = [sums_z(d) for d in range(1, nz)] + [sums_y(d) for d in range(1, ny)]
    for partner in partners:
        pl.semaphore_signal(barrier, inc=1, device_id=partner, device_id_type=MESH)
    weights(weight_yx, weight_z, gy, ny, gz, nz)
    for load in loads:
        load.wait()

    def weight_of(k):
        return weight_yx[...] * weight_z[pl.ds(k, 1), :]

    def prepare(k, carry):
        d = design_v[k]
        low_v[k], high_v[k] = bounds(weight_of(k), d, solid_v[k], void_v[k])
        amount[k] = d * jnp.sqrt(-amount[k] * weight_of(k))
        return carry

    lax.fori_loop(0, lz, prepare, 0)
    pl.semaphore_wait(barrier, len(partners))

    def everywhere(n, row):
        sum_start(n, row, gz, nz, sums_z, sums, send_r, recv_r)
        row = sum_finish(n, nz, sums, recv_r)
        sum_start(n + 1, row, gy, ny, sums_y, sums, send_r, recv_r)
        return sum_finish(n + 1, ny, sums, recv_r)

    target = total_target(lz, ly, lx, nz, ny)
    lane = iota((1, 128), 1)
    inside = (lane >= 1) & (lane < SPLIT)
    wide = FINE * SPLIT
    factors = [E ** (-0.5 * (LOW_LOG + wide * j)) for j in range(SPLIT + 1)]
    row = everywhere(0, volumes(amount, low_v, high_v, None, factors, range(SPLIT + 1)))
    index = count_above(row, inside, target)
    low = LOW_LOG + wide * index
    ends = (entry(row, index), entry(row, index + 1.0))
    factors = [E ** (-0.5 * FINE * j) for j in range(1, SPLIT)]
    row = everywhere(
        2, volumes(amount, low_v, high_v, jnp.exp(-0.5 * low), factors, range(1, SPLIT))
    )
    row = jnp.where(lane == 0, ends[0], jnp.where(lane == SPLIT, ends[1], row))
    index = count_above(row, inside, target)
    final = secant(low + FINE * index, entry(row, index), entry(row, index + 1.0), target)
    factor = jnp.exp(-0.5 * final)

    def finish(k, carry):
        new_v[k] = finished(amount[k], weight_of(k), factor, design_v[k], solid_v[k], void_v[k])
        return carry

    lax.fori_loop(0, lz, finish, 0)
    store = pltpu.make_async_copy(new_v, new_design, store_sem)
    store.start()
    for n, size in enumerate((nz, ny, nz, ny)):
        sum_sent(n, size, sums, send_r)
    store.wait()


def written_kernel(new_design, sens, new_out, sens_out, sem):
    copies = [
        pltpu.make_async_copy(src, dst, sem.at[n])
        for n, (src, dst) in enumerate(((new_design, new_out), (sens, sens_out)))
    ]
    for copy in copies:
        copy.start()
    for copy in copies:
        copy.wait()


def per_device(displacement, design, void_mask, solid_mask, stiffness):
    nz, ny = lax.axis_size("gz"), lax.axis_size("gy")
    lz, ly, lx = design.shape
    brick = jax.ShapeDtypeStruct(design.shape, F32)
    padded = (lz + 2 * H, ly + 16, lx)
    anywhere = pl.BlockSpec(memory_space=pltpu.HBM)
    sem = pltpu.SemaphoreType
    nodes = pltpu.VMEM((3, lz + 1, ly + 8, lx), F32)
    line, table = pltpu.VMEM((lz, lx), F32), pltpu.VMEM((ly, lx), F32)
    bricks = [pltpu.VMEM(design.shape, F32)] * 4
    masks = [pltpu.VMEM(design.shape, jnp.int32)] * 2
    sums = pltpu.VMEM((4, max(nz, ny), 1, 128), F32)
    new_design, sens, found = pl.pallas_call(
        functools.partial(kernel, nz, ny),
        out_shape=(brick, brick, jax.ShapeDtypeStruct((1,), jnp.int32)),
        in_specs=[anywhere] * 4 + [pl.BlockSpec(memory_space=pltpu.VMEM)],
        out_specs=(anywhere, anywhere, pl.BlockSpec(memory_space=pltpu.SMEM)),
        scratch_shapes=[
            nodes,
            pltpu.VMEM(padded, F32),
            pltpu.VMEM(padded, F32),
            pltpu.VMEM((lz, ly + 16, lx), F32),
            *masks,
            *bricks,
            pltpu.VMEM(design.shape, F32),
            pltpu.VMEM(design.shape, F32),
            nodes, nodes, nodes,
            pltpu.VMEM((lz + 1, ly // 8, 8, lx), F32),
            pltpu.VMEM((lx, lx), BF16),
            pltpu.VMEM((192, 224), BF16),
            table, table, line, line,
            pltpu.VMEM((8, ly, lx), F32),
            pltpu.VMEM((8, 16, lx), F32),
            pltpu.VMEM((2, 16, lx), F32),
            sums,
            sem.DMA((4,)), sem.DMA((2,)),
            sem.DMA((11,)), sem.DMA((11,)), sem.DMA((8,)), sem.DMA((8,)),
            sem.DMA((4,)), sem.DMA((4,)), sem.REGULAR,
        ],
        compiler_params=pltpu.CompilerParams(
            collective_id=0, has_side_effects=True, vmem_limit_bytes=60 * 1024 * 1024
        ),
    )(displacement, design, void_mask, solid_mask, stiffness)

    def exact(new_design, design, void_mask, solid_mask, sens):
        return pl.pallas_call(
            functools.partial(exact_kernel, nz, ny),
            out_shape=brick,
            in_specs=[anywhere] * 4,
            out_specs=anywhere,
            scratch_shapes=[
                pltpu.VMEM(design.shape, F32), *masks,
                *bricks,
                table, line, sums,
                sem.DMA((4,)), sem.DMA, sem.DMA((4,)), sem.DMA((4,)),
            ],
            compiler_params=pltpu.CompilerParams(
                collective_id=1, has_side_effects=True, vmem_limit_bytes=60 * 1024 * 1024
            ),
        )(design, void_mask, solid_mask, sens)

    new_design = lax.switch(
        found[0], (exact, lambda new_design, *rest: new_design),
        new_design, design, void_mask, solid_mask, sens,
    )
    return pl.pallas_call(
        written_kernel,
        out_shape=(brick, brick),
        in_specs=[anywhere] * 2,
        out_specs=(anywhere, anywhere),
        scratch_shapes=[sem.DMA((2,))],
        compiler_params=pltpu.CompilerParams(vmem_limit_bytes=4 * 1024 * 1024),
    )(new_design, sens)


def solution(mesh):
    return jax.shard_map(
        per_device,
        mesh=mesh,
        in_specs=(
            P(None, "gz", "gy", None),
            P("gz", "gy", None),
            P("gz", "gy", None),
            P("gz", "gy", None),
            P(),
        ),
        out_specs=(P("gz", "gy", None), P("gz", "gy", None)),
        check_vma=False,
    )
```

```python
import functools

import jax
import jax.numpy as jnp
from jax import lax
from jax.experimental import pallas as pl
from jax.experimental.pallas import tpu as pltpu
from jax.sharding import PartitionSpec as P

MESH = pl.DeviceIdType.MESH
F32 = jnp.float32
BF16 = jnp.bfloat16

TAPS = (1.0, 2.0, 3.0, 4.0, 3.0, 2.0, 1.0)
LOW_LOG = -25.0
HIGH_LOG = 25.0
MOVE_LIMIT = 0.2
VOLUME_FRACTION = 0.5
PENALTY = 3.0
SPLIT = 16
GRID = SPLIT * SPLIT
FINE = (HIGH_LOG - LOW_LOG) / GRID
ROUGH = 64
WINDOW = 8
E = 2.718281828459045

H = 3
Y0 = 8


def line_total(p, extent):
    low = jnp.maximum(3 - p, 0)
    high = jnp.maximum(p - (extent - 4), 0)
    missing = low * (low + 1) + high * (high + 1)
    return 16.0 - 0.5 * missing.astype(F32)


def line_spread(p, extent):
    total = None
    for d in range(-3, 4):
        near = p + d
        term = jnp.where(
            (near >= 0) & (near < extent), TAPS[d + 3] / line_total(near, extent), 0.0
        )
        total = term if total is None else total + term
    return total


def iota(shape, dim):
    return lax.broadcasted_iota(jnp.int32, shape, dim)


def split_bf16(x):
    high = x.astype(BF16)
    low = (x - high.astype(F32)).astype(BF16)
    return high, low


def dot(a, b):
    return jnp.dot(a, b, preferred_element_type=F32)


def row_filter(ref, layer, rows, first=0):
    at = Y0 - H + first
    c = [ref[layer, at + t : at + t + rows, :] for t in range(7)]
    return (c[0] + c[6]) + 2.0 * (c[1] + c[5]) + 3.0 * (c[2] + c[4]) + 4.0 * c[3]


def layer_filter(src, dst, layers, first=0, rows=None, first_row=0):
    rows = src.shape[1] if rows is None else rows
    for r in range(0, rows, 8):
        for c in range(0, src.shape[2], 128):
            col = slice(c, c + 128)
            f = [src[first + k, first_row + r : first_row + r + 8, col] for k in range(layers + 2 * H)]
            f = [a + b for a, b in zip(f, f[1:])]
            f = [a + b for a, b in zip(f, f[2:])]
            f = [a + b for a, b in zip(f, f[1:])]
            f = [a + b for a, b in zip(f, f[2:])]
            for k in range(layers):
                dst[k, r : r + 8, col] = f[k]


def sum_start(n, row, at, size, to, sums, send, recv):
    sums[n, at] = row
    copies = [
        pltpu.make_async_remote_copy(
            src_ref=sums.at[n, at], dst_ref=sums.at[n, at],
            send_sem=send.at[n], recv_sem=recv.at[n],
            device_id=to(d), device_id_type=MESH,
        )
        for d in range(1, size)
    ]
    for copy in copies:
        copy.start()


def sum_finish(n, size, sums, recv):
    everyone = sums.at[n, 0 : size - 1]
    pltpu.make_async_copy(everyone, everyone, recv.at[n]).wait()
    return jnp.sum(sums[n, 0:size], axis=0)


def sum_sent(n, size, sums, send):
    everyone = sums.at[n, 0 : size - 1]
    pltpu.make_async_copy(everyone, everyone, send.at[n]).wait()


def to_lanes(rows, lanes):
    count = -(-(max(lanes) + 1) // 8) * 8
    sub = iota((count, 128), 0)
    stacked = jnp.zeros((count, 128), F32)
    for row, j in zip(rows, lanes):
        stacked = jnp.where(sub == j, jnp.sum(row, axis=0, keepdims=True), stacked)
    line = jnp.sum(stacked, axis=1, keepdims=True)
    return jnp.sum(jnp.where(sub == iota((count, 128), 1), line, 0.0), axis=0, keepdims=True)


def volumes(amount, low_v, high_v, scale, factors, lanes):
    lz, ly, lx = amount.shape

    def layer(k, totals):
        totals = list(totals)
        for r in range(0, ly, 8):
            for c in range(0, lx, 128):
                at = (k, slice(r, r + 8), slice(c, c + 128))
                a, low, high = amount[at], low_v[at], high_v[at]
                if scale is not None:
                    a = a * scale
                for j, factor in enumerate(factors):
                    totals[j] = totals[j] + jnp.minimum(jnp.maximum(a * factor, low), high)
        return tuple(totals)

    totals = lax.fori_loop(0, lz, layer, tuple(jnp.zeros((8, 128), F32) for _ in factors))
    return to_lanes(totals, lanes)


def count_above(row, inside, target):
    return jnp.sum(jnp.where(inside & (row > target), 1.0, 0.0), axis=1, keepdims=True)


def entry(row, index):
    at = iota(row.shape, 1).astype(F32)
    return jnp.sum(jnp.where(at == index, row, 0.0), axis=1, keepdims=True)


def secant(low, low_volume, high_volume, target):
    return low + FINE * ((low_volume - target) / (low_volume - high_volume))


def weights(ref, z_ref, gy, ny, gz, nz):
    ly, lx = ref.shape
    lz = z_ref.shape[0]
    ref[...] = line_spread(iota((ly, lx), 0) + gy * ly, ly * ny) * line_spread(iota((ly, lx), 1), lx)
    z_ref[...] = line_spread(iota((lz, lx), 0) + gz * lz, lz * nz)


def bounds(weight, d, solid, void):
    low = jnp.maximum(d - MOVE_LIMIT, 0.0) * weight
    high = jnp.minimum(d + MOVE_LIMIT, 1.0) * weight
    is_solid, is_void = solid == 1, void == 1
    low = jnp.where(is_solid, weight, jnp.where(is_void, 0.0, low))
    high = jnp.where(is_solid, weight, jnp.where(is_void, 0.0, high))
    return low, high


def finished(a, weight, factor, d, solid, void):
    moved = (a / weight) * factor
    moved = jnp.minimum(
        jnp.maximum(moved, jnp.maximum(d - MOVE_LIMIT, 0.0)), jnp.minimum(d + MOVE_LIMIT, 1.0)
    )
    return jnp.where(solid == 1, 1.0, jnp.where(void == 1, 0.0, moved))


def total_target(lz, ly, lx, nz, ny):
    return VOLUME_FRACTION * (lz * nz) * (ly * ny) * lx


def kernel(
    nz, ny,
    disp, design, void, solid, stiff,
    new_design, sens, found,
    dpad, fpad, qpad, zbuf, void_v, solid_v, energy, amount, low_v, high_v, sens_v, new_v,
    shifted, double, double_s, edge, tx, k_rows, cube_yx, weight_yx, cube_z, weight_z, zs, qs, zq, sums,
    load_sem, store_sem, send1, recv1, send2, recv2, send_r, recv_r,
):
    lz, ly, lx = design.shape
    gz, gy = lax.axis_index("gz"), lax.axis_index("gy")
    has = {
        (1, 0): gz < nz - 1, (-1, 0): gz > 0, (0, 1): gy < ny - 1, (0, -1): gy > 0,
    }
    for dz in (-1, 1):
        for dy in (-1, 1):
            has[dz, dy] = has[dz, 0] & has[0, dy]

    def peer(dz, dy):
        return (lax.rem(gz + dz % nz, nz), lax.rem(gy + dy % ny, ny))

    directions = [(1, 0), (-1, 0), (0, 1), (0, -1), (1, 1), (1, -1), (-1, 1), (-1, -1)]

    own_f = fpad.at[H : H + lz, Y0 : Y0 + ly, :]
    loads = [
        pltpu.make_async_copy(disp, dpad.at[:, 0:lz, 0:ly, :], load_sem.at[0]),
        pltpu.make_async_copy(design, own_f, load_sem.at[1]),
        pltpu.make_async_copy(void, void_v, load_sem.at[2]),
        pltpu.make_async_copy(solid, solid_v, load_sem.at[3]),
    ]
    for copy in loads:
        copy.start()

    barrier = pltpu.get_barrier_semaphore()
    ways = directions + [(d, 0) for d in range(2, nz - 1)] + [(0, d) for d in range(2, ny - 1)]
    for way in ways:
        pl.semaphore_signal(barrier, inc=1, device_id=peer(*way), device_id_type=MESH)

    for pad in (fpad, qpad):
        @pl.when(gz == 0)
        def _():
            pad[0:H] = jnp.zeros_like(pad[0:H])

        @pl.when(gz == nz - 1)
        def _():
            pad[lz + H :] = jnp.zeros_like(pad[lz + H :])

        @pl.when(gy == 0)
        def _():
            pad[:, 0:Y0] = jnp.zeros_like(pad[:, 0:Y0])

        @pl.when(gy == ny - 1)
        def _():
            pad[:, Y0 + ly :] = jnp.zeros_like(pad[:, Y0 + ly :])

    @pl.when(gz == nz - 1)
    def _():
        dpad[:, lz] = jnp.zeros_like(dpad[:, lz])

    @pl.when(gy == ny - 1)
    def _():
        dpad[:, :, ly:] = jnp.zeros_like(dpad[:, :, ly:])

    pl.semaphore_wait(barrier, len(ways))

    near_z = {1: slice(lz - H, lz), -1: slice(0, H), 0: slice(0, lz)}
    near_y = {1: slice(ly - H, ly), -1: slice(0, H), 0: slice(0, ly)}
    far_z = {1: slice(0, H), -1: slice(H + lz, lz + 2 * H), 0: slice(H, H + lz)}
    far_y = {1: slice(Y0 - H, Y0), -1: slice(Y0 + ly, Y0 + ly + H), 0: slice(Y0, Y0 + ly)}

    def halo(src, src_at, pad, send, recv, n):
        dz, dy = directions[n]
        return pltpu.make_async_remote_copy(
            src_ref=src.at[src_at[0][dz], src_at[1][dy], :],
            dst_ref=pad.at[far_z[dz], far_y[dy], :],
            send_sem=send.at[n], recv_sem=recv.at[n],
            device_id=peer(dz, dy), device_id_type=MESH,
        )

    def start(direction, copy):
        @pl.when(has[direction])
        def _():
            copy.start()

    def wait_recv(direction, copy):
        @pl.when(has[-direction[0], -direction[1]])
        def _():
            copy.wait_recv()

    def wait_send(direction, copy):
        @pl.when(has[direction])
        def _():
            copy.wait_send()

    def nodes(n, direction, layers, rows, to_layers, to_rows):
        return direction, pltpu.make_async_remote_copy(
            src_ref=disp.at[:, layers, rows, :],
            dst_ref=dpad.at[:, to_layers, to_rows, :],
            send_sem=send1.at[8 + n], recv_sem=recv1.at[8 + n],
            device_id=peer(*direction), device_id_type=MESH,
        )

    first_z, top_z = slice(0, 1), slice(lz, lz + 1)
    first_y, top_y = slice(0, 1), slice(ly, ly + 1)
    own_z, own_y = slice(0, lz), slice(0, ly)
    node_copies = [
        nodes(0, (0, -1), own_z, first_y, own_z, top_y),
        nodes(1, (-1, -1), first_z, first_y, top_z, top_y),
        nodes(2, (-1, 0), first_z, own_y, top_z, own_y),
    ]
    design_copies = [
        (directions[n], halo(design, (near_z, near_y), fpad, send1, recv1, n)) for n in range(8)
    ]
    for n in (4, 5, 6, 7, 2, 3):
        start(*design_copies[n])
    start(*node_copies[1])
    start(*node_copies[0])
    start(*design_copies[0])
    start(*design_copies[1])

    across = jnp.abs(iota((lx, lx), 0) - iota((lx, lx), 1))
    tx[...] = jnp.maximum(4 - across, 0).astype(F32).astype(BF16)
    full_z, full_y = lz * nz, ly * ny
    row_at = iota((ly, lx), 0) + gy * ly
    col_at = iota((ly, lx), 1)
    inv_yx = 1.0 / (line_total(row_at, full_y) * line_total(col_at, lx))
    cube_yx[...] = (-PENALTY) * inv_yx * inv_yx * inv_yx
    layer_at = iota((lz, lx), 0) + gz * lz
    inv_z = 1.0 / line_total(layer_at, full_z)
    cube_z[...] = inv_z * inv_z * inv_z
    weights(weight_yx, weight_z, gy, ny, gz, nz)

    size, width = 24 * 8, 12 * 8 + 16
    pick = (lax.shift_right_logical(iota((size, 24), 0), 3) == iota((size, 24), 1)).astype(F32).astype(BF16)
    entry_at, col = iota((24, 2 * width), 0), iota((24, 2 * width), 1)

    def part_col(col):
        return jnp.where(col >= width, col - width, col)

    col = part_col(col)
    corner = sum((entry_at >= 6 * n).astype(jnp.int32) for n in (1, 2, 3))
    step_y = corner & 1
    rest = entry_at - 6 * corner
    group = jnp.where(corner >= 2, 6, 0) + rest
    tail = col - 12 * 8
    tail_rest = tail & 7
    tail_group = jnp.where(tail_rest < 6, jnp.where(tail >= 8, 6, 0) + tail_rest, -1)
    col_group = jnp.where(col < 12 * 8, lax.shift_right_logical(col, 3), tail_group)
    places = [
        ((group == col_group) & (step_y == n)).astype(F32).astype(BF16) for n in range(2)
    ]
    col = part_col(iota((size, 2 * width), 1))
    up = jnp.where(col < 12 * 8, col & 7, 8) - (iota((size, 2 * width), 0) & 7)
    halves = []
    for part in split_bf16(stiff[...]):
        rows = dot(pick, part).astype(BF16)
        same, next_row = dot(rows, places[0]), dot(rows, places[1])
        halves.append(jnp.where(up == 0, same, jnp.where(up == 1, next_row, 0.0)))
    is_low = iota((size, 2 * width), 1) >= width
    k_rows[...] = jnp.where(is_low, halves[1], halves[0]).astype(BF16)

    def nodes_at(k, first, last):
        at = slice(first, last)
        last_col = iota((last - first, lx), 1) == lx - 1
        for q in range(3):
            u = dpad[q, k, at]
            v = jnp.where(last_col, 0.0, pltpu.roll(u, lx - 1, 1))
            shifted[q, k, at] = v
            double[q, k, at] = 2.0 * u - u.astype(BF16).astype(F32)
            double_s[q, k, at] = 2.0 * v - v.astype(BF16).astype(F32)

    def ninth_rows(k, tiles_of):
        for tile in tiles_of:
            at = slice(8 * tile + 8, 8 * tile + 9)
            rows = [ref[q, k, at, :] for ref in (dpad, shifted) for q in range(3)]
            edge[k, tile] = jnp.concatenate(rows + [jnp.zeros((2, lx), F32)], axis=0)

    def element_rows(k, tile):
        at = slice(8 * tile, 8 * tile + 8)
        u = [ref[q, k + a, at, :] for a in range(2) for ref in (dpad, shifted) for q in range(3)]
        u += [edge[k + a, tile] for a in range(2)]
        high = jnp.concatenate(u, axis=0).astype(BF16)
        forces = dot(k_rows[...], jnp.concatenate([high, high], axis=0))
        total = None
        for n in range(24):
            a, b, c, q = n // 12, n // 6 % 2, n // 3 % 2, n % 3
            ref = double_s if c else double
            term = ref[q, k + a, 8 * tile + b : 8 * tile + b + 8, :] * forces[8 * n : 8 * n + 8]
            total = term if total is None else total + term
        energy[k, at, :] = jnp.maximum(total, 0.0)

    tiles = ly // 8

    def energy_of(count, layer_of, tiles_of):
        def body(n, carry):
            for k in layer_of(n):
                for tile in tiles_of:
                    element_rows(k, tile)
            return carry

        lax.fori_loop(0, count, body, 0)

    inner = lz - 2 * H
    sums_z, sums_y = lambda d: peer(d, 0), lambda d: peer(0, d)
    target = total_target(lz, ly, lx, nz, ny)
    lane = iota((1, 128), 1)

    def weight_of(k):
        return weight_yx[...] * weight_z[pl.ds(k, 1), :]

    s_z, s_y = lz // 2 - 1, ly // 2 - 4
    q_z, q_y = s_z - H, s_y - 4
    for load in loads:
        load.wait()

    def own_nodes(k, carry):
        nodes_at(k, 0, ly)
        ninth_rows(k, range(tiles - 1))
        return carry

    lax.fori_loop(0, lz, own_nodes, 0)
    energy_of(4, lambda n: [q_z + 2 * n, q_z + 2 * n + 1], [q_y // 8, q_y // 8 + 1])
    start(*node_copies[2])
    layer_filter(fpad, zs, 8, H + q_z - H, ly, Y0)
    f = jnp.concatenate([row_filter(zs, k, 16, q_y - Y0) for k in range(8)], axis=0)
    high, low = split_bf16(f)
    f = dot(high, tx[...]) + dot(low, tx[...])
    f = jnp.concatenate(
        [
            f[16 * k : 16 * k + 16] * f[16 * k : 16 * k + 16]
            * (energy[q_z + k, q_y : q_y + 16] * (cube_yx[q_y : q_y + 16] * cube_z[q_z + k : q_z + k + 1]))
            for k in range(8)
        ],
        axis=0,
    )
    high, low = split_bf16(f)
    f = dot(high, tx[...]) + dot(low, tx[...])
    for k in range(8):
        qs[k] = f[16 * k : 16 * k + 16]
    layer_filter(qs, zq, 2)
    sample = []
    for k in range(2):
        rows = slice(s_y, s_y + 8)
        d = fpad[H + s_z + k, Y0 + s_y : Y0 + s_y + 8]
        weight = weight_yx[rows] * weight_z[s_z + k : s_z + k + 1]
        a = d * jnp.sqrt(-row_filter(zq, k, 8, 4 - (Y0)) * weight)
        lo, hi = bounds(weight, d, solid_v[s_z + k, rows], void_v[s_z + k, rows])
        for c in range(0, lx, 128):
            sample.append((a[:, c : c + 128], lo[:, c : c + 128], hi[:, c : c + 128]))
    rough = (HIGH_LOG - LOW_LOG) / ROUGH
    totals = []
    for j in range(ROUGH):
        factor = E ** (-0.5 * (LOW_LOG + rough * j))
        parts = [jnp.minimum(jnp.maximum(a * factor, lo), hi) for a, lo, hi in sample]
        total = parts[0]
        for part in parts[1:]:
            total = total + part
        totals.append(total)
    row = to_lanes(totals, range(ROUGH))
    sum_start(0, row, gz, nz, sums_z, sums, send_r, recv_r)

    energy_of(2 * H - 1, lambda n: [n + (n // H) * inner], range(tiles - 1))
    rest = [k for k in range(H, lz - H) if not q_z <= k < q_z + 8]
    others = [t for t in range(1, tiles - 1) if not q_y // 8 <= t < q_y // 8 + 2]
    energy_of(1, lambda n: rest, range(1, tiles - 1))
    if others:
        energy_of(8, lambda n: [q_z + n], others)
    energy_of(inner // 2, lambda n: [H + 2 * n, H + 2 * n + 1], [0])
    wait_recv(*node_copies[0])
    wait_recv(*node_copies[1])

    def side_nodes(k, carry):
        nodes_at(k, ly, ly + 8)
        ninth_rows(k, [tiles - 1])
        return carry

    lax.fori_loop(0, lz, side_nodes, 0)
    energy_of((lz - 1) // 3, lambda n: [3 * n, 3 * n + 1, 3 * n + 2], [tiles - 1])

    for copy in design_copies:
        wait_recv(*copy)
    layer_filter(fpad, zbuf, lz)

    def source(layers, first, last):
        n = last - first
        f = jnp.concatenate([row_filter(zbuf, k, n, first) for k in layers], axis=0)
        high, low = split_bf16(f)
        f = dot(high, tx[...]) + dot(low, tx[...])
        cube = cube_yx[first:last]
        f = jnp.concatenate(
            [
                f[i * n : (i + 1) * n] * f[i * n : (i + 1) * n]
                * (energy[k, first:last] * (cube * cube_z[k : k + 1, :]))
                for i, k in enumerate(layers)
            ],
            axis=0,
        )
        high, low = split_bf16(f)
        f = dot(high, tx[...]) + dot(low, tx[...])
        for i, k in enumerate(layers):
            qpad[H + k, Y0 + first : Y0 + last, :] = f[i * n : (i + 1) * n]

    own_zq = {1: slice(lz, lz + H), -1: slice(H, 2 * H), 0: slice(H, H + lz)}
    own_yq = {1: slice(Y0 + ly - H, Y0 + ly), -1: slice(Y0, Y0 + H), 0: slice(Y0, Y0 + ly)}
    source_copies = [
        (directions[n], halo(qpad, (own_zq, own_yq), qpad, send2, recv2, n)) for n in range(8)
    ]
    middle = range(H, lz - H)
    source(range(H), 0, ly)
    source(middle, 0, 8)
    source(middle, ly - 8, ly)
    wait_recv(*node_copies[2])
    nodes_at(lz, 0, ly + 8)
    ninth_rows(lz, range(tiles))
    for tile in range(tiles):
        element_rows(lz - 1, tile)
    source(range(lz - H, lz), 0, ly)
    for n in (4, 5, 6, 7, 2, 3, 0, 1):
        start(*source_copies[n])
    row = sum_finish(0, nz, sums, recv_r)
    sum_start(1, row, gy, ny, sums_y, sums, send_r, recv_r)

    source(range(H, lz // 2), 8, ly - 8)
    source(range(lz // 2, lz - H), 8, ly - 8)

    def bounds_of(k, carry):
        low_v[k], high_v[k] = bounds(weight_of(k), fpad[H + k, Y0 : Y0 + ly, :], solid_v[k], void_v[k])
        return carry

    lax.fori_loop(0, lz, bounds_of, 0)

    row = sum_finish(1, ny, sums, recv_r)
    part = target * (16.0 / (lz * ly))
    index = count_above(row, lane < ROUGH, part)
    below, above = entry(row, index - 1.0), entry(row, index)
    step = jnp.where((index > 0.0) & (index < ROUGH), (below - part) / (below - above), 0.0)
    guess = (GRID // ROUGH) * (index - 1.0 + step)
    first = jnp.clip(jnp.floor(guess) - (WINDOW // 2 - 1), 0.0, GRID + 1.0 - WINDOW)
    low = LOW_LOG + FINE * first
    window_factor = jnp.exp(-0.5 * low)
    factors = [E ** (-0.5 * FINE * j) for j in range(WINDOW)]

    for copy in source_copies:
        wait_recv(*copy)
    layer_filter(qpad, zbuf, lz)
    for k in range(lz):
        s = row_filter(zbuf, k, ly)
        sens_v[k] = s
        amount[k] = fpad[H + k, Y0 : Y0 + ly, :] * jnp.sqrt(-s * weight_of(k))
    store_sens = pltpu.make_async_copy(sens_v, sens, store_sem.at[0])
    store_sens.start()

    row = volumes(amount, low_v, high_v, window_factor, factors, range(WINDOW))
    sum_start(2, row, gz, nz, sums_z, sums, send_r, recv_r)
    row = sum_finish(2, nz, sums, recv_r)
    sum_start(3, row, gy, ny, sums_y, sums, send_r, recv_r)
    row = sum_finish(3, ny, sums, recv_r)
    index = count_above(row, lane < WINDOW, target)
    hit = (index > 0.0) & (index < WINDOW)
    found[0] = jnp.sum(jnp.where(hit, 1.0, 0.0)).astype(jnp.int32)
    index = index - 1.0
    final = secant(low + FINE * index, entry(row, index), entry(row, index + 1.0), target)
    factor = jnp.exp(-0.5 * final)

    def finish(k, carry):
        d = fpad[H + k, Y0 : Y0 + ly, :]
        new_v[k] = finished(amount[k], weight_of(k), factor, d, solid_v[k], void_v[k])
        return carry

    lax.fori_loop(0, lz, finish, 0)
    store_new = pltpu.make_async_copy(new_v, new_design, store_sem.at[1])
    store_new.start()

    for copy in node_copies + design_copies + source_copies:
        wait_send(*copy)
    for n, size in enumerate((nz, ny, nz, ny)):
        sum_sent(n, size, sums, send_r)
    store_sens.wait()
    store_new.wait()


def exact_kernel(
    nz, ny,
    design, void, solid, sens,
    new_design,
    design_v, void_v, solid_v, amount, low_v, high_v, new_v, weight_yx, weight_z, sums,
    load_sem, store_sem, send_r, recv_r,
):
    lz, ly, lx = design.shape
    gz, gy = lax.axis_index("gz"), lax.axis_index("gy")

    def sums_z(d):
        return (lax.rem(gz + d, nz), gy)

    def sums_y(d):
        return (gz, lax.rem(gy + d, ny))

    loads = [
        pltpu.make_async_copy(src, dst, load_sem.at[n])
        for n, (src, dst) in enumerate(
            ((design, design_v), (void, void_v), (solid, solid_v), (sens, amount))
        )
    ]
    for load in loads:
        load.start()
    barrier = pltpu.get_barrier_semaphore()
    partners = [sums_z(d) for d in range(1, nz)] + [sums_y(d) for d in range(1, ny)]
    for partner in partners:
        pl.semaphore_signal(barrier, inc=1, device_id=partner, device_id_type=MESH)
    weights(weight_yx, weight_z, gy, ny, gz, nz)
    for load in loads:
        load.wait()

    def weight_of(k):
        return weight_yx[...] * weight_z[pl.ds(k, 1), :]

    def prepare(k, carry):
        d = design_v[k]
        low_v[k], high_v[k] = bounds(weight_of(k), d, solid_v[k], void_v[k])
        amount[k] = d * jnp.sqrt(-amount[k] * weight_of(k))
        return carry

    lax.fori_loop(0, lz, prepare, 0)
    pl.semaphore_wait(barrier, len(partners))

    def everywhere(n, row):
        sum_start(n, row, gz, nz, sums_z, sums, send_r, recv_r)
        row = sum_finish(n, nz, sums, recv_r)
        sum_start(n + 1, row, gy, ny, sums_y, sums, send_r, recv_r)
        return sum_finish(n + 1, ny, sums, recv_r)

    target = total_target(lz, ly, lx, nz, ny)
    lane = iota((1, 128), 1)
    inside = (lane >= 1) & (lane < SPLIT)
    wide = FINE * SPLIT
    factors = [E ** (-0.5 * (LOW_LOG + wide * j)) for j in range(SPLIT + 1)]
    row = everywhere(0, volumes(amount, low_v, high_v, None, factors, range(SPLIT + 1)))
    index = count_above(row, inside, target)
    low = LOW_LOG + wide * index
    ends = (entry(row, index), entry(row, index + 1.0))
    factors = [E ** (-0.5 * FINE * j) for j in range(1, SPLIT)]
    row = everywhere(
        2, volumes(amount, low_v, high_v, jnp.exp(-0.5 * low), factors, range(1, SPLIT))
    )
    row = jnp.where(lane == 0, ends[0], jnp.where(lane == SPLIT, ends[1], row))
    index = count_above(row, inside, target)
    final = secant(low + FINE * index, entry(row, index), entry(row, index + 1.0), target)
    factor = jnp.exp(-0.5 * final)

    def finish(k, carry):
        new_v[k] = finished(amount[k], weight_of(k), factor, design_v[k], solid_v[k], void_v[k])
        return carry

    lax.fori_loop(0, lz, finish, 0)
    store = pltpu.make_async_copy(new_v, new_design, store_sem)
    store.start()
    for n, size in enumerate((nz, ny, nz, ny)):
        sum_sent(n, size, sums, send_r)
    store.wait()


def written_kernel(new_design, sens, new_out, sens_out, sem):
    copies = [
        pltpu.make_async_copy(src, dst, sem.at[n])
        for n, (src, dst) in enumerate(((new_design, new_out), (sens, sens_out)))
    ]
    for copy in copies:
        copy.start()
    for copy in copies:
        copy.wait()


def per_device(displacement, design, void_mask, solid_mask, stiffness):
    nz, ny = lax.axis_size("gz"), lax.axis_size("gy")
    lz, ly, lx = design.shape
    brick = jax.ShapeDtypeStruct(design.shape, F32)
    padded = (lz + 2 * H, ly + 16, lx)
    anywhere = pl.BlockSpec(memory_space=pltpu.HBM)
    sem = pltpu.SemaphoreType
    nodes = pltpu.VMEM((3, lz + 1, ly + 8, lx), F32)
    line, table = pltpu.VMEM((lz, lx), F32), pltpu.VMEM((ly, lx), F32)
    bricks = [pltpu.VMEM(design.shape, F32)] * 4
    masks = [pltpu.VMEM(design.shape, jnp.int32)] * 2
    sums = pltpu.VMEM((4, max(nz, ny), 1, 128), F32)
    new_design, sens, found = pl.pallas_call(
        functools.partial(kernel, nz, ny),
        out_shape=(brick, brick, jax.ShapeDtypeStruct((1,), jnp.int32)),
        in_specs=[anywhere] * 4 + [pl.BlockSpec(memory_space=pltpu.VMEM)],
        out_specs=(anywhere, anywhere, pl.BlockSpec(memory_space=pltpu.SMEM)),
        scratch_shapes=[
            nodes,
            pltpu.VMEM(padded, F32),
            pltpu.VMEM(padded, F32),
            pltpu.VMEM((lz, ly + 16, lx), F32),
            *masks,
            *bricks,
            pltpu.VMEM(design.shape, F32),
            pltpu.VMEM(design.shape, F32),
            nodes, nodes, nodes,
            pltpu.VMEM((lz + 1, ly // 8, 8, lx), F32),
            pltpu.VMEM((lx, lx), BF16),
            pltpu.VMEM((192, 224), BF16),
            table, table, line, line,
            pltpu.VMEM((8, ly, lx), F32),
            pltpu.VMEM((8, 16, lx), F32),
            pltpu.VMEM((2, 16, lx), F32),
            sums,
            sem.DMA((4,)), sem.DMA((2,)),
            sem.DMA((11,)), sem.DMA((11,)), sem.DMA((8,)), sem.DMA((8,)),
            sem.DMA((4,)), sem.DMA((4,)),
        ],
        compiler_params=pltpu.CompilerParams(
            collective_id=0, has_side_effects=True, vmem_limit_bytes=60 * 1024 * 1024
        ),
    )(displacement, design, void_mask, solid_mask, stiffness)

    def exact(new_design, design, void_mask, solid_mask, sens):
        return pl.pallas_call(
            functools.partial(exact_kernel, nz, ny),
            out_shape=brick,
            in_specs=[anywhere] * 4,
            out_specs=anywhere,
            scratch_shapes=[
                pltpu.VMEM(design.shape, F32), *masks,
                *bricks,
                table, line, sums,
                sem.DMA((4,)), sem.DMA, sem.DMA((4,)), sem.DMA((4,)),
            ],
            compiler_params=pltpu.CompilerParams(
                collective_id=1, has_side_effects=True, vmem_limit_bytes=60 * 1024 * 1024
            ),
        )(design, void_mask, solid_mask, sens)

    new_design = lax.switch(
        found[0], (exact, lambda new_design, *rest: new_design),
        new_design, design, void_mask, solid_mask, sens,
    )
    return pl.pallas_call(
        written_kernel,
        out_shape=(brick, brick),
        in_specs=[anywhere] * 2,
        out_specs=(anywhere, anywhere),
        scratch_shapes=[sem.DMA((2,))],
        compiler_params=pltpu.CompilerParams(vmem_limit_bytes=4 * 1024 * 1024),
    )(new_design, sens)


def solution(mesh):
    return jax.shard_map(
        per_device,
        mesh=mesh,
        in_specs=(
            P(None, "gz", "gy", None),
            P("gz", "gy", None),
            P("gz", "gy", None),
            P("gz", "gy", None),
            P(),
        ),
        out_specs=(P("gz", "gy", None), P("gz", "gy", None)),
        check_vma=False,
    )
```

```python
import functools

import jax
import jax.numpy as jnp
from jax import lax
from jax.experimental import pallas as pl
from jax.experimental.pallas import tpu as pltpu
from jax.sharding import PartitionSpec as P

MESH = pl.DeviceIdType.MESH
NEAR_Z = [(d, 0) for d in (2, -2, 3, -3, 4, -4, 5, -5, 6, -6)]
NEAR_Y = [(0, d) for d in (2, -2, 8, 7, 9, 6, 10)]
F32 = jnp.float32
BF16 = jnp.bfloat16

TAPS = (1.0, 2.0, 3.0, 4.0, 3.0, 2.0, 1.0)
LOW_LOG = -25.0
HIGH_LOG = 25.0
MOVE_LIMIT = 0.2
VOLUME_FRACTION = 0.5
PENALTY = 3.0
SPLIT = 16
GRID = SPLIT * SPLIT
FINE = (HIGH_LOG - LOW_LOG) / GRID
ROUGH = 64
WINDOW = 8
E = 2.718281828459045

H = 3
Y0 = 8


def line_total(p, extent):
    low = jnp.maximum(3 - p, 0)
    high = jnp.maximum(p - (extent - 4), 0)
    missing = low * (low + 1) + high * (high + 1)
    return 16.0 - 0.5 * missing.astype(F32)


def line_spread(p, extent):
    total = None
    for d in range(-3, 4):
        near = p + d
        term = jnp.where(
            (near >= 0) & (near < extent), TAPS[d + 3] / line_total(near, extent), 0.0
        )
        total = term if total is None else total + term
    return total


def iota(shape, dim):
    return lax.broadcasted_iota(jnp.int32, shape, dim)


def split_bf16(x):
    high = x.astype(BF16)
    low = (x - high.astype(F32)).astype(BF16)
    return high, low


def dot(a, b):
    return jnp.dot(a, b, preferred_element_type=F32)


def row_filter(ref, layer, rows, first=0):
    at = Y0 - H + first
    c = [ref[layer, at + t : at + t + rows, :] for t in range(7)]
    return (c[0] + c[6]) + 2.0 * (c[1] + c[5]) + 3.0 * (c[2] + c[4]) + 4.0 * c[3]


def layer_filter(src, dst, layers, first=0, rows=None, shift=0, to=0):
    for r in range(0, src.shape[1], 8) if rows is None else rows:
        for c in range(0, src.shape[2], 128):
            col = slice(c, c + 128)
            f = [src[first + k, shift + r : shift + r + 8, col] for k in range(layers + 2 * H)]
            f = [a + b for a, b in zip(f, f[1:])]
            f = [a + b for a, b in zip(f, f[2:])]
            f = [a + b for a, b in zip(f, f[1:])]
            f = [a + b for a, b in zip(f, f[2:])]
            for k in range(layers):
                dst[to + k, r : r + 8, col] = f[k]


def sum_start(n, row, at, size, to, sums, send, recv):
    sums[n, at] = row
    copies = [
        pltpu.make_async_remote_copy(
            src_ref=sums.at[n, at], dst_ref=sums.at[n, at],
            send_sem=send.at[n], recv_sem=recv.at[n],
            device_id=to(d), device_id_type=MESH,
        )
        for d in range(1, size)
    ]
    for copy in copies:
        copy.start()


def sum_finish(n, size, sums, recv):
    everyone = sums.at[n, 0 : size - 1]
    pltpu.make_async_copy(everyone, everyone, recv.at[n]).wait()
    return jnp.sum(sums[n, 0:size], axis=0)


def sum_sent(n, size, sums, send):
    everyone = sums.at[n, 0 : size - 1]
    pltpu.make_async_copy(everyone, everyone, send.at[n]).wait()


def to_lanes(rows, lanes):
    count = -(-(max(lanes) + 1) // 8) * 8
    sub = iota((count, 128), 0)
    stacked = jnp.zeros((count, 128), F32)
    for row, j in zip(rows, lanes):
        stacked = jnp.where(sub == j, jnp.sum(row, axis=0, keepdims=True), stacked)
    line = jnp.sum(stacked, axis=1, keepdims=True)
    return jnp.sum(jnp.where(sub == iota((count, 128), 1), line, 0.0), axis=0, keepdims=True)


def volumes(amount, low_v, high_v, scale, factors, lanes):
    lz, ly, lx = amount.shape

    def layer(k, totals):
        totals = list(totals)
        for r in range(0, ly, 8):
            for c in range(0, lx, 128):
                at = (k, slice(r, r + 8), slice(c, c + 128))
                a, low, high = amount[at], low_v[at], high_v[at]
                if scale is not None:
                    a = a * scale
                for j, factor in enumerate(factors):
                    totals[j] = totals[j] + jnp.minimum(jnp.maximum(a * factor, low), high)
        return tuple(totals)

    totals = lax.fori_loop(0, lz, layer, tuple(jnp.zeros((8, 128), F32) for _ in factors))
    return to_lanes(totals, lanes)


def count_above(row, inside, target):
    return jnp.sum(jnp.where(inside & (row > target), 1.0, 0.0), axis=1, keepdims=True)


def entry(row, index):
    at = iota(row.shape, 1).astype(F32)
    return jnp.sum(jnp.where(at == index, row, 0.0), axis=1, keepdims=True)


def secant(low, low_volume, high_volume, target):
    return low + FINE * ((low_volume - target) / (low_volume - high_volume))


def weights(ref, z_ref, gy, ny, gz, nz):
    ly, lx = ref.shape
    lz = z_ref.shape[0]
    ref[...] = line_spread(iota((ly, lx), 0) + gy * ly, ly * ny) * line_spread(iota((ly, lx), 1), lx)
    z_ref[...] = line_spread(iota((lz, lx), 0) + gz * lz, lz * nz)


def bounds(weight, d, solid, void):
    low = jnp.maximum(d - MOVE_LIMIT, 0.0) * weight
    high = jnp.minimum(d + MOVE_LIMIT, 1.0) * weight
    is_solid, is_void = solid == 1, void == 1
    low = jnp.where(is_solid, weight, jnp.where(is_void, 0.0, low))
    high = jnp.where(is_solid, weight, jnp.where(is_void, 0.0, high))
    return low, high


def finished(b, factor, d, solid, void):
    moved = jnp.minimum(
        jnp.maximum(b * factor, jnp.maximum(d - MOVE_LIMIT, 0.0)), jnp.minimum(d + MOVE_LIMIT, 1.0)
    )
    return jnp.where(solid == 1, 1.0, jnp.where(void == 1, 0.0, moved))


def total_target(lz, ly, lx, nz, ny):
    return VOLUME_FRACTION * (lz * nz) * (ly * ny) * lx


def kernel(
    nz, ny,
    disp, design, void, solid, stiff,
    fields, found, factor_out,
    dpad, fpad, qpad, zbuf, void_v, solid_v, energy, amount, scaled, low_v, high_v, sens_v,
    shifted, double, double_s, edge, tx, stiff_v, k_rows, cube_yx, weight_yx, inv_yx, cube_z, weight_z, inv_z, zs, qs, zq, sums,
    load_sem, store_sem, send1, recv1, send2, recv2, send_r, recv_r, known,
):
    lz, ly, lx = design.shape
    gz, gy = lax.axis_index("gz"), lax.axis_index("gy")
    has = {
        (1, 0): gz < nz - 1, (-1, 0): gz > 0, (0, 1): gy < ny - 1, (0, -1): gy > 0,
    }
    for dz in (-1, 1):
        for dy in (-1, 1):
            has[dz, dy] = has[dz, 0] & has[0, dy]

    def peer(dz, dy):
        return (lax.rem(gz + dz % nz, nz), lax.rem(gy + dy % ny, ny))

    directions = [(1, 0), (-1, 0), (0, 1), (0, -1), (1, 1), (1, -1), (-1, 1), (-1, -1)]

    own_f = fpad.at[H : H + lz, Y0 : Y0 + ly, :]
    loads = [
        pltpu.make_async_copy(disp, dpad.at[:, 0:lz, 0:ly, :], load_sem.at[0]),
        pltpu.make_async_copy(design, own_f, load_sem.at[1]),
        pltpu.make_async_copy(void, void_v, load_sem.at[2]),
        pltpu.make_async_copy(solid, solid_v, load_sem.at[3]),
        pltpu.make_async_copy(stiff, stiff_v, load_sem.at[4]),
    ]
    for copy in loads:
        copy.start()

    barrier = pltpu.get_barrier_semaphore()
    ways = directions + NEAR_Z + NEAR_Y
    for way in ways:
        pl.semaphore_signal(barrier, inc=1, device_id=peer(*way), device_id_type=MESH)

    tells = ((2, 0), (-2, 0), (0, 2), (0, -2))

    for pad in (fpad, qpad):
        @pl.when(gz == 0)
        def _():
            pad[0:H] = jnp.zeros_like(pad[0:H])

        @pl.when(gz == nz - 1)
        def _():
            pad[lz + H :] = jnp.zeros_like(pad[lz + H :])

        @pl.when(gy == 0)
        def _():
            pad[:, 0:Y0] = jnp.zeros_like(pad[:, 0:Y0])

        @pl.when(gy == ny - 1)
        def _():
            pad[:, Y0 + ly :] = jnp.zeros_like(pad[:, Y0 + ly :])

    @pl.when(gz == nz - 1)
    def _():
        dpad[:, lz] = jnp.zeros_like(dpad[:, lz])

    @pl.when(gy == ny - 1)
    def _():
        dpad[:, :, ly:] = jnp.zeros_like(dpad[:, :, ly:])

    pl.semaphore_wait(barrier, len(ways))
    for way in tells:
        pl.semaphore_signal(known, inc=1, device_id=peer(*way), device_id_type=MESH)

    near_z = {1: slice(lz - H, lz), -1: slice(0, H), 0: slice(0, lz)}
    near_y = {1: slice(ly - H, ly), -1: slice(0, H), 0: slice(0, ly)}
    far_z = {1: slice(0, H), -1: slice(H + lz, lz + 2 * H), 0: slice(H, H + lz)}
    far_y = {1: slice(Y0 - H, Y0), -1: slice(Y0 + ly, Y0 + ly + H), 0: slice(Y0, Y0 + ly)}

    def halo(src, src_at, pad, send, recv, n):
        dz, dy = directions[n]
        return pltpu.make_async_remote_copy(
            src_ref=src.at[src_at[0][dz], src_at[1][dy], :],
            dst_ref=pad.at[far_z[dz], far_y[dy], :],
            send_sem=send.at[n], recv_sem=recv.at[n],
            device_id=peer(dz, dy), device_id_type=MESH,
        )

    def start(direction, copy):
        @pl.when(has[direction])
        def _():
            copy.start()

    def wait_recv(direction, copy):
        @pl.when(has[-direction[0], -direction[1]])
        def _():
            copy.wait_recv()

    def wait_send(direction, copy):
        @pl.when(has[direction])
        def _():
            copy.wait_send()

    def nodes(n, direction, layers, rows, to_layers, to_rows):
        return direction, pltpu.make_async_remote_copy(
            src_ref=disp.at[:, layers, rows, :],
            dst_ref=dpad.at[:, to_layers, to_rows, :],
            send_sem=send1.at[8 + n], recv_sem=recv1.at[8 + n],
            device_id=peer(*direction), device_id_type=MESH,
        )

    first_z, top_z = slice(0, 1), slice(lz, lz + 1)
    first_y, top_y = slice(0, 1), slice(ly, ly + 1)
    own_z, own_y = slice(0, lz), slice(0, ly)
    node_copies = [
        nodes(0, (0, -1), own_z, first_y, own_z, top_y),
        nodes(1, (-1, -1), first_z, first_y, top_z, top_y),
        nodes(2, (-1, 0), first_z, own_y, top_z, own_y),
    ]
    design_copies = [
        (directions[n], halo(design, (near_z, near_y), fpad, send1, recv1, n)) for n in range(8)
    ]
    for n in (4, 5, 6, 7, 2, 3):
        start(*design_copies[n])
    start(*node_copies[1])
    start(*node_copies[0])
    start(*design_copies[0])
    start(*design_copies[1])
    start(*node_copies[2])

    across = jnp.abs(iota((lx, lx), 0) - iota((lx, lx), 1))
    tx[...] = jnp.maximum(4 - across, 0).astype(F32).astype(BF16)
    full_z, full_y = lz * nz, ly * ny
    row_at = iota((ly, lx), 0) + gy * ly
    col_at = iota((ly, lx), 1)
    inv = 1.0 / (line_total(row_at, full_y) * line_total(col_at, lx))
    cube_yx[...] = (-PENALTY) * inv * inv * inv
    layer_at = iota((lz, lx), 0) + gz * lz
    inv = 1.0 / line_total(layer_at, full_z)
    cube_z[...] = inv * inv * inv
    weights(weight_yx, weight_z, gy, ny, gz, nz)
    inv_yx[...] = 1.0 / weight_yx[...]
    inv_z[...] = 1.0 / weight_z[...]

    size, width = 24 * 8, 12 * 8 + 16
    pick = (lax.shift_right_logical(iota((size, 24), 0), 3) == iota((size, 24), 1)).astype(F32).astype(BF16)
    entry_at, col = iota((24, 2 * width), 0), iota((24, 2 * width), 1)

    def part_col(col):
        return jnp.where(col >= width, col - width, col)

    col = part_col(col)
    corner = sum((entry_at >= 6 * n).astype(jnp.int32) for n in (1, 2, 3))
    step_y = corner & 1
    rest = entry_at - 6 * corner
    group = jnp.where(corner >= 2, 6, 0) + rest
    tail = col - 12 * 8
    tail_rest = tail & 7
    tail_group = jnp.where(tail_rest < 6, jnp.where(tail >= 8, 6, 0) + tail_rest, -1)
    col_group = jnp.where(col < 12 * 8, lax.shift_right_logical(col, 3), tail_group)
    places = [
        ((group == col_group) & (step_y == n)).astype(F32).astype(BF16) for n in range(2)
    ]
    col = part_col(iota((size, 2 * width), 1))
    up = jnp.where(col < 12 * 8, col & 7, 8) - (iota((size, 2 * width), 0) & 7)
    halves = []
    loads[4].wait()
    for part in split_bf16(stiff_v[...]):
        rows = dot(pick, part).astype(BF16)
        same, next_row = dot(rows, places[0]), dot(rows, places[1])
        halves.append(jnp.where(up == 0, same, jnp.where(up == 1, next_row, 0.0)))
    is_low = iota((size, 2 * width), 1) >= width
    k_rows[...] = jnp.where(is_low, halves[1], halves[0]).astype(BF16)

    def nodes_at(k, first, last):
        at = slice(first, last)
        last_col = iota((last - first, lx), 1) == lx - 1
        for q in range(3):
            u = dpad[q, k, at]
            v = jnp.where(last_col, 0.0, pltpu.roll(u, lx - 1, 1))
            shifted[q, k, at] = v
            double[q, k, at] = 2.0 * u - u.astype(BF16).astype(F32)
            double_s[q, k, at] = 2.0 * v - v.astype(BF16).astype(F32)

    def ninth_rows(k, tiles_of):
        for tile in tiles_of:
            at = slice(8 * tile + 8, 8 * tile + 9)
            rows = [ref[q, k, at, :] for ref in (dpad, shifted) for q in range(3)]
            edge[k, tile] = jnp.concatenate(rows + [jnp.zeros((2, lx), F32)], axis=0)

    def element_rows(k, tile):
        at = slice(8 * tile, 8 * tile + 8)
        u = [ref[q, k + a, at, :] for a in range(2) for ref in (dpad, shifted) for q in range(3)]
        u += [edge[k + a, tile] for a in range(2)]
        high = jnp.concatenate(u, axis=0).astype(BF16)
        forces = dot(k_rows[...], jnp.concatenate([high, high], axis=0))
        total = None
        for n in range(24):
            a, b, c, q = n // 12, n // 6 % 2, n // 3 % 2, n % 3
            ref = double_s if c else double
            term = ref[q, k + a, 8 * tile + b : 8 * tile + b + 8, :] * forces[8 * n : 8 * n + 8]
            total = term if total is None else total + term
        energy[k, at, :] = jnp.maximum(total, 0.0)

    tiles = ly // 8

    def energy_of(count, layer_of, tiles_of):
        def body(n, carry):
            for k in layer_of(n):
                for tile in tiles_of:
                    element_rows(k, tile)
            return carry

        lax.fori_loop(0, count, body, 0)

    inner = lz - 2 * H
    sums_z, sums_y = lambda d: peer(d, 0), lambda d: peer(0, d)
    target = total_target(lz, ly, lx, nz, ny)
    lane = iota((1, 128), 1)

    def weight_of(k):
        return weight_yx[...] * weight_z[pl.ds(k, 1), :]

    s_z, s_y = lz // 2 - 1, ly // 2 - 4
    q_z, q_y = s_z - H, s_y - 4
    for load in loads[:4]:
        load.wait()

    def own_nodes(k, carry):
        nodes_at(k, 0, ly)
        ninth_rows(k, range(tiles - 1))
        return carry

    lax.fori_loop(0, lz, own_nodes, 0)
    energy_of(4, lambda n: [q_z + 2 * n, q_z + 2 * n + 1], [q_y // 8, q_y // 8 + 1])
    layer_filter(fpad, zs, 8, q_z, range(0, ly, 8), Y0)
    f = jnp.concatenate([row_filter(zs, k, 16, q_y - Y0) for k in range(8)], axis=0)
    high, low = split_bf16(f)
    f = dot(high, tx[...]) + dot(low, tx[...])
    f = jnp.concatenate(
        [
            f[16 * k : 16 * k + 16] * f[16 * k : 16 * k + 16]
            * (energy[q_z + k, q_y : q_y + 16] * (cube_yx[q_y : q_y + 16] * cube_z[q_z + k : q_z + k + 1]))
            for k in range(8)
        ],
        axis=0,
    )
    high, low = split_bf16(f)
    f = dot(high, tx[...]) + dot(low, tx[...])
    for k in range(8):
        qs[k] = f[16 * k : 16 * k + 16]
    layer_filter(qs, zq, 2)
    sample = []
    for k in range(2):
        rows = slice(s_y, s_y + 8)
        d = fpad[H + s_z + k, Y0 + s_y : Y0 + s_y + 8]
        weight = weight_yx[rows] * weight_z[s_z + k : s_z + k + 1]
        a = d * jnp.sqrt(-row_filter(zq, k, 8, 4 - (Y0)) * weight)
        lo, hi = bounds(weight, d, solid_v[s_z + k, rows], void_v[s_z + k, rows])
        for c in range(0, lx, 128):
            sample.append((a[:, c : c + 128], lo[:, c : c + 128], hi[:, c : c + 128]))
    rough = (HIGH_LOG - LOW_LOG) / ROUGH
    totals = []
    for j in range(ROUGH):
        factor = E ** (-0.5 * (LOW_LOG + rough * j))
        parts = [jnp.minimum(jnp.maximum(a * factor, lo), hi) for a, lo, hi in sample]
        total = parts[0]
        for part in parts[1:]:
            total = total + part
        totals.append(total)
    row = to_lanes(totals, range(ROUGH))
    pl.semaphore_wait(known, len(tells))
    sum_start(0, row, gz, nz, sums_z, sums, send_r, recv_r)

    energy_of(2 * H - 1, lambda n: [n + (n // H) * inner], range(tiles - 1))
    rest = [k for k in range(H, lz - H) if not q_z <= k < q_z + 8]
    others = [t for t in range(1, tiles - 1) if not q_y // 8 <= t < q_y // 8 + 2]
    energy_of(1, lambda n: rest, range(1, tiles - 1))
    if others:
        energy_of(8, lambda n: [q_z + n], others)
    energy_of(inner // 2, lambda n: [H + 2 * n, H + 2 * n + 1], [0])
    wait_recv(*node_copies[0])
    wait_recv(*node_copies[1])

    def side_nodes(k, carry):
        nodes_at(k, ly, ly + 8)
        ninth_rows(k, [tiles - 1])
        return carry

    lax.fori_loop(0, lz, side_nodes, 0)
    energy_of((lz - 1) // 3, lambda n: [3 * n, 3 * n + 1, 3 * n + 2], [tiles - 1])

    for copy in design_copies:
        wait_recv(*copy)
    layer_filter(fpad, zbuf, lz)

    def source(layers, first, last):
        n = last - first
        f = jnp.concatenate([row_filter(zbuf, k, n, first) for k in layers], axis=0)
        high, low = split_bf16(f)
        f = dot(high, tx[...]) + dot(low, tx[...])
        cube = cube_yx[first:last]
        f = jnp.concatenate(
            [
                f[i * n : (i + 1) * n] * f[i * n : (i + 1) * n]
                * (energy[k, first:last] * (cube * cube_z[k : k + 1, :]))
                for i, k in enumerate(layers)
            ],
            axis=0,
        )
        high, low = split_bf16(f)
        f = dot(high, tx[...]) + dot(low, tx[...])
        for i, k in enumerate(layers):
            qpad[H + k, Y0 + first : Y0 + last, :] = f[i * n : (i + 1) * n]

    own_zq = {1: slice(lz, lz + H), -1: slice(H, 2 * H), 0: slice(H, H + lz)}
    own_yq = {1: slice(Y0 + ly - H, Y0 + ly), -1: slice(Y0, Y0 + H), 0: slice(Y0, Y0 + ly)}
    source_copies = [
        (directions[n], halo(qpad, (own_zq, own_yq), qpad, send2, recv2, n)) for n in range(8)
    ]
    middle = range(H, lz - H)
    source(range(H), 0, ly)
    start(*source_copies[1])
    start(*source_copies[6])
    start(*source_copies[7])
    source(middle, 0, 8)
    source(middle, ly - 8, ly)
    wait_recv(*node_copies[2])
    nodes_at(lz, 0, ly + 8)
    ninth_rows(lz, range(tiles))
    for tile in range(tiles):
        element_rows(lz - 1, tile)
    source(range(lz - H, lz), 0, ly)
    for n in (2, 3, 4, 5, 0):
        start(*source_copies[n])
    source(range(H, lz // 2), 8, ly - 8)
    source(range(lz // 2, lz - H), 8, ly - 8)

    def bounds_of(k, carry):
        low_v[k], high_v[k] = bounds(weight_of(k), fpad[H + k, Y0 : Y0 + ly, :], solid_v[k], void_v[k])
        return carry

    lax.fori_loop(0, lz, bounds_of, 0)

    row = sum_finish(0, nz, sums, recv_r)
    sum_start(1, row, gy, ny, sums_y, sums, send_r, recv_r)

    def finish_sens(k, first, last):
        at = slice(first, last)
        s = row_filter(zbuf, k, last - first, first)
        sens_v[k, at] = s
        b = fpad[H + k, Y0 + first : Y0 + last] * jnp.sqrt(-s * (inv_yx[at] * inv_z[k : k + 1]))
        amount[k, at] = b
        scaled[k, at] = b * (weight_yx[at] * weight_z[k : k + 1])

    for copy in source_copies:
        wait_recv(*copy)
    layer_filter(qpad, zbuf, lz)
    for k in range(lz):
        finish_sens(k, 0, ly)
    stores = [
        pltpu.make_async_copy(src, dst, store_sem.at[n])
        for n, (src, dst) in enumerate(((sens_v, fields.at[0]), (amount, fields.at[1])))
    ]
    for store in stores:
        store.start()

    row = sum_finish(1, ny, sums, recv_r)
    part = target * (16.0 / (lz * ly))
    index = count_above(row, lane < ROUGH, part)
    below, above = entry(row, index - 1.0), entry(row, index)
    step = jnp.where((index > 0.0) & (index < ROUGH), (below - part) / (below - above), 0.0)
    guess = (GRID // ROUGH) * (index - 1.0 + step)
    first = jnp.clip(jnp.floor(guess) - (WINDOW // 2 - 1), 0.0, GRID + 1.0 - WINDOW)
    low = LOW_LOG + FINE * first
    window_factor = jnp.exp(-0.5 * low)
    factors = [E ** (-0.5 * FINE * j) for j in range(WINDOW)]
    row = volumes(scaled, low_v, high_v, window_factor, factors, range(WINDOW))
    sum_start(2, row, gz, nz, sums_z, sums, send_r, recv_r)
    row = sum_finish(2, nz, sums, recv_r)
    sum_start(3, row, gy, ny, sums_y, sums, send_r, recv_r)
    row = sum_finish(3, ny, sums, recv_r)
    index = count_above(row, lane < WINDOW, target)
    hit = (index > 0.0) & (index < WINDOW)
    found[0] = jnp.sum(jnp.where(hit, 1.0, 0.0)).astype(jnp.int32)
    index = index - 1.0
    final = secant(low + FINE * index, entry(row, index), entry(row, index + 1.0), target)
    factor = jnp.exp(-0.5 * final)

    factor_out[0] = jnp.sum(factor)

    for copy in node_copies + design_copies + source_copies:
        wait_send(*copy)
    for n, size in enumerate((nz, ny, nz, ny)):
        sum_sent(n, size, sums, send_r)
    for store in stores:
        store.wait()


def exact_kernel(
    nz, ny,
    design, void, solid, fields,
    factor_out,
    design_v, void_v, solid_v, amount, low_v, high_v, weight_yx, weight_z, sums,
    load_sem, send_r, recv_r,
):
    lz, ly, lx = design.shape
    gz, gy = lax.axis_index("gz"), lax.axis_index("gy")

    def sums_z(d):
        return (lax.rem(gz + d, nz), gy)

    def sums_y(d):
        return (gz, lax.rem(gy + d, ny))

    loads = [
        pltpu.make_async_copy(src, dst, load_sem.at[n])
        for n, (src, dst) in enumerate(
            ((design, design_v), (void, void_v), (solid, solid_v), (fields.at[0], amount))
        )
    ]
    for load in loads:
        load.start()
    barrier = pltpu.get_barrier_semaphore()
    partners = [sums_z(d) for d in range(1, nz)] + [sums_y(d) for d in range(1, ny)]
    for partner in partners:
        pl.semaphore_signal(barrier, inc=1, device_id=partner, device_id_type=MESH)
    weights(weight_yx, weight_z, gy, ny, gz, nz)
    for load in loads:
        load.wait()

    def weight_of(k):
        return weight_yx[...] * weight_z[pl.ds(k, 1), :]

    def prepare(k, carry):
        d = design_v[k]
        low_v[k], high_v[k] = bounds(weight_of(k), d, solid_v[k], void_v[k])
        amount[k] = d * jnp.sqrt(-amount[k] * weight_of(k))
        return carry

    lax.fori_loop(0, lz, prepare, 0)
    pl.semaphore_wait(barrier, len(partners))

    def everywhere(n, row):
        sum_start(n, row, gz, nz, sums_z, sums, send_r, recv_r)
        row = sum_finish(n, nz, sums, recv_r)
        sum_start(n + 1, row, gy, ny, sums_y, sums, send_r, recv_r)
        return sum_finish(n + 1, ny, sums, recv_r)

    target = total_target(lz, ly, lx, nz, ny)
    lane = iota((1, 128), 1)
    inside = (lane >= 1) & (lane < SPLIT)
    wide = FINE * SPLIT
    factors = [E ** (-0.5 * (LOW_LOG + wide * j)) for j in range(SPLIT + 1)]
    row = everywhere(0, volumes(amount, low_v, high_v, None, factors, range(SPLIT + 1)))
    index = count_above(row, inside, target)
    low = LOW_LOG + wide * index
    ends = (entry(row, index), entry(row, index + 1.0))
    factors = [E ** (-0.5 * FINE * j) for j in range(1, SPLIT)]
    row = everywhere(
        2, volumes(amount, low_v, high_v, jnp.exp(-0.5 * low), factors, range(1, SPLIT))
    )
    row = jnp.where(lane == 0, ends[0], jnp.where(lane == SPLIT, ends[1], row))
    index = count_above(row, inside, target)
    final = secant(low + FINE * index, entry(row, index), entry(row, index + 1.0), target)
    factor = jnp.exp(-0.5 * final)

    factor_out[0] = jnp.sum(factor)
    for n, size in enumerate((nz, ny, nz, ny)):
        sum_sent(n, size, sums, send_r)


def written_kernel(
    factor, design, void, solid, fields, new_out, sens_out, new_v, store_sem, sens_sem
):
    parts, step = new_v.shape[0], new_v.shape[1]
    copy_sens = pltpu.make_async_copy(fields.at[0], sens_out, sens_sem)
    copy_sens.start()
    stores = []
    for n in range(parts):
        at = slice(n * step, (n + 1) * step)
        new_v[n] = finished(fields[1, at], factor[0], design[at], solid[at], void[at])
        stores.append(pltpu.make_async_copy(new_v.at[n], new_out.at[at], store_sem.at[n]))
        stores[n].start()
    for store in stores:
        store.wait()
    copy_sens.wait()


def per_device(displacement, design, void_mask, solid_mask, stiffness):
    nz, ny = lax.axis_size("gz"), lax.axis_size("gy")
    lz, ly, lx = design.shape
    brick = jax.ShapeDtypeStruct(design.shape, F32)
    padded = (lz + 2 * H, ly + 16, lx)
    anywhere = pl.BlockSpec(memory_space=pltpu.HBM)
    sem = pltpu.SemaphoreType
    nodes = pltpu.VMEM((3, lz + 1, ly + 8, lx), F32)
    line, table = pltpu.VMEM((lz, lx), F32), pltpu.VMEM((ly, lx), F32)
    bricks = [pltpu.VMEM(design.shape, F32)] * 4
    masks = [pltpu.VMEM(design.shape, jnp.int32)] * 2
    sums = pltpu.VMEM((4, max(nz, ny), 1, 128), F32)
    scalar = pl.BlockSpec(memory_space=pltpu.SMEM)
    one = jax.ShapeDtypeStruct((1,), F32)
    fields, found, factor = pl.pallas_call(
        functools.partial(kernel, nz, ny),
        out_shape=(
            jax.ShapeDtypeStruct((2, *design.shape), F32), jax.ShapeDtypeStruct((1,), jnp.int32), one
        ),
        in_specs=[anywhere] * 5,
        out_specs=(anywhere, scalar, scalar),
        scratch_shapes=[
            nodes,
            pltpu.VMEM(padded, F32),
            pltpu.VMEM(padded, F32),
            pltpu.VMEM((lz, ly + 16, lx), F32),
            *masks,
            *bricks,
            pltpu.VMEM(design.shape, F32), pltpu.VMEM(design.shape, F32),
            nodes, nodes, nodes,
            pltpu.VMEM((lz + 1, ly // 8, 8, lx), F32),
            pltpu.VMEM((lx, lx), BF16),
            pltpu.VMEM((24, 24), F32),
            pltpu.VMEM((192, 224), BF16),
            table, table, table, line, line, line,
            pltpu.VMEM((8, ly, lx), F32),
            pltpu.VMEM((8, 16, lx), F32),
            pltpu.VMEM((2, 16, lx), F32),
            sums,
            sem.DMA((5,)), sem.DMA((2,)),
            sem.DMA((11,)), sem.DMA((11,)), sem.DMA((8,)), sem.DMA((8,)),
            sem.DMA((4,)), sem.DMA((4,)), sem.REGULAR,
        ],
        compiler_params=pltpu.CompilerParams(
            collective_id=0, has_side_effects=True, vmem_limit_bytes=60 * 1024 * 1024
        ),
    )(displacement, design, void_mask, solid_mask, stiffness)

    def exact(factor, design, void_mask, solid_mask, fields):
        return pl.pallas_call(
            functools.partial(exact_kernel, nz, ny),
            out_shape=one,
            in_specs=[anywhere] * 4,
            out_specs=scalar,
            scratch_shapes=[
                pltpu.VMEM(design.shape, F32), *masks,
                *bricks[:3],
                table, line, sums,
                sem.DMA((4,)), sem.DMA((4,)), sem.DMA((4,)),
            ],
            compiler_params=pltpu.CompilerParams(
                collective_id=1, has_side_effects=True, vmem_limit_bytes=60 * 1024 * 1024
            ),
        )(design, void_mask, solid_mask, fields)

    factor = lax.switch(
        found[0], (exact, lambda factor, *rest: factor),
        factor, design, void_mask, solid_mask, fields,
    )
    parts = 4
    return pl.pallas_call(
        written_kernel,
        out_shape=(brick, brick),
        in_specs=[scalar] + [pl.BlockSpec(memory_space=pltpu.VMEM)] * 4,
        out_specs=(anywhere, anywhere),
        scratch_shapes=[
            pltpu.VMEM((parts, lz // parts, ly, lx), F32), sem.DMA((parts,)), sem.DMA
        ],
        compiler_params=pltpu.CompilerParams(vmem_limit_bytes=16 * 1024 * 1024),
    )(factor, design, void_mask, solid_mask, fields)


def solution(mesh):
    return jax.shard_map(
        per_device,
        mesh=mesh,
        in_specs=(
            P(None, "gz", "gy", None),
            P("gz", "gy", None),
            P("gz", "gy", None),
            P("gz", "gy", None),
            P(),
        ),
        out_specs=(P("gz", "gy", None), P("gz", "gy", None)),
        check_vma=False,
    )
```

```python
import functools

import jax
import jax.numpy as jnp
from jax import lax
from jax.experimental import pallas as pl
from jax.experimental.pallas import tpu as pltpu
from jax.sharding import PartitionSpec as P

MESH = pl.DeviceIdType.MESH
NEAR_Z = [(d, 0) for d in (2, -2, 3, -3, 4, -4, 5, -5, 6, -6)]
NEAR_Y = [(0, d) for d in (2, -2, 8, 7, 9, 6, 10)]
F32 = jnp.float32
BF16 = jnp.bfloat16

TAPS = (1.0, 2.0, 3.0, 4.0, 3.0, 2.0, 1.0)
LOW_LOG = -25.0
HIGH_LOG = 25.0
MOVE_LIMIT = 0.2
VOLUME_FRACTION = 0.5
PENALTY = 3.0
SPLIT = 16
GRID = SPLIT * SPLIT
FINE = (HIGH_LOG - LOW_LOG) / GRID
ROUGH = 64
WINDOW = 6
E = 2.718281828459045

H = 3
Y0 = 8


def line_total(p, extent):
    low = jnp.maximum(3 - p, 0)
    high = jnp.maximum(p - (extent - 4), 0)
    missing = low * (low + 1) + high * (high + 1)
    return 16.0 - 0.5 * missing.astype(F32)


def line_spread(p, extent):
    total = None
    for d in range(-3, 4):
        near = p + d
        term = jnp.where(
            (near >= 0) & (near < extent), TAPS[d + 3] / line_total(near, extent), 0.0
        )
        total = term if total is None else total + term
    return total


def iota(shape, dim):
    return lax.broadcasted_iota(jnp.int32, shape, dim)


def split_bf16(x):
    high = x.astype(BF16)
    low = (x - high.astype(F32)).astype(BF16)
    return high, low


def dot(a, b):
    return jnp.dot(a, b, preferred_element_type=F32)


def row_filter(ref, layer, rows, first=0):
    at = Y0 - H + first
    c = [ref[layer, at + t : at + t + rows, :] for t in range(7)]
    return (c[0] + c[6]) + 2.0 * (c[1] + c[5]) + 3.0 * (c[2] + c[4]) + 4.0 * c[3]


def layer_filter(src, dst, layers, first=0, rows=None, shift=0, to=0):
    for r in range(0, src.shape[1], 8) if rows is None else rows:
        for c in range(0, src.shape[2], 128):
            col = slice(c, c + 128)
            f = [src[first + k, shift + r : shift + r + 8, col] for k in range(layers + 2 * H)]
            f = [a + b for a, b in zip(f, f[1:])]
            f = [a + b for a, b in zip(f, f[2:])]
            f = [a + b for a, b in zip(f, f[1:])]
            f = [a + b for a, b in zip(f, f[2:])]
            for k in range(layers):
                dst[to + k, r : r + 8, col] = f[k]


def sum_start(n, row, at, size, to, sums, send, recv):
    sums[n, at] = row
    copies = [
        pltpu.make_async_remote_copy(
            src_ref=sums.at[n, at], dst_ref=sums.at[n, at],
            send_sem=send.at[n], recv_sem=recv.at[n],
            device_id=to(d), device_id_type=MESH,
        )
        for d in range(1, size)
    ]
    for copy in copies:
        copy.start()


def sum_finish(n, size, sums, recv):
    everyone = sums.at[n, 0 : size - 1]
    pltpu.make_async_copy(everyone, everyone, recv.at[n]).wait()
    return jnp.sum(sums[n, 0:size], axis=0)


def sum_sent(n, size, sums, send):
    everyone = sums.at[n, 0 : size - 1]
    pltpu.make_async_copy(everyone, everyone, send.at[n]).wait()


def to_lanes(rows, lanes):
    count = -(-(max(lanes) + 1) // 8) * 8
    sub = iota((count, 128), 0)
    stacked = jnp.zeros((count, 128), F32)
    for row, j in zip(rows, lanes):
        stacked = jnp.where(sub == j, jnp.sum(row, axis=0, keepdims=True), stacked)
    line = jnp.sum(stacked, axis=1, keepdims=True)
    return jnp.sum(jnp.where(sub == iota((count, 128), 1), line, 0.0), axis=0, keepdims=True)


def volumes(amount, low_v, high_v, scale, factors, lanes):
    lz, ly, lx = amount.shape

    def layer(k, totals):
        totals = list(totals)
        for r in range(0, ly, 8):
            for c in range(0, lx, 128):
                at = (k, slice(r, r + 8), slice(c, c + 128))
                a, low, high = amount[at], low_v[at], high_v[at]
                if scale is not None:
                    a = a * scale
                for j, factor in enumerate(factors):
                    totals[j] = totals[j] + jnp.minimum(jnp.maximum(a * factor, low), high)
        return tuple(totals)

    totals = lax.fori_loop(0, lz, layer, tuple(jnp.zeros((8, 128), F32) for _ in factors))
    return to_lanes(totals, lanes)


def count_above(row, inside, target):
    return jnp.sum(jnp.where(inside & (row > target), 1.0, 0.0), axis=1, keepdims=True)


def entry(row, index):
    at = iota(row.shape, 1).astype(F32)
    return jnp.sum(jnp.where(at == index, row, 0.0), axis=1, keepdims=True)


def secant(low, low_volume, high_volume, target):
    return low + FINE * ((low_volume - target) / (low_volume - high_volume))


def weights(ref, z_ref, gy, ny, gz, nz):
    ly, lx = ref.shape
    lz = z_ref.shape[0]
    ref[...] = line_spread(iota((ly, lx), 0) + gy * ly, ly * ny) * line_spread(iota((ly, lx), 1), lx)
    z_ref[...] = line_spread(iota((lz, lx), 0) + gz * lz, lz * nz)


def bounds(weight, d, solid, void):
    low = jnp.maximum(d - MOVE_LIMIT, 0.0) * weight
    high = jnp.minimum(d + MOVE_LIMIT, 1.0) * weight
    is_solid, is_void = solid == 1, void == 1
    low = jnp.where(is_solid, weight, jnp.where(is_void, 0.0, low))
    high = jnp.where(is_solid, weight, jnp.where(is_void, 0.0, high))
    return low, high


def finished(b, factor, d, solid, void):
    moved = jnp.minimum(
        jnp.maximum(b * factor, jnp.maximum(d - MOVE_LIMIT, 0.0)), jnp.minimum(d + MOVE_LIMIT, 1.0)
    )
    return jnp.where(solid == 1, 1.0, jnp.where(void == 1, 0.0, moved))


def total_target(lz, ly, lx, nz, ny):
    return VOLUME_FRACTION * (lz * nz) * (ly * ny) * lx


def kernel(
    nz, ny,
    disp, design, void, solid, stiff,
    fields, found, factor_out,
    dpad, fpad, qpad, zbuf, void_v, solid_v, energy, amount, scaled, low_v, high_v, sens_v,
    shifted, double, double_s, edge, tx, stiff_v, k_rows, cube_yx, weight_yx, inv_yx, cube_z, weight_z, inv_z, zs, qs, zq, sums,
    load_sem, store_sem, send1, recv1, send2, recv2, send_r, recv_r, known,
):
    lz, ly, lx = design.shape
    gz, gy = lax.axis_index("gz"), lax.axis_index("gy")
    has = {
        (1, 0): gz < nz - 1, (-1, 0): gz > 0, (0, 1): gy < ny - 1, (0, -1): gy > 0,
    }
    for dz in (-1, 1):
        for dy in (-1, 1):
            has[dz, dy] = has[dz, 0] & has[0, dy]

    def peer(dz, dy):
        return (lax.rem(gz + dz % nz, nz), lax.rem(gy + dy % ny, ny))

    directions = [(1, 0), (-1, 0), (0, 1), (0, -1), (1, 1), (1, -1), (-1, 1), (-1, -1)]

    own_f = fpad.at[H : H + lz, Y0 : Y0 + ly, :]
    loads = [
        pltpu.make_async_copy(disp, dpad.at[:, 0:lz, 0:ly, :], load_sem.at[0]),
        pltpu.make_async_copy(design, own_f, load_sem.at[1]),
        pltpu.make_async_copy(void, void_v, load_sem.at[2]),
        pltpu.make_async_copy(solid, solid_v, load_sem.at[3]),
        pltpu.make_async_copy(stiff, stiff_v, load_sem.at[4]),
    ]
    for copy in loads:
        copy.start()

    barrier = pltpu.get_barrier_semaphore()
    ways = directions + NEAR_Z + NEAR_Y
    for way in ways:
        pl.semaphore_signal(barrier, inc=1, device_id=peer(*way), device_id_type=MESH)

    tells = ((2, 0), (-2, 0), (0, 2), (0, -2))

    for pad in (fpad, qpad):
        @pl.when(gz == 0)
        def _():
            pad[0:H] = jnp.zeros_like(pad[0:H])

        @pl.when(gz == nz - 1)
        def _():
            pad[lz + H :] = jnp.zeros_like(pad[lz + H :])

        @pl.when(gy == 0)
        def _():
            pad[:, 0:Y0] = jnp.zeros_like(pad[:, 0:Y0])

        @pl.when(gy == ny - 1)
        def _():
            pad[:, Y0 + ly :] = jnp.zeros_like(pad[:, Y0 + ly :])

    @pl.when(gz == nz - 1)
    def _():
        dpad[:, lz] = jnp.zeros_like(dpad[:, lz])

    @pl.when(gy == ny - 1)
    def _():
        dpad[:, :, ly:] = jnp.zeros_like(dpad[:, :, ly:])

    pl.semaphore_wait(barrier, len(ways))
    for way in tells:
        pl.semaphore_signal(known, inc=1, device_id=peer(*way), device_id_type=MESH)

    near_z = {1: slice(lz - H, lz), -1: slice(0, H), 0: slice(0, lz)}
    near_y = {1: slice(ly - H, ly), -1: slice(0, H), 0: slice(0, ly)}
    far_z = {1: slice(0, H), -1: slice(H + lz, lz + 2 * H), 0: slice(H, H + lz)}
    far_y = {1: slice(Y0 - H, Y0), -1: slice(Y0 + ly, Y0 + ly + H), 0: slice(Y0, Y0 + ly)}

    def halo(src, src_at, pad, send, recv, n):
        dz, dy = directions[n]
        return pltpu.make_async_remote_copy(
            src_ref=src.at[src_at[0][dz], src_at[1][dy], :],
            dst_ref=pad.at[far_z[dz], far_y[dy], :],
            send_sem=send.at[n], recv_sem=recv.at[n],
            device_id=peer(dz, dy), device_id_type=MESH,
        )

    def start(direction, copy):
        @pl.when(has[direction])
        def _():
            copy.start()

    def wait_recv(direction, copy):
        @pl.when(has[-direction[0], -direction[1]])
        def _():
            copy.wait_recv()

    def wait_send(direction, copy):
        @pl.when(has[direction])
        def _():
            copy.wait_send()

    def nodes(n, direction, layers, rows, to_layers, to_rows):
        return direction, pltpu.make_async_remote_copy(
            src_ref=disp.at[:, layers, rows, :],
            dst_ref=dpad.at[:, to_layers, to_rows, :],
            send_sem=send1.at[8 + n], recv_sem=recv1.at[8 + n],
            device_id=peer(*direction), device_id_type=MESH,
        )

    first_z, top_z = slice(0, 1), slice(lz, lz + 1)
    first_y, top_y = slice(0, 1), slice(ly, ly + 1)
    own_z, own_y = slice(0, lz), slice(0, ly)
    node_copies = [
        nodes(0, (0, -1), own_z, first_y, own_z, top_y),
        nodes(1, (-1, -1), first_z, first_y, top_z, top_y),
        nodes(2, (-1, 0), first_z, own_y, top_z, own_y),
    ]
    design_copies = [
        (directions[n], halo(design, (near_z, near_y), fpad, send1, recv1, n)) for n in range(8)
    ]
    for n in (4, 5, 6, 7, 2, 3):
        start(*design_copies[n])
    start(*node_copies[1])
    start(*node_copies[0])
    start(*design_copies[0])
    start(*design_copies[1])
    start(*node_copies[2])

    across = jnp.abs(iota((lx, lx), 0) - iota((lx, lx), 1))
    tx[...] = jnp.maximum(4 - across, 0).astype(F32).astype(BF16)
    full_z, full_y = lz * nz, ly * ny
    row_at = iota((ly, lx), 0) + gy * ly
    col_at = iota((ly, lx), 1)
    inv = 1.0 / (line_total(row_at, full_y) * line_total(col_at, lx))
    cube_yx[...] = (-PENALTY) * inv * inv * inv
    layer_at = iota((lz, lx), 0) + gz * lz
    inv = 1.0 / line_total(layer_at, full_z)
    cube_z[...] = inv * inv * inv
    weights(weight_yx, weight_z, gy, ny, gz, nz)
    inv_yx[...] = 1.0 / weight_yx[...]
    inv_z[...] = 1.0 / weight_z[...]

    size, width = 24 * 8, 12 * 8 + 16
    pick = (lax.shift_right_logical(iota((size, 24), 0), 3) == iota((size, 24), 1)).astype(F32).astype(BF16)
    entry_at, col = iota((24, 2 * width), 0), iota((24, 2 * width), 1)

    def part_col(col):
        return jnp.where(col >= width, col - width, col)

    col = part_col(col)
    corner = sum((entry_at >= 6 * n).astype(jnp.int32) for n in (1, 2, 3))
    step_y = corner & 1
    rest = entry_at - 6 * corner
    group = jnp.where(corner >= 2, 6, 0) + rest
    tail = col - 12 * 8
    tail_rest = tail & 7
    tail_group = jnp.where(tail_rest < 6, jnp.where(tail >= 8, 6, 0) + tail_rest, -1)
    col_group = jnp.where(col < 12 * 8, lax.shift_right_logical(col, 3), tail_group)
    places = [
        ((group == col_group) & (step_y == n)).astype(F32).astype(BF16) for n in range(2)
    ]
    col = part_col(iota((size, 2 * width), 1))
    up = jnp.where(col < 12 * 8, col & 7, 8) - (iota((size, 2 * width), 0) & 7)
    halves = []
    loads[4].wait()
    for part in split_bf16(stiff_v[...]):
        rows = dot(pick, part).astype(BF16)
        same, next_row = dot(rows, places[0]), dot(rows, places[1])
        halves.append(jnp.where(up == 0, same, jnp.where(up == 1, next_row, 0.0)))
    is_low = iota((size, 2 * width), 1) >= width
    k_rows[...] = jnp.where(is_low, halves[1], halves[0]).astype(BF16)

    def nodes_at(k, first, last):
        at = slice(first, last)
        last_col = iota((last - first, lx), 1) == lx - 1
        for q in range(3):
            u = dpad[q, k, at]
            v = jnp.where(last_col, 0.0, pltpu.roll(u, lx - 1, 1))
            shifted[q, k, at] = v
            double[q, k, at] = 2.0 * u - u.astype(BF16).astype(F32)
            double_s[q, k, at] = 2.0 * v - v.astype(BF16).astype(F32)

    def ninth_rows(k, tiles_of):
        for tile in tiles_of:
            at = slice(8 * tile + 8, 8 * tile + 9)
            rows = [ref[q, k, at, :] for ref in (dpad, shifted) for q in range(3)]
            edge[k, tile] = jnp.concatenate(rows + [jnp.zeros((2, lx), F32)], axis=0)

    def element_rows(k, tile):
        at = slice(8 * tile, 8 * tile + 8)
        u = [ref[q, k + a, at, :] for a in range(2) for ref in (dpad, shifted) for q in range(3)]
        u += [edge[k + a, tile] for a in range(2)]
        high = jnp.concatenate(u, axis=0).astype(BF16)
        forces = dot(k_rows[...], jnp.concatenate([high, high], axis=0))
        total = None
        for n in range(24):
            a, b, c, q = n // 12, n // 6 % 2, n // 3 % 2, n % 3
            ref = double_s if c else double
            term = ref[q, k + a, 8 * tile + b : 8 * tile + b + 8, :] * forces[8 * n : 8 * n + 8]
            total = term if total is None else total + term
        energy[k, at, :] = jnp.maximum(total, 0.0)

    tiles = ly // 8

    def energy_of(count, layer_of, tiles_of):
        def body(n, carry):
            for k in layer_of(n):
                for tile in tiles_of:
                    element_rows(k, tile)
            return carry

        lax.fori_loop(0, count, body, 0)

    inner = lz - 2 * H
    sums_z, sums_y = lambda d: peer(d, 0), lambda d: peer(0, d)
    target = total_target(lz, ly, lx, nz, ny)
    lane = iota((1, 128), 1)

    def weight_of(k):
        return weight_yx[...] * weight_z[pl.ds(k, 1), :]

    s_z, s_y = lz // 2 - 1, ly // 2 - 4
    q_z, q_y = s_z - H, s_y - 4
    for load in loads[:4]:
        load.wait()

    def own_nodes(k, carry):
        nodes_at(k, 0, ly)
        ninth_rows(k, range(tiles - 1))
        return carry

    lax.fori_loop(0, lz, own_nodes, 0)
    energy_of(4, lambda n: [q_z + 2 * n, q_z + 2 * n + 1], [q_y // 8, q_y // 8 + 1])
    layer_filter(fpad, zs, 8, q_z, range(0, ly, 8), Y0)
    f = jnp.concatenate([row_filter(zs, k, 16, q_y - Y0) for k in range(8)], axis=0)
    high, low = split_bf16(f)
    f = dot(high, tx[...]) + dot(low, tx[...])
    f = jnp.concatenate(
        [
            f[16 * k : 16 * k + 16] * f[16 * k : 16 * k + 16]
            * (energy[q_z + k, q_y : q_y + 16] * (cube_yx[q_y : q_y + 16] * cube_z[q_z + k : q_z + k + 1]))
            for k in range(8)
        ],
        axis=0,
    )
    high, low = split_bf16(f)
    f = dot(high, tx[...]) + dot(low, tx[...])
    for k in range(8):
        qs[k] = f[16 * k : 16 * k + 16]
    layer_filter(qs, zq, 2)
    sample = []
    for k in range(2):
        rows = slice(s_y, s_y + 8)
        d = fpad[H + s_z + k, Y0 + s_y : Y0 + s_y + 8]
        weight = weight_yx[rows] * weight_z[s_z + k : s_z + k + 1]
        a = d * jnp.sqrt(-row_filter(zq, k, 8, 4 - (Y0)) * weight)
        lo, hi = bounds(weight, d, solid_v[s_z + k, rows], void_v[s_z + k, rows])
        for c in range(0, lx, 128):
            sample.append((a[:, c : c + 128], lo[:, c : c + 128], hi[:, c : c + 128]))
    rough = (HIGH_LOG - LOW_LOG) / ROUGH
    totals = []
    for j in range(ROUGH):
        factor = E ** (-0.5 * (LOW_LOG + rough * j))
        parts = [jnp.minimum(jnp.maximum(a * factor, lo), hi) for a, lo, hi in sample]
        total = parts[0]
        for part in parts[1:]:
            total = total + part
        totals.append(total)
    row = to_lanes(totals, range(ROUGH))
    pl.semaphore_wait(known, len(tells))
    sum_start(0, row, gz, nz, sums_z, sums, send_r, recv_r)

    energy_of(2 * H - 1, lambda n: [n + (n // H) * inner], range(tiles - 1))
    rest = [k for k in range(H, lz - H) if not q_z <= k < q_z + 8]
    others = [t for t in range(1, tiles - 1) if not q_y // 8 <= t < q_y // 8 + 2]
    energy_of(1, lambda n: rest, range(1, tiles - 1))
    if others:
        energy_of(8, lambda n: [q_z + n], others)
    energy_of(inner // 2, lambda n: [H + 2 * n, H + 2 * n + 1], [0])
    wait_recv(*node_copies[0])
    wait_recv(*node_copies[1])

    def side_nodes(k, carry):
        nodes_at(k, ly, ly + 8)
        ninth_rows(k, [tiles - 1])
        return carry

    lax.fori_loop(0, lz, side_nodes, 0)
    energy_of((lz - 1) // 3, lambda n: [3 * n, 3 * n + 1, 3 * n + 2], [tiles - 1])

    for copy in design_copies:
        wait_recv(*copy)
    layer_filter(fpad, zbuf, lz)

    def source(layers, first, last):
        n = last - first
        f = jnp.concatenate([row_filter(zbuf, k, n, first) for k in layers], axis=0)
        high, low = split_bf16(f)
        f = dot(high, tx[...]) + dot(low, tx[...])
        cube = cube_yx[first:last]
        f = jnp.concatenate(
            [
                f[i * n : (i + 1) * n] * f[i * n : (i + 1) * n]
                * (energy[k, first:last] * (cube * cube_z[k : k + 1, :]))
                for i, k in enumerate(layers)
            ],
            axis=0,
        )
        high, low = split_bf16(f)
        f = dot(high, tx[...]) + dot(low, tx[...])
        for i, k in enumerate(layers):
            qpad[H + k, Y0 + first : Y0 + last, :] = f[i * n : (i + 1) * n]

    own_zq = {1: slice(lz, lz + H), -1: slice(H, 2 * H), 0: slice(H, H + lz)}
    own_yq = {1: slice(Y0 + ly - H, Y0 + ly), -1: slice(Y0, Y0 + H), 0: slice(Y0, Y0 + ly)}
    source_copies = [
        (directions[n], halo(qpad, (own_zq, own_yq), qpad, send2, recv2, n)) for n in range(8)
    ]
    middle = range(H, lz - H)
    source(range(H), 0, ly)
    start(*source_copies[1])
    start(*source_copies[6])
    start(*source_copies[7])
    source(middle, 0, 8)
    source(middle, ly - 8, ly)
    wait_recv(*node_copies[2])
    nodes_at(lz, 0, ly + 8)
    ninth_rows(lz, range(tiles))
    for tile in range(tiles):
        element_rows(lz - 1, tile)
    source(range(lz - H, lz), 0, ly)
    for n in (2, 3, 4, 5, 0):
        start(*source_copies[n])
    source(range(H, lz // 2), 8, ly - 8)
    source(range(lz // 2, lz - H), 8, ly - 8)

    def bounds_of(k, carry):
        low_v[k], high_v[k] = bounds(weight_of(k), fpad[H + k, Y0 : Y0 + ly, :], solid_v[k], void_v[k])
        return carry

    lax.fori_loop(0, lz, bounds_of, 0)

    row = sum_finish(0, nz, sums, recv_r)
    sum_start(1, row, gy, ny, sums_y, sums, send_r, recv_r)

    def finish_sens(k, first, last):
        at = slice(first, last)
        s = row_filter(zbuf, k, last - first, first)
        sens_v[k, at] = s
        b = fpad[H + k, Y0 + first : Y0 + last] * jnp.sqrt(-s * (inv_yx[at] * inv_z[k : k + 1]))
        amount[k, at] = b
        scaled[k, at] = b * (weight_yx[at] * weight_z[k : k + 1])

    every = range(0, ly + 16, 8)
    layer_filter(qpad, zbuf, inner, H, range(Y0, Y0 + ly, 8), 0, H)
    for k in middle:
        finish_sens(k, 8, ly - 8)
    for copy in source_copies:
        wait_recv(*copy)
    layer_filter(qpad, zbuf, H, 0, every)
    layer_filter(qpad, zbuf, H, lz - H, every, 0, lz - H)
    layer_filter(qpad, zbuf, inner, H, (0, Y0 + ly), 0, H)
    for k in range(lz):
        if k in middle:
            finish_sens(k, 0, 8)
            finish_sens(k, ly - 8, ly)
        else:
            finish_sens(k, 0, ly)
    stores = [
        pltpu.make_async_copy(src, dst, store_sem.at[n])
        for n, (src, dst) in enumerate(((sens_v, fields.at[0]), (amount, fields.at[1])))
    ]
    for store in stores:
        store.start()

    row = sum_finish(1, ny, sums, recv_r)
    part = target * (16.0 / (lz * ly))
    index = count_above(row, lane < ROUGH, part)
    below, above = entry(row, index - 1.0), entry(row, index)
    step = jnp.where((index > 0.0) & (index < ROUGH), (below - part) / (below - above), 0.0)
    guess = (GRID // ROUGH) * (index - 1.0 + step)
    first = jnp.clip(jnp.floor(guess) - (WINDOW // 2 - 1), 0.0, GRID + 1.0 - WINDOW)
    low = LOW_LOG + FINE * first
    window_factor = jnp.exp(-0.5 * low)
    factors = [E ** (-0.5 * FINE * j) for j in range(WINDOW)]
    row = volumes(scaled, low_v, high_v, window_factor, factors, range(WINDOW))
    sum_start(2, row, gz, nz, sums_z, sums, send_r, recv_r)
    row = sum_finish(2, nz, sums, recv_r)
    sum_start(3, row, gy, ny, sums_y, sums, send_r, recv_r)
    row = sum_finish(3, ny, sums, recv_r)
    index = count_above(row, lane < WINDOW, target)
    hit = (index > 0.0) & (index < WINDOW)
    found[0] = jnp.sum(jnp.where(hit, 1.0, 0.0)).astype(jnp.int32)
    index = index - 1.0
    final = secant(low + FINE * index, entry(row, index), entry(row, index + 1.0), target)
    factor = jnp.exp(-0.5 * final)

    factor_out[0] = jnp.sum(factor)

    for copy in node_copies + design_copies + source_copies:
        wait_send(*copy)
    for n, size in enumerate((nz, ny, nz, ny)):
        sum_sent(n, size, sums, send_r)
    for store in stores:
        store.wait()


def exact_kernel(
    nz, ny,
    design, void, solid, fields,
    factor_out,
    design_v, void_v, solid_v, amount, low_v, high_v, weight_yx, weight_z, sums,
    load_sem, send_r, recv_r,
):
    lz, ly, lx = design.shape
    gz, gy = lax.axis_index("gz"), lax.axis_index("gy")

    def sums_z(d):
        return (lax.rem(gz + d, nz), gy)

    def sums_y(d):
        return (gz, lax.rem(gy + d, ny))

    loads = [
        pltpu.make_async_copy(src, dst, load_sem.at[n])
        for n, (src, dst) in enumerate(
            ((design, design_v), (void, void_v), (solid, solid_v), (fields.at[0], amount))
        )
    ]
    for load in loads:
        load.start()
    barrier = pltpu.get_barrier_semaphore()
    partners = [sums_z(d) for d in range(1, nz)] + [sums_y(d) for d in range(1, ny)]
    for partner in partners:
        pl.semaphore_signal(barrier, inc=1, device_id=partner, device_id_type=MESH)
    weights(weight_yx, weight_z, gy, ny, gz, nz)
    for load in loads:
        load.wait()

    def weight_of(k):
        return weight_yx[...] * weight_z[pl.ds(k, 1), :]

    def prepare(k, carry):
        d = design_v[k]
        low_v[k], high_v[k] = bounds(weight_of(k), d, solid_v[k], void_v[k])
        amount[k] = d * jnp.sqrt(-amount[k] * weight_of(k))
        return carry

    lax.fori_loop(0, lz, prepare, 0)
    pl.semaphore_wait(barrier, len(partners))

    def everywhere(n, row):
        sum_start(n, row, gz, nz, sums_z, sums, send_r, recv_r)
        row = sum_finish(n, nz, sums, recv_r)
        sum_start(n + 1, row, gy, ny, sums_y, sums, send_r, recv_r)
        return sum_finish(n + 1, ny, sums, recv_r)

    target = total_target(lz, ly, lx, nz, ny)
    lane = iota((1, 128), 1)
    inside = (lane >= 1) & (lane < SPLIT)
    wide = FINE * SPLIT
    factors = [E ** (-0.5 * (LOW_LOG + wide * j)) for j in range(SPLIT + 1)]
    row = everywhere(0, volumes(amount, low_v, high_v, None, factors, range(SPLIT + 1)))
    index = count_above(row, inside, target)
    low = LOW_LOG + wide * index
    ends = (entry(row, index), entry(row, index + 1.0))
    factors = [E ** (-0.5 * FINE * j) for j in range(1, SPLIT)]
    row = everywhere(
        2, volumes(amount, low_v, high_v, jnp.exp(-0.5 * low), factors, range(1, SPLIT))
    )
    row = jnp.where(lane == 0, ends[0], jnp.where(lane == SPLIT, ends[1], row))
    index = count_above(row, inside, target)
    final = secant(low + FINE * index, entry(row, index), entry(row, index + 1.0), target)
    factor = jnp.exp(-0.5 * final)

    factor_out[0] = jnp.sum(factor)
    for n, size in enumerate((nz, ny, nz, ny)):
        sum_sent(n, size, sums, send_r)


def written_kernel(
    factor, design, void, solid, fields, new_out, sens_out, new_v, store_sem, sens_sem
):
    parts, step = new_v.shape[0], new_v.shape[1]
    copy_sens = pltpu.make_async_copy(fields.at[0], sens_out, sens_sem)
    copy_sens.start()
    stores = []
    for n in range(parts):
        at = slice(n * step, (n + 1) * step)
        new_v[n] = finished(fields[1, at], factor[0], design[at], solid[at], void[at])
        stores.append(pltpu.make_async_copy(new_v.at[n], new_out.at[at], store_sem.at[n]))
        stores[n].start()
    for store in stores:
        store.wait()
    copy_sens.wait()


def per_device(displacement, design, void_mask, solid_mask, stiffness):
    nz, ny = lax.axis_size("gz"), lax.axis_size("gy")
    lz, ly, lx = design.shape
    brick = jax.ShapeDtypeStruct(design.shape, F32)
    padded = (lz + 2 * H, ly + 16, lx)
    anywhere = pl.BlockSpec(memory_space=pltpu.HBM)
    sem = pltpu.SemaphoreType
    nodes = pltpu.VMEM((3, lz + 1, ly + 8, lx), F32)
    line, table = pltpu.VMEM((lz, lx), F32), pltpu.VMEM((ly, lx), F32)
    bricks = [pltpu.VMEM(design.shape, F32)] * 4
    masks = [pltpu.VMEM(design.shape, jnp.int32)] * 2
    sums = pltpu.VMEM((4, max(nz, ny), 1, 128), F32)
    scalar = pl.BlockSpec(memory_space=pltpu.SMEM)
    one = jax.ShapeDtypeStruct((1,), F32)
    fields, found, factor = pl.pallas_call(
        functools.partial(kernel, nz, ny),
        out_shape=(
            jax.ShapeDtypeStruct((2, *design.shape), F32), jax.ShapeDtypeStruct((1,), jnp.int32), one
        ),
        in_specs=[anywhere] * 5,
        out_specs=(anywhere, scalar, scalar),
        scratch_shapes=[
            nodes,
            pltpu.VMEM(padded, F32),
            pltpu.VMEM(padded, F32),
            pltpu.VMEM((lz, ly + 16, lx), F32),
            *masks,
            *bricks,
            pltpu.VMEM(design.shape, F32), pltpu.VMEM(design.shape, F32),
            nodes, nodes, nodes,
            pltpu.VMEM((lz + 1, ly // 8, 8, lx), F32),
            pltpu.VMEM((lx, lx), BF16),
            pltpu.VMEM((24, 24), F32),
            pltpu.VMEM((192, 224), BF16),
            table, table, table, line, line, line,
            pltpu.VMEM((8, ly, lx), F32),
            pltpu.VMEM((8, 16, lx), F32),
            pltpu.VMEM((2, 16, lx), F32),
            sums,
            sem.DMA((5,)), sem.DMA((2,)),
            sem.DMA((11,)), sem.DMA((11,)), sem.DMA((8,)), sem.DMA((8,)),
            sem.DMA((4,)), sem.DMA((4,)), sem.REGULAR,
        ],
        compiler_params=pltpu.CompilerParams(
            collective_id=0, has_side_effects=True, vmem_limit_bytes=60 * 1024 * 1024
        ),
    )(displacement, design, void_mask, solid_mask, stiffness)

    def exact(factor, design, void_mask, solid_mask, fields):
        return pl.pallas_call(
            functools.partial(exact_kernel, nz, ny),
            out_shape=one,
            in_specs=[anywhere] * 4,
            out_specs=scalar,
            scratch_shapes=[
                pltpu.VMEM(design.shape, F32), *masks,
                *bricks[:3],
                table, line, sums,
                sem.DMA((4,)), sem.DMA((4,)), sem.DMA((4,)),
            ],
            compiler_params=pltpu.CompilerParams(
                collective_id=1, has_side_effects=True, vmem_limit_bytes=60 * 1024 * 1024
            ),
        )(design, void_mask, solid_mask, fields)

    factor = lax.switch(
        found[0], (exact, lambda factor, *rest: factor),
        factor, design, void_mask, solid_mask, fields,
    )
    parts = 8
    return pl.pallas_call(
        written_kernel,
        out_shape=(brick, brick),
        in_specs=[scalar] + [pl.BlockSpec(memory_space=pltpu.VMEM)] * 4,
        out_specs=(anywhere, anywhere),
        scratch_shapes=[
            pltpu.VMEM((parts, lz // parts, ly, lx), F32), sem.DMA((parts,)), sem.DMA
        ],
        compiler_params=pltpu.CompilerParams(vmem_limit_bytes=16 * 1024 * 1024),
    )(factor, design, void_mask, solid_mask, fields)


def solution(mesh):
    return jax.shard_map(
        per_device,
        mesh=mesh,
        in_specs=(
            P(None, "gz", "gy", None),
            P("gz", "gy", None),
            P("gz", "gy", None),
            P("gz", "gy", None),
            P(),
        ),
        out_specs=(P("gz", "gy", None), P("gz", "gy", None)),
        check_vma=False,
    )
```
